512 devices in a mesh: tile: 128 (over y, z, core), clip: 4 (over x).
Axes of the slice: x: 4, y: 8, z: 8, core: 2. Of those that a mesh axis runs over, the one named last changes fastest.
Arguments:
- features: bfloat16 [4, 128, 96, 3, 4096], P('clip', 'tile'), may hold values from -6 to 6
- conv_weight: bfloat16 [3, 9, 3, 96], replicated, may hold values from -0.125 to 0.125
- bias: float32 [3], replicated, may hold values from -2 to 2
- blend_profile: int32 [32], replicated, may hold values from 1 to 8
- tile_ids: int32 [4, 128], P('clip'), may hold values from 0 to 127, each once within a row
- reward_grad: bfloat16 [4, 128, 3, 4096], P('clip', 'tile'), may hold values from -6 to 6
Outputs:
- decoded: bfloat16 [4, 128, 3, 4096], P('clip', 'tile')
- feature_grad: bfloat16 [4, 128, 96, 3, 4096], P('clip', 'tile')
- weight_grad: float32 [3, 9, 3, 96], replicated
- bias_grad: float32 [3], replicated
The draws below stay inside these ranges and needn't reach their ends.
Inputs may be any that keep to these rules, and one draw needn't show every extreme that they name: Each row of tile_ids names each of the 128 tiles of the window once; tile v lies in tile row v // 16 and tile column v % 16.
All inputs are finite; a program needn't handle non-finite values.
Results may differ from the reference program's by a relative error of at most 0.023.
Values may be sent and summed in bfloat16 or wider, within the bound.
No kernel may reach another device: no remote copies, remote signals or barrier semaphores. Data moves between devices by JAX's collectives and lax.ppermute only.
A program may use at most 64 MiB of HBM per device.

```python
import math
import jax
import jax.numpy as jnp
from jax import lax

CH = 96
RGB = 3
TIN = 3
OV = 32
TILE = 64
TX = 16
PIX = 4096
SLOTS = 128
CLIPS = 4
FRAME_H = 288
FRAME_W = 544


def place_ends(values, stream_key, low, high):
    longest = values.shape.index(max(values.shape))
    spots = []
    for shift in (0, 1):
        where = [jax.random.randint(jax.random.fold_in(stream_key, axis), (), 0, length) for axis, length in enumerate(values.shape)]
        where[longest] = (where[longest] + shift) % values.shape[longest]
        spots.append(tuple(where))
    return values.at[spots[0]].set(low).at[spots[1]].set(high)


def steps_of(stream_key, dims, shards, smallest, largest):
    def one(axis_at, shards_of):
        heights = jax.random.uniform(jax.random.fold_in(jax.random.fold_in(stream_key, 6), axis_at), (shards_of,), jnp.float32, smallest / len(shards), largest / len(shards))
        return jnp.repeat(jnp.exp(heights), dims[axis_at] // shards_of).reshape((-1,) + (1,) * (len(dims) - axis_at - 1))

    factor_of = one(*shards[0])
    for cut in shards[1:]:
        factor_of = factor_of * one(*cut)
    return factor_of


def centred(key, dims, deviation, reach, pieces=(), held_as=jnp.bfloat16):
    gain = steps_of(key, dims, pieces, -0.22, 0.18) if pieces else 1.0
    drawn = jax.random.normal(key, dims, jnp.float32) * deviation * gain
    return jnp.minimum(jnp.maximum(drawn, -reach), reach).astype(held_as)


def setup_inputs(seed: int = 0) -> dict:
    seeds = jax.random.split(jax.random.key(seed), 7)
    features = centred(seeds[0], (CLIPS, SLOTS, CH, TIN, PIX), 1.0, 6.0, ((0, 4), (1, 128)))
    conv_weight = centred(seeds[1], (TIN, 9, RGB, CH), (27 * CH) ** -0.5, 0.125)
    bias = centred(seeds[2], (RGB,), 0.5, 2.0, (), jnp.float32)
    blend_profile = place_ends(jax.random.randint(seeds[3], (OV,), 1, 9), jax.random.fold_in(seeds[3], 1), 1, 8).astype(jnp.int32)
    tile_ids = jax.vmap(lambda own: jax.random.permutation(own, SLOTS))(jax.random.split(seeds[4], CLIPS)).reshape((CLIPS, SLOTS)).astype(jnp.int32)
    reward_grad = centred(seeds[5], (CLIPS, SLOTS, RGB, PIX), 1.0, 6.0, ((0, 4), (1, 128)))
    return {"features": features, "conv_weight": conv_weight, "bias": bias, "blend_profile": blend_profile, "tile_ids": tile_ids, "reward_grad": reward_grad}


def reference(features, conv_weight, bias, blend_profile, tile_ids, reward_grad):
    stride = TILE - OV
    places = jnp.arange(TILE)
    distance = jnp.minimum(jnp.minimum(places, TILE - 1 - places), OV - 1)
    factor = blend_profile.astype(jnp.float32)[distance]
    weight_map = factor[:, None] * factor[None, :]
    kernel = conv_weight.astype(jnp.float32).reshape(3, 3, 3, RGB, CH).transpose(3, 4, 0, 1, 2)
    bias_f = bias.astype(jnp.float32)

    def conv_tiles(kernel_f, values):
        result = lax.conv_general_dilated(values.reshape(SLOTS, CH, TIN, TILE, TILE), kernel_f, (1, 1, 1), ((0, 0), (1, 1), (1, 1)), dimension_numbers=('NCDHW', 'OIDHW', 'NCDHW'), precision=lax.Precision.HIGHEST)
        return result[:, :, 0]

    def paint_tiles(values, anchor_rows, anchor_cols):

        def add_one(canvas, entry_data):
            tile_val, anchor_y, anchor_x = entry_data
            corner = (jnp.int32(0), anchor_y, anchor_x)
            current = lax.dynamic_slice(canvas, corner, (RGB, TILE, TILE))
            return (lax.dynamic_update_slice(canvas, current + tile_val, corner), None)
        canvas, unused_out = lax.scan(add_one, jnp.zeros((RGB, FRAME_H, FRAME_W), jnp.float32), (values, anchor_rows, anchor_cols))
        return canvas

    def read_tiles(canvas, anchor_rows, anchor_cols):
        return jax.vmap(lambda anchor_y, anchor_x: lax.dynamic_slice(canvas, (jnp.int32(0), anchor_y, anchor_x), (RGB, TILE, TILE)))(anchor_rows, anchor_cols)

    def one_clip(entry_data):
        features_clip, tile_list, cotangent = entry_data
        values = features_clip.astype(jnp.float32)
        anchor_rows = (tile_list // TX * stride).astype(jnp.int32)
        anchor_cols = (tile_list % TX * stride).astype(jnp.int32)
        tile_image, pullback = jax.vjp(conv_tiles, kernel, values)
        tile_image = tile_image + bias_f[None, :, None, None]
        tile_image = lax.optimization_barrier(tile_image.astype(jnp.bfloat16)).astype(jnp.float32)
        weights = jnp.broadcast_to(weight_map, (SLOTS, RGB, TILE, TILE))
        coverage = read_tiles(paint_tiles(weights, anchor_rows, anchor_cols), anchor_rows, anchor_cols)
        blended = read_tiles(paint_tiles(weights * tile_image, anchor_rows, anchor_cols), anchor_rows, anchor_cols) / coverage
        grads = cotangent.astype(jnp.float32).reshape(SLOTS, RGB, TILE, TILE)
        summed = read_tiles(paint_tiles(grads, anchor_rows, anchor_cols), anchor_rows, anchor_cols)
        image_grad = (weights / coverage * summed).astype(jnp.bfloat16)
        image_grad = lax.optimization_barrier(image_grad).astype(jnp.float32)
        kernel_grad, value_grad = pullback(image_grad)
        return (blended.astype(jnp.bfloat16).reshape(SLOTS, RGB, PIX), value_grad.reshape(SLOTS, CH, TIN, PIX).astype(jnp.bfloat16), kernel_grad, lax.optimization_barrier(jnp.sum(image_grad, axis=(0, 2, 3))))
    decoded, feature_grad, kernel_grads, bias_grads = lax.map(one_clip, (features, tile_ids, reward_grad))
    grad_scale = 1.0 / math.sqrt(CLIPS * SLOTS * PIX)
    weight_grad = lax.optimization_barrier(jnp.sum(kernel_grads, 0)).transpose(2, 3, 4, 0, 1).reshape(TIN, 9, RGB, CH) * grad_scale
    bias_grad = lax.optimization_barrier(jnp.sum(bias_grads, 0)) * grad_scale
    return (decoded, feature_grad, weight_grad, bias_grad)
```

```python
import functools
import math

import jax
import jax.numpy as jnp
from jax import lax
from jax.experimental import pallas as pl
from jax.experimental.pallas import tpu as pltpu
from jax.sharding import PartitionSpec as P

EDGE = 64
OV = 32
PIX = EDGE * EDGE
SLOTS = 128
TX = 16
TY = SLOTS // TX
CH = 96
RGB = 3
TIN = 3
LANES = 128
ROWS = PIX // LANES
BOTH = 2 * SLOTS


f32 = jnp.float32
bf16 = jnp.bfloat16


def iota(shape, dim):
    return lax.broadcasted_iota(jnp.int32, shape, dim)


def lane_of_row():
    row = iota((LANES, LANES), 0)
    lane = iota((LANES, LANES), 1)
    target = (row // 64) * 64 + (row % 2) * 32 + (row // 2) % 32
    return (lane == target).astype(f32).astype(bf16)


def rows_of_half(rh):
    return [qy * 16 + rh * 8 + r8 for qy in range(2) for r8 in range(8)]


def pack_half(pieces):
    block = jnp.concatenate(pieces, axis=0).astype(bf16)
    return lax.dot_general(lane_of_row(), block, (((1,), (1,)), ((), ())), preferred_element_type=f32)


def unpack_half(block):
    return lax.dot_general(block, lane_of_row(), (((0,), (0,)), ((), ())), preferred_element_type=f32)


def shift_lanes(value, amount):
    size = value.shape[1]
    amount = amount % size
    return value if amount == 0 else pltpu.roll(value, size - amount, 1)


def profile_at(index, profile_ref):
    out = jnp.zeros(index.shape, f32)
    for m in range(OV):
        out = jnp.where(index == m, profile_ref[m].astype(f32), out)
    return out


def blend_parts(ids_ref, profile_ref, own):
    ids = ids_ref[...].astype(f32)
    slot_row = iota((BOTH, SLOTS), 0) // 2
    spread = slot_row == iota((BOTH, SLOTS), 1)
    id_col = jnp.sum(jnp.where(spread, jnp.broadcast_to(ids, (BOTH, SLOTS)), 0.0), axis=1, keepdims=True)
    onehot = (iota((SLOTS, BOTH), 1) // 2 == iota((SLOTS, BOTH), 0)).astype(f32).astype(bf16)
    id_row = jnp.dot(
        jnp.broadcast_to(ids, (8, SLOTS)).astype(bf16), onehot, preferred_element_type=f32
    )[0:1]
    qx_col = iota((BOTH, 1), 0) % 2
    side = (2 * qx_col - 1).astype(f32)
    tile_row = jnp.floor(id_col * (1.0 / TX))
    tile_col = id_col - tile_row * TX
    to_edge = jnp.where(qx_col == 1, TX - 1.0 - tile_col, tile_col)
    col_there = jnp.minimum(to_edge, 1.0)
    beside = jnp.where(to_edge > 0.5, id_col + side, 999.0)
    same = (iota((BOTH, BOTH), 0) - iota((BOTH, BOTH), 1)) % 2 == 0
    gap = id_row - jnp.where(same, id_col, beside)
    mats = [(gap == step).astype(f32).astype(bf16) for step in (0.0, -float(TX), float(TX))]
    rh = own // 64
    par = (own // 32) % 2
    rx = own % 32
    lane = iota((1, LANES), 1)
    lower = lane >= 64
    ry = 2 * (8 * rh + (lane // 8) % 8) + par
    fy = profile_at(jnp.where(lower, OV - 1 - ry, ry), profile_ref)
    fy_other = pltpu.roll(jnp.broadcast_to(fy, (8, LANES)), 64, 1)[0:1]
    left = profile_ref[rx].astype(f32)
    right = profile_ref[OV - 1 - rx].astype(f32)
    fx = jnp.where(qx_col == 0, left, right)
    fx_other = jnp.where(qx_col == 0, right, left)
    row_there = jnp.minimum(jnp.where(lower, TY - 1.0 - tile_row, tile_row), 1.0)
    weight = fx * fy
    coverage = (fx + col_there * fx_other) * (fy + row_there * fy_other)
    return mats, weight, coverage


def overlap_sum(mats, parts):
    total = []
    for mat in mats:
        got = jnp.dot(mat, parts[0], preferred_element_type=f32)
        for part in parts[1:]:
            got = got + jnp.dot(mat, part, preferred_element_type=f32)
        total.append(got)
    lower = iota((BOTH, LANES), 1) >= 64
    return total[0] + pltpu.roll(jnp.where(lower, total[1], total[2]), 64, 1)


def slot_of_lane(shape):
    return iota(shape, 1) % 8


def pack_grads_kernel(grad_ref, out_ref, held):
    held[...] = jnp.zeros_like(held)
    held[0:RGB, :] = grad_ref[...].astype(f32)
    for rh in range(2):
        pieces = [held[:, r * LANES : (r + 1) * LANES] for r in rows_of_half(rh)]
        out_ref[rh * LANES : (rh + 1) * LANES, :] = pack_half(pieces).astype(bf16)


def conv_kernel(chunk, feat_ref, weight_ref, bias_ref, out_ref, taps):
    step = pl.program_id(0)
    total = jnp.zeros((72, chunk), f32)
    for t in range(TIN):
        total += jnp.dot(weight_ref[t], feat_ref[t], preferred_element_type=f32)
    taps[:, pl.ds(pl.multiple_of(step * chunk, chunk), chunk)] = total

    @pl.when(step == pl.num_programs(0) - 1)
    def _():
        lane = iota((8, PIX), 1)
        image = jnp.zeros((8, PIX), f32)
        for kx in range(3):
            column = jnp.zeros((8, PIX), f32)
            for ky in range(3):
                tap = 3 * ky + kx
                moved = shift_lanes(taps[tap * 8 : tap * 8 + 8, :], (ky - 1) * EDGE)
                if ky == 0:
                    moved = jnp.where(lane >= EDGE, moved, 0.0)
                elif ky == 2:
                    moved = jnp.where(lane < PIX - EDGE, moved, 0.0)
                column = column + moved
            moved = shift_lanes(column, kx - 1)
            if kx == 0:
                moved = jnp.where(lane % EDGE != 0, moved, 0.0)
            elif kx == 2:
                moved = jnp.where(lane % EDGE != EDGE - 1, moved, 0.0)
            image = image + moved
        row = iota((8, 1), 0)
        shift = jnp.zeros((8, 1), f32)
        for o in range(RGB):
            shift = jnp.where(row == o, bias_ref[o], shift)
        image = pltpu.roll(image + shift, RGB, 0)
        for rh in range(2):
            pieces = [image[:, r * LANES : (r + 1) * LANES] for r in rows_of_half(rh)]
            out_ref[rh * LANES : (rh + 1) * LANES, :] = pack_half(pieces).astype(bf16)


def blend_grads_kernel(got_ref, image_ref, ids_ref, profile_ref, own_ref, out_ref):
    mats, weight, coverage = blend_parts(ids_ref, profile_ref, own_ref[0])
    summed = overlap_sum(mats, [got_ref[...]])
    grads = weight / coverage * summed
    slot = slot_of_lane((BOTH, LANES))
    out_ref[...] = jnp.where(slot < RGB, grads, image_ref[...].astype(f32)).astype(bf16)


def grad_stack(grad, taps):
    lane = iota((8, PIX), 1)
    for kx in range(3):
        moved_x = shift_lanes(grad, 1 - kx)
        if kx == 0:
            moved_x = jnp.where(lane % EDGE != EDGE - 1, moved_x, 0.0)
        elif kx == 2:
            moved_x = jnp.where(lane % EDGE != 0, moved_x, 0.0)
        for ky in range(3):
            moved = shift_lanes(moved_x, (1 - ky) * EDGE)
            if ky == 0:
                moved = jnp.where(lane < PIX - EDGE, moved, 0.0)
            elif ky == 2:
                moved = jnp.where(lane >= EDGE, moved, 0.0)
            tap = 3 * ky + kx
            taps[tap * 8 : tap * 8 + 8, :] = moved


def weight_grad_kernel(chunk, got_ref, feat_ref, out_ref, grad_ref, feats, taps, sem):
    copy = pltpu.make_async_copy(feat_ref, feats, sem)
    copy.start()
    row = iota((8, LANES), 0)
    for rh in range(2):
        block = unpack_half(got_ref[rh * LANES : (rh + 1) * LANES, :])
        for n, r in enumerate(rows_of_half(rh)):
            piece = block[n * 8 : n * 8 + 8, :]
            grad_ref[:, r * LANES : (r + 1) * LANES] = jnp.where(row < RGB, piece, 0.0)
    grad = grad_ref[...]
    grad_stack(grad, taps)
    bias = lax.dot_general(
        jnp.ones((8, PIX), bf16), grad.astype(bf16), (((1,), (1,)), ((), ())), preferred_element_type=f32
    )
    copy.wait()
    sums = [jnp.zeros((CH, 72), f32) for _ in range(TIN)]
    for at in range(0, PIX, chunk):
        part = taps[:, at : at + chunk].astype(bf16)
        for t in range(TIN):
            sums[t] += lax.dot_general(
                feats[t, :, at : at + chunk], part, (((1,), (1,)), ((), ())), preferred_element_type=f32
            )
    rows = []
    side = jnp.zeros((8, LANES - CH), f32)
    for t in range(TIN):
        turned = sums[t].T
        for tap in range(9):
            rows.append(jnp.concatenate([turned[tap * 8 : tap * 8 + 8, :], side], axis=1))
    rows.append(jnp.concatenate([bias, jnp.zeros((8, LANES - 8), f32)], axis=1))
    while len(rows) < ROWS:
        rows.append(jnp.zeros((8, LANES), f32))
    for rh in range(2):
        pieces = [rows[r] for r in rows_of_half(rh)]
        out_ref[rh * LANES : (rh + 1) * LANES, :] = pack_half(pieces).astype(bf16)


def feature_grad_kernel(chunk, grad_ref, weight_ref, out_ref, taps):
    step = pl.program_id(0)

    @pl.when(step == 0)
    def _():
        grad_stack(grad_ref[...], taps)

    part = taps[:, pl.ds(pl.multiple_of(step * chunk, chunk), chunk)].astype(bf16)
    for t in range(TIN):
        out_ref[t] = lax.dot_general(
            weight_ref[t], part, (((0,), (0,)), ((), ())), preferred_element_type=f32
        ).astype(bf16)


def blend_images_kernel(got_ref, ids_ref, profile_ref, own_ref, out_ref):
    mats, weight, coverage = blend_parts(ids_ref, profile_ref, own_ref[0])
    slot = slot_of_lane((BOTH, LANES))
    weighted = weight * jnp.where(slot >= RGB, got_ref[...].astype(f32), 0.0)
    high = weighted.astype(bf16)
    low = (weighted - high.astype(f32)).astype(bf16)
    out_ref[...] = (overlap_sum(mats, [high, low]) / coverage).astype(bf16)


def sum_tiles_kernel(got_ref, out_ref):
    pick = (iota((8, BOTH), 0) == iota((8, BOTH), 1) % 2).astype(f32).astype(bf16)
    total = jnp.dot(pick, got_ref[...], preferred_element_type=f32)
    for c in range(4):
        out_ref[c] = total


def spread_kernel(got_ref, image_ref, out_ref):
    total = got_ref[0] + got_ref[1] + got_ref[2] + got_ref[3]
    even = iota((BOTH, LANES), 0) % 2 == 0
    both = jnp.where(even, total[0:1], total[1:2])
    slot = slot_of_lane((BOTH, LANES))
    out_ref[...] = jnp.where(slot < RGB, both, image_ref[...].astype(f32)).astype(bf16)


def finish_kernel(scale, got_ref, weight_ref, bias_ref, image_ref):
    for rh in range(2):
        block = unpack_half(got_ref[rh * LANES : (rh + 1) * LANES, :])
        for n, r in enumerate(rows_of_half(rh)):
            piece = block[n * 8 : n * 8 + 8, :]
            image_ref[:, r * LANES : (r + 1) * LANES] = piece[RGB : 2 * RGB].astype(bf16)
            if r < 9 * TIN:
                weight_ref[r // 9, r % 9] = piece[0:RGB, 0:CH] * scale
            elif r == 9 * TIN:
                bias_ref[...] = piece[0:1, 0:RGB] * scale


VM = pl.BlockSpec(memory_space=pltpu.VMEM)
SM = pl.BlockSpec(memory_space=pltpu.SMEM)
ANY = pl.BlockSpec(memory_space=pl.ANY)
LIMIT = 40 * 1024 * 1024
message = jax.ShapeDtypeStruct((BOTH, LANES), bf16)


def cost(flops, size):
    return pl.CostEstimate(flops=flops, bytes_accessed=size, transcendentals=0)


def params():
    return pltpu.CompilerParams(vmem_limit_bytes=LIMIT)


def exchange(rows, axis):
    return lax.all_to_all(rows, axis, 0, 0, tiled=True)


def exchange_tiles(rows):
    return exchange(rows.reshape(SLOTS, 2, LANES), "tile").reshape(BOTH, LANES)


def per_device(features, conv_weight, bias, blend_profile, tile_ids, reward_grad):
    chunk = 1024
    own = lax.axis_index("tile").reshape(1).astype(jnp.int32)
    feats = jnp.transpose(features[0, 0], (1, 0, 2))
    weights = jnp.pad(conv_weight, ((0, 0), (0, 0), (0, 8 - RGB), (0, 0))).reshape(TIN, 72, CH)

    grads_out = pl.pallas_call(
        pack_grads_kernel,
        out_shape=message,
        in_specs=[VM],
        out_specs=VM,
        scratch_shapes=[pltpu.VMEM((8, PIX), f32)],
        compiler_params=params(),
        cost_estimate=cost(1 << 20, 1 << 17),
        name="pack_grads",
    )(reward_grad[0, 0])
    grads_got = exchange_tiles(grads_out)

    images_out = pl.pallas_call(
        functools.partial(conv_kernel, chunk),
        out_shape=message,
        grid=(PIX // chunk,),
        in_specs=[
            pl.BlockSpec((TIN, CH, chunk), lambda i: (0, 0, i)),
            pl.BlockSpec((TIN, 72, CH), lambda i: (0, 0, 0)),
            SM,
        ],
        out_specs=pl.BlockSpec((BOTH, LANES), lambda i: (0, 0)),
        scratch_shapes=[pltpu.VMEM((72, PIX), f32)],
        compiler_params=params(),
        cost_estimate=cost(2 * 72 * 288 * PIX, 1 << 22),
        name="conv",
    )(feats, weights, bias)

    back_out = pl.pallas_call(
        blend_grads_kernel,
        out_shape=message,
        in_specs=[VM, VM, VM, SM, SM],
        out_specs=VM,
        compiler_params=params(),
        cost_estimate=cost(1 << 26, 1 << 18),
        name="blend_grads",
    )(grads_got, images_out, tile_ids, blend_profile, own)
    back_got = exchange_tiles(back_out)

    weight_out, grad_rows = pl.pallas_call(
        functools.partial(weight_grad_kernel, chunk),
        out_shape=(message, jax.ShapeDtypeStruct((8, PIX), f32)),
        in_specs=[VM, ANY],
        out_specs=(VM, VM),
        scratch_shapes=[
            pltpu.VMEM((TIN, CH, PIX), bf16),
            pltpu.VMEM((72, PIX), f32),
            pltpu.SemaphoreType.DMA,
        ],
        compiler_params=params(),
        cost_estimate=cost(2 * 72 * 288 * PIX, 1 << 22),
        name="weight_grad",
    )(back_got, feats)
    weight_got = exchange_tiles(weight_out)

    feature_rows = pl.pallas_call(
        functools.partial(feature_grad_kernel, chunk),
        out_shape=jax.ShapeDtypeStruct((TIN, CH, PIX), bf16),
        grid=(PIX // chunk,),
        in_specs=[
            pl.BlockSpec((8, PIX), lambda i: (0, 0)),
            pl.BlockSpec((TIN, 72, CH), lambda i: (0, 0, 0)),
        ],
        out_specs=pl.BlockSpec((TIN, CH, chunk), lambda i: (0, 0, i)),
        scratch_shapes=[pltpu.VMEM((72, PIX), f32)],
        compiler_params=params(),
        cost_estimate=cost(2 * 72 * 288 * PIX, 1 << 22),
        name="feature_grad",
    )(grad_rows, weights)
    feature_grad = jnp.transpose(feature_rows, (1, 0, 2))[None, None]

    blended = pl.pallas_call(
        blend_images_kernel,
        out_shape=message,
        in_specs=[VM, VM, SM, SM],
        out_specs=VM,
        compiler_params=params(),
        cost_estimate=cost(1 << 27, 1 << 18),
        name="blend_images",
    )(back_got, tile_ids, blend_profile, own)

    tile_sum = pl.pallas_call(
        sum_tiles_kernel,
        out_shape=jax.ShapeDtypeStruct((4, 8, LANES), f32),
        in_specs=[VM],
        out_specs=VM,
        compiler_params=params(),
        cost_estimate=cost(1 << 20, 1 << 17),
        name="sum_tiles",
    )(weight_got)
    clip_got = exchange(tile_sum, "clip")

    spread_out = pl.pallas_call(
        spread_kernel,
        out_shape=message,
        in_specs=[VM, VM],
        out_specs=VM,
        compiler_params=params(),
        cost_estimate=cost(1 << 20, 1 << 17),
        name="spread",
    )(clip_got, blended)
    spread_got = exchange_tiles(spread_out)

    scale = 1.0 / math.sqrt(lax.axis_size("clip") * lax.axis_size("tile") * PIX)
    weight_grad, bias_grad, decoded = pl.pallas_call(
        functools.partial(finish_kernel, scale),
        out_shape=(
            jax.ShapeDtypeStruct((TIN, 9, RGB, CH), f32),
            jax.ShapeDtypeStruct((1, RGB), f32),
            jax.ShapeDtypeStruct((RGB, PIX), bf16),
        ),
        in_specs=[VM],
        out_specs=(VM, VM, VM),
        compiler_params=params(),
        cost_estimate=cost(1 << 20, 1 << 17),
        name="finish",
    )(spread_got)
    return (decoded[None, None], feature_grad, weight_grad, bias_grad.reshape(RGB))


def solution(mesh):
    return jax.shard_map(
        per_device,
        mesh=mesh,
        in_specs=(
            P("clip", "tile", None, None, None),
            P(),
            P(),
            P(),
            P("clip", None),
            P("clip", "tile", None, None),
        ),
        out_specs=(P("clip", "tile", None, None), P("clip", "tile", None, None, None), P(), P()),
        check_vma=False,
    )
```

```python
import functools
import math

import jax
import jax.numpy as jnp
from jax import lax
from jax.experimental import pallas as pl
from jax.experimental.pallas import tpu as pltpu
from jax.sharding import Mesh
from jax.sharding import PartitionSpec as P

EDGE = 64
OV = 32
PIX = EDGE * EDGE
SLOTS = 128
TX = 16
TY = SLOTS // TX
CH = 96
RGB = 3
TIN = 3
LANES = 128
ROWS = PIX // LANES
BOTH = 2 * SLOTS
TAPS = 9
STACK = TAPS * 8
HALF = 32
MAIN = 30
BIAS_ROW = 30


f32 = jnp.float32
bf16 = jnp.bfloat16


def iota(shape, dim):
    return lax.broadcasted_iota(jnp.int32, shape, dim)


def lane_of_row():
    row = iota((LANES, LANES), 0)
    lane = iota((LANES, LANES), 1)
    target = (row // 64) * 64 + (row % 2) * 32 + (row // 2) % 32
    return (lane == target).astype(f32).astype(bf16)


def rows_of_half(rh):
    return [qy * 16 + rh * 8 + r8 for qy in range(2) for r8 in range(8)]


def pack_half(pieces):
    block = jnp.concatenate(pieces, axis=0).astype(bf16)
    return lax.dot_general(lane_of_row(), block, (((1,), (1,)), ((), ())), preferred_element_type=f32)


def unpack_half(block):
    return lax.dot_general(block, lane_of_row(), (((0,), (0,)), ((), ())), preferred_element_type=f32)


def shift_lanes(value, amount):
    size = value.shape[1]
    amount = amount % size
    return value if amount == 0 else pltpu.roll(value, size - amount, 1)


def profile_at(index, profile_ref):
    out = jnp.zeros(index.shape, f32)
    for m in range(OV):
        out = jnp.where(index == m, profile_ref[m].astype(f32), out)
    return out


def blend_prep_kernel(ids_ref, profile_ref, own_ref, feat_ref, mats_ref, before_ref, after_ref, held_ref, sem):
    copy = pltpu.make_async_copy(feat_ref, held_ref, sem)
    copy.start()
    own = own_ref[0]
    ids = ids_ref[...].astype(f32)
    slot_row = iota((BOTH, SLOTS), 0) // 2
    spread = slot_row == iota((BOTH, SLOTS), 1)
    id_col = jnp.sum(jnp.where(spread, jnp.broadcast_to(ids, (BOTH, SLOTS)), 0.0), axis=1, keepdims=True)
    onehot = (iota((SLOTS, BOTH), 1) // 2 == iota((SLOTS, BOTH), 0)).astype(f32).astype(bf16)
    id_row = jnp.dot(
        jnp.broadcast_to(ids, (8, SLOTS)).astype(bf16), onehot, preferred_element_type=f32
    )[0:1]
    qx_col = iota((BOTH, 1), 0) % 2
    side = (2 * qx_col - 1).astype(f32)
    tile_row = jnp.floor(id_col * (1.0 / TX))
    tile_col = id_col - tile_row * TX
    to_edge = jnp.where(qx_col == 1, TX - 1.0 - tile_col, tile_col)
    col_there = jnp.minimum(to_edge, 1.0)
    beside = jnp.where(to_edge > 0.5, id_col + side, 999.0)
    same = (iota((BOTH, BOTH), 0) - iota((BOTH, BOTH), 1)) % 2 == 0
    gap = id_row - jnp.where(same, id_col, beside)
    for n, step in enumerate((0.0, -float(TX), float(TX))):
        mats_ref[n * BOTH : (n + 1) * BOTH, :] = (gap == step).astype(f32).astype(bf16)
    rh = own // 64
    par = (own // 32) % 2
    rx = own % 32
    lane = iota((1, LANES), 1)
    lower = lane >= 64
    ry = 2 * (8 * rh + (lane // 8) % 8) + par
    fy = profile_at(jnp.where(lower, OV - 1 - ry, ry), profile_ref)
    fy_other = pltpu.roll(jnp.broadcast_to(fy, (8, LANES)), 64, 1)[0:1]
    left = profile_ref[rx].astype(f32)
    right = profile_ref[OV - 1 - rx].astype(f32)
    fx = jnp.where(qx_col == 0, left, right)
    fx_other = jnp.where(qx_col == 0, right, left)
    row_there = jnp.minimum(jnp.where(lower, TY - 1.0 - tile_row, tile_row), 1.0)
    weight = fx * fy
    coverage = (fx + col_there * fx_other) * (fy + row_there * fy_other)
    grads = iota((BOTH, LANES), 1) % 8 < RGB
    before_ref[...] = jnp.where(grads, 1.0, weight)
    after_ref[...] = jnp.where(grads, weight, 1.0) / coverage
    copy.wait()


def blend_kernel(got_ref, mats_ref, before_ref, after_ref, out_ref):
    source = got_ref[...].astype(f32) * before_ref[...]
    high = source.astype(bf16)
    low = (source - high.astype(f32)).astype(bf16)
    total = []
    for n in range(3):
        mat = mats_ref[n * BOTH : (n + 1) * BOTH, :]
        total.append(
            jnp.dot(mat, high, preferred_element_type=f32) + jnp.dot(mat, low, preferred_element_type=f32)
        )
    lower = iota((BOTH, LANES), 1) >= 64
    summed = total[0] + pltpu.roll(jnp.where(lower, total[1], total[2]), 64, 1)
    out_ref[...] = (summed * after_ref[...]).astype(bf16)


def stack_weights(weight_ref, held):
    held[...] = jnp.zeros_like(held)
    for t in range(TIN):
        for tap in range(TAPS):
            held[t, tap * 8 : tap * 8 + RGB, :] = weight_ref[t, tap].astype(f32)


def conv_kernel(chunk, feat_ref, weight_ref, bias_ref, grad_ref, out_ref, feats, held, taps, sems):
    copies = []
    for n in range(PIX // chunk):
        part = pl.ds(n * chunk, chunk)
        copies.append(pltpu.make_async_copy(feat_ref.at[:, :, part], feats.at[:, :, part], sems.at[n]))
        copies[-1].start()
    stack_weights(weight_ref, held)
    kernels = [held[t].astype(bf16) for t in range(TIN)]
    for n in range(PIX // chunk):
        copies[n].wait()
        total = jnp.zeros((STACK, chunk), f32)
        for t in range(TIN):
            total += jnp.dot(kernels[t], feats[t, :, n * chunk : (n + 1) * chunk], preferred_element_type=f32)
        taps[:, n * chunk : (n + 1) * chunk] = total
    lane = iota((8, PIX), 1)
    image = jnp.zeros((8, PIX), f32)
    for kx in range(3):
        column = jnp.zeros((8, PIX), f32)
        for ky in range(3):
            tap = 3 * ky + kx
            moved = shift_lanes(taps[tap * 8 : tap * 8 + 8, :], (ky - 1) * EDGE)
            if ky == 0:
                moved = jnp.where(lane >= EDGE, moved, 0.0)
            elif ky == 2:
                moved = jnp.where(lane < PIX - EDGE, moved, 0.0)
            column = column + moved
        moved = shift_lanes(column, kx - 1)
        if kx == 0:
            moved = jnp.where(lane % EDGE != 0, moved, 0.0)
        elif kx == 2:
            moved = jnp.where(lane % EDGE != EDGE - 1, moved, 0.0)
        image = image + moved
    row = iota((8, 1), 0)
    shift = jnp.zeros((8, 1), f32)
    for o in range(RGB):
        shift = jnp.where(row == o, bias_ref[o], shift)
    taps[0:8, :] = pltpu.roll(image + shift, RGB, 0)
    taps[0:RGB, :] = grad_ref[...].astype(f32)
    for rh in range(2):
        pieces = [taps[0:8, r * LANES : (r + 1) * LANES] for r in rows_of_half(rh)]
        out_ref[rh * LANES : (rh + 1) * LANES, :] = pack_half(pieces).astype(bf16)


def grad_stack(grad, taps):
    lane = iota((8, PIX), 1)
    for kx in range(3):
        moved_x = shift_lanes(grad, 1 - kx)
        if kx == 0:
            moved_x = jnp.where(lane % EDGE != EDGE - 1, moved_x, 0.0)
        elif kx == 2:
            moved_x = jnp.where(lane % EDGE != 0, moved_x, 0.0)
        for ky in range(3):
            moved = shift_lanes(moved_x, (1 - ky) * EDGE)
            if ky == 0:
                moved = jnp.where(lane < PIX - EDGE, moved, 0.0)
            elif ky == 2:
                moved = jnp.where(lane >= EDGE, moved, 0.0)
            tap = 3 * ky + kx
            taps[tap * 8 : tap * 8 + 8, :] = moved


def split_bias(half):
    at = iota((HALF, LANES), 0) == BIAS_ROW
    lane = iota((HALF, LANES), 1)
    total = half + pltpu.roll(half, LANES - RGB, 1)
    high = total.astype(bf16).astype(f32)
    low = pltpu.roll(total - high, RGB, 1)
    pair = jnp.where(lane < RGB, high, jnp.where(lane < 2 * RGB, low, half))
    return jnp.where(at, pair, half).astype(bf16)


def weight_grad_kernel(chunk, got_ref, feat_ref, out_ref, grad_ref, taps):
    row = iota((8, LANES), 0)
    for rh in range(2):
        block = unpack_half(got_ref[rh * LANES : (rh + 1) * LANES, :])
        for n, r in enumerate(rows_of_half(rh)):
            piece = block[n * 8 : n * 8 + 8, :]
            grad_ref[:, r * LANES : (r + 1) * LANES] = jnp.where(row < RGB, piece, 0.0)
    grad = grad_ref[...]
    grad_stack(grad, taps)
    bias = lax.dot_general(
        jnp.ones((8, PIX), bf16), grad.astype(bf16), (((1,), (1,)), ((), ())), preferred_element_type=f32
    )
    sums = [jnp.zeros((CH, STACK), f32) for _ in range(TIN)]
    for at in range(0, PIX, chunk):
        part = taps[:, at : at + chunk].astype(bf16)
        for t in range(TIN):
            sums[t] += lax.dot_general(
                feat_ref[t, :, at : at + chunk], part, (((1,), (1,)), ((), ())), preferred_element_type=f32
            )
    rows = jnp.concatenate([total.T for total in sums], axis=0)
    rows = jnp.concatenate([rows, jnp.zeros((TIN * STACK, LANES - CH), f32)], axis=1).astype(bf16)
    for h in range(2):
        place = iota((HALF, TIN * STACK), 0)
        source = iota((HALF, TIN * STACK), 1)
        rank = jnp.where(source % 8 < RGB, (source // 8) * RGB + source % 8, -1)
        main = (rank == h * MAIN + place) & (place < MAIN)
        side = rank == 2 * MAIN + (h * HALF + place) // 3
        front = jnp.dot(main.astype(f32).astype(bf16), rows, preferred_element_type=f32)
        back = jnp.dot(side.astype(f32).astype(bf16), rows, preferred_element_type=f32)
        third = (h * HALF + iota((HALF, LANES), 0)) % 3
        tail = jnp.zeros((HALF, LANES), f32)
        for c in range(3):
            tail = jnp.where(third == c, pltpu.roll(back, CH - 32 * c, 1), tail)
        half = jnp.where(iota((HALF, LANES), 1) < CH, front, tail)
        at_bias = (iota((HALF, LANES), 0) == BIAS_ROW) & (iota((HALF, LANES), 1) < CH)
        bias_wide = jnp.concatenate([bias, jnp.zeros((8, LANES - 8), f32)], axis=1)[0:1]
        bias_wide = jnp.where(iota((1, LANES), 1) < RGB, bias_wide, 0.0)
        half = split_bias(jnp.where(at_bias, bias_wide, half))
        for y in range(8):
            out_ref[2 * y + h] = half


def feature_grad_kernel(chunk, grad_ref, weight_ref, out_ref, taps, held):
    step = pl.program_id(0)

    @pl.when(step == 0)
    def _():
        stack_weights(weight_ref, held)
        grad_stack(grad_ref[...], taps)

    part = taps[:, pl.ds(pl.multiple_of(step * chunk, chunk), chunk)].astype(bf16)
    for t in range(TIN):
        out_ref[t] = lax.dot_general(
            held[t].astype(bf16), part, (((0,), (0,)), ((), ())), preferred_element_type=f32
        ).astype(bf16)


def decode_kernel(got_ref, image_ref):
    for rh in range(2):
        block = unpack_half(got_ref[rh * LANES : (rh + 1) * LANES, :])
        for n, r in enumerate(rows_of_half(rh)):
            image_ref[:, r * LANES : (r + 1) * LANES] = block[n * 8 + RGB : n * 8 + 2 * RGB].astype(bf16)


def add_up(got_ref, first, count):
    total = got_ref[first].astype(f32)
    for n in range(first + 1, first + count):
        total = total + got_ref[n].astype(f32)
    return total


def sum_kernel(got_ref, out_ref):
    half = split_bias(add_up(got_ref, 0, got_ref.shape[0]))
    for n in range(out_ref.shape[0]):
        out_ref[n] = half


def finish_kernel(scale, got_ref, weight_ref, bias_ref, held, others):
    for h in range(2):
        held[h * HALF : (h + 1) * HALF, :] = add_up(got_ref, 4 * h, 4) * scale
    bias = held[BIAS_ROW : BIAS_ROW + 1, :]
    bias_ref[...] = bias[:, 0:RGB] + bias[:, RGB : 2 * RGB]
    count = TIN * TAPS * RGB - 2 * MAIN
    lane = iota((count, LANES), 1)
    tail = jnp.zeros((count, LANES), f32)
    for c in range(3):
        turned = pltpu.roll(held[pl.ds(c, count, stride=3), :], (32 + 32 * c) % LANES, 1)
        tail = jnp.where(lane // 32 == c, turned, tail)
    others[0:count, :] = tail
    for n in range(TIN * TAPS):
        at = n * RGB
        if at < 2 * MAIN:
            at = (at // MAIN) * HALF + at % MAIN
            value = held[at : at + RGB, 0:CH]
        else:
            at -= 2 * MAIN
            value = others[at : at + RGB, 0:CH]
        weight_ref[n // TAPS, n % TAPS] = value


VM = pl.BlockSpec(memory_space=pltpu.VMEM)
SM = pl.BlockSpec(memory_space=pltpu.SMEM)
HBM = pl.BlockSpec(memory_space=pltpu.HBM)
LIMIT = 40 * 1024 * 1024
FULL = 64 * 1024 * 1024
message = jax.ShapeDtypeStruct((BOTH, LANES), bf16)


def call(body, out_shape, in_specs, scratch=(), flops=1 << 20, size=1 << 17, name=None, limit=LIMIT, **rest):
    return pl.pallas_call(
        body,
        out_shape=out_shape,
        in_specs=in_specs,
        scratch_shapes=list(scratch),
        compiler_params=pltpu.CompilerParams(vmem_limit_bytes=limit),
        cost_estimate=pl.CostEstimate(flops=flops, bytes_accessed=size, transcendentals=0),
        name=name,
        **rest,
    )


def exchange(rows, axes):
    return lax.all_to_all(rows, axes, 0, 0, tiled=True)


def exchange_tiles(rows):
    return exchange(rows.reshape(SLOTS, 2, LANES), ("y", "z", "c")).reshape(BOTH, LANES)


def per_device(features, conv_weight, bias, blend_profile, tile_ids, reward_grad):
    chunk = 1024
    conv_flops = 2 * STACK * TIN * CH * PIX
    own = lax.axis_index(("y", "z", "c")).reshape(1).astype(jnp.int32)
    feats = jnp.transpose(features[0, 0], (1, 0, 2))

    parts_out = call(
        functools.partial(conv_kernel, chunk),
        message,
        [HBM, VM, SM, VM],
        [
            pltpu.VMEM((TIN, CH, PIX), bf16),
            pltpu.VMEM((TIN, STACK, CH), f32),
            pltpu.VMEM((STACK, PIX), f32),
            pltpu.SemaphoreType.DMA((PIX // chunk,)),
        ],
        conv_flops,
        1 << 22,
        "conv",
        FULL,
        out_specs=VM,
    )(feats, conv_weight, bias, reward_grad[0, 0])
    parts_got = exchange_tiles(parts_out)

    factors = jax.ShapeDtypeStruct((BOTH, LANES), f32)
    mats, before, after, feats_held = call(
        blend_prep_kernel,
        (
            jax.ShapeDtypeStruct((3 * BOTH, BOTH), bf16),
            factors,
            factors,
            jax.ShapeDtypeStruct((TIN, CH, PIX), bf16),
        ),
        [VM, SM, SM, HBM],
        [pltpu.SemaphoreType.DMA],
        1 << 25,
        1 << 22,
        "blend_prep",
        out_specs=(VM, VM, VM, VM),
    )(tile_ids, blend_profile, own, feats)
    blend_out = call(
        blend_kernel, message, [VM, VM, VM, VM], (), 1 << 27, 1 << 20, "blend", out_specs=VM
    )(parts_got, mats, before, after)
    blend_got = exchange_tiles(blend_out)

    sums, grad_rows = call(
        functools.partial(weight_grad_kernel, chunk),
        (
            jax.ShapeDtypeStruct((16, HALF, LANES), bf16),
            jax.ShapeDtypeStruct((8, PIX), f32),
        ),
        [VM, VM],
        [pltpu.VMEM((STACK, PIX), f32)],
        conv_flops,
        1 << 22,
        "weight_grad",
        out_specs=(VM, VM),
    )(blend_got, feats_held)
    feature_rows = call(
        functools.partial(feature_grad_kernel, chunk),
        jax.ShapeDtypeStruct((TIN, CH, PIX), bf16),
        [
            pl.BlockSpec((8, PIX), lambda i: (0, 0)),
            pl.BlockSpec((TIN, TAPS, RGB, CH), lambda i: (0, 0, 0, 0)),
        ],
        [pltpu.VMEM((STACK, PIX), f32), pltpu.VMEM((TIN, STACK, CH), f32)],
        conv_flops,
        1 << 22,
        "feature_grad",
        grid=(PIX // chunk,),
        out_specs=pl.BlockSpec((TIN, CH, chunk), lambda i: (0, 0, i)),
    )(grad_rows, conv_weight)
    feature_grad = jnp.transpose(feature_rows, (1, 0, 2))[None, None]
    decoded = call(
        decode_kernel, jax.ShapeDtypeStruct((RGB, PIX), bf16), [VM], name="decode", out_specs=VM
    )(blend_got)
    sums = exchange(sums, ("y", "c"))
    sums, feature_grad = lax.optimization_barrier((sums, feature_grad))
    sums = call(
        sum_kernel, jax.ShapeDtypeStruct((8, HALF, LANES), bf16), [VM], name="sum_y", out_specs=VM
    )(sums)
    sums = exchange(sums, "z")
    sums, decoded = lax.optimization_barrier((sums, decoded))
    sums = call(
        sum_kernel, jax.ShapeDtypeStruct((8, HALF, LANES), bf16), [VM], name="sum_z", out_specs=VM
    )(sums)
    sums = exchange(sums, ("c", "clip"))
    scale = 1.0 / math.sqrt(4 * SLOTS * PIX)
    weight_grad, bias_grad = call(
        functools.partial(finish_kernel, scale),
        (
            jax.ShapeDtypeStruct((TIN, TAPS, RGB, CH), f32),
            jax.ShapeDtypeStruct((1, RGB), f32),
        ),
        [VM],
        [pltpu.VMEM((2 * HALF, LANES), f32), pltpu.VMEM((24, LANES), f32)],
        name="finish",
        out_specs=(VM, VM),
    )(sums)

    return (decoded[None, None], feature_grad, weight_grad, bias_grad.reshape(RGB))


def solution(mesh):
    parts = Mesh(mesh.devices.reshape(8, 8, 2, 4), ("y", "z", "c", "clip"))
    tile = ("y", "z", "c")
    return jax.shard_map(
        per_device,
        mesh=parts,
        in_specs=(
            P("clip", tile, None, None, None),
            P(),
            P(),
            P(),
            P("clip", None),
            P("clip", tile, None, None),
        ),
        out_specs=(P("clip", tile, None, None), P("clip", tile, None, None, None), P(), P()),
        check_vma=False,
    )
```

```python
import functools
import math

import jax
import jax.numpy as jnp
from jax import lax
from jax.experimental import pallas as pl
from jax.experimental.pallas import tpu as pltpu
from jax.sharding import Mesh
from jax.sharding import PartitionSpec as P

EDGE = 64
OV = 32
PIX = EDGE * EDGE
SLOTS = 128
TX = 16
TY = SLOTS // TX
CH = 96
RGB = 3
TIN = 3
LANES = 128
ROWS = PIX // LANES
BOTH = 2 * SLOTS
TAPS = 9
STACK = TAPS * 8
HALF = 32
MAIN = 30
BIAS_ROW = 30


f32 = jnp.float32
bf16 = jnp.bfloat16


def iota(shape, dim):
    return lax.broadcasted_iota(jnp.int32, shape, dim)


def lane_of_row():
    row = iota((LANES, LANES), 0)
    lane = iota((LANES, LANES), 1)
    target = (row // 64) * 64 + (row % 2) * 32 + (row // 2) % 32
    return (lane == target).astype(f32).astype(bf16)


def rows_of_half(rh):
    return [qy * 16 + rh * 8 + r8 for qy in range(2) for r8 in range(8)]


def pack_half(pieces):
    block = jnp.concatenate(pieces, axis=0).astype(bf16)
    return lax.dot_general(lane_of_row(), block, (((1,), (1,)), ((), ())), preferred_element_type=f32)


def unpack_half(block):
    return lax.dot_general(block, lane_of_row(), (((0,), (0,)), ((), ())), preferred_element_type=f32)


def shift_lanes(value, amount):
    size = value.shape[1]
    amount = amount % size
    return value if amount == 0 else pltpu.roll(value, size - amount, 1)


def profile_at(index, profile_ref):
    out = jnp.zeros(index.shape, f32)
    for m in range(OV):
        out = jnp.where(index == m, profile_ref[m].astype(f32), out)
    return out


def blend_prep(ids, profile_ref, own, mats_ref, before_ref, after_ref):
    slot_row = iota((BOTH, SLOTS), 0) // 2
    spread = slot_row == iota((BOTH, SLOTS), 1)
    id_col = jnp.sum(jnp.where(spread, jnp.broadcast_to(ids, (BOTH, SLOTS)), 0.0), axis=1, keepdims=True)
    onehot = (iota((SLOTS, BOTH), 1) // 2 == iota((SLOTS, BOTH), 0)).astype(f32).astype(bf16)
    id_row = jnp.dot(
        jnp.broadcast_to(ids, (8, SLOTS)).astype(bf16), onehot, preferred_element_type=f32
    )[0:1]
    qx_col = iota((BOTH, 1), 0) % 2
    side = (2 * qx_col - 1).astype(f32)
    tile_row = jnp.floor(id_col * (1.0 / TX))
    tile_col = id_col - tile_row * TX
    to_edge = jnp.where(qx_col == 1, TX - 1.0 - tile_col, tile_col)
    col_there = jnp.minimum(to_edge, 1.0)
    beside = jnp.where(to_edge > 0.5, id_col + side, 999.0)
    same = (iota((BOTH, BOTH), 0) - iota((BOTH, BOTH), 1)) % 2 == 0
    gap = id_row - jnp.where(same, id_col, beside)
    for n, step in enumerate((0.0, -float(TX), float(TX))):
        mats_ref[n * BOTH : (n + 1) * BOTH, :] = (gap == step).astype(f32).astype(bf16)
    rh = own // 64
    par = (own // 32) % 2
    rx = own % 32
    lane = iota((1, LANES), 1)
    lower = lane >= 64
    ry = 2 * (8 * rh + (lane // 8) % 8) + par
    fy = profile_at(jnp.where(lower, OV - 1 - ry, ry), profile_ref)
    fy_other = pltpu.roll(jnp.broadcast_to(fy, (8, LANES)), 64, 1)[0:1]
    left = profile_ref[rx].astype(f32)
    right = profile_ref[OV - 1 - rx].astype(f32)
    fx = jnp.where(qx_col == 0, left, right)
    fx_other = jnp.where(qx_col == 0, right, left)
    row_there = jnp.minimum(jnp.where(lower, TY - 1.0 - tile_row, tile_row), 1.0)
    weight = fx * fy
    coverage = (fx + col_there * fx_other) * (fy + row_there * fy_other)
    grads = iota((BOTH, LANES), 1) % 8 < RGB
    before_ref[...] = jnp.where(grads, 1.0, weight)
    after_ref[...] = jnp.where(grads, weight, 1.0) / coverage


def blend_kernel(got_ref, mats_ref, before_ref, after_ref, out_ref):
    source = got_ref[...].astype(f32) * before_ref[...]
    high = source.astype(bf16)
    low = (source - high.astype(f32)).astype(bf16)
    total = []
    for n in range(3):
        mat = mats_ref[n * BOTH : (n + 1) * BOTH, :]
        total.append(
            jnp.dot(mat, high, preferred_element_type=f32) + jnp.dot(mat, low, preferred_element_type=f32)
        )
    lower = iota((BOTH, LANES), 1) >= 64
    summed = total[0] + pltpu.roll(jnp.where(lower, total[1], total[2]), 64, 1)
    out_ref[...] = (summed * after_ref[...]).astype(bf16)


def stack_weights(weight_ref, held):
    held[...] = jnp.zeros_like(held)
    for t in range(TIN):
        for tap in range(TAPS):
            held[t, tap * 8 : tap * 8 + RGB, :] = weight_ref[t, tap].astype(f32)


def conv_kernel(
    chunk,
    feat_ref,
    weight_hbm,
    bias_hbm,
    grad_hbm,
    ids_hbm,
    profile_hbm,
    own_ref,
    out_ref,
    mats_ref,
    before_ref,
    after_ref,
    feats,
    weight_ref,
    bias_ref,
    grad_ref,
    ids_ref,
    profile_ref,
    held,
    taps,
    small_sems,
    sems,
):
    small = [(ids_hbm, ids_ref), (profile_hbm, profile_ref), (weight_hbm, weight_ref), (grad_hbm, grad_ref), (bias_hbm, bias_ref)]
    moves = [pltpu.make_async_copy(src, dst, small_sems.at[n]) for n, (src, dst) in enumerate(small)]
    for move in moves:
        move.start()
    copies = []
    for n in range(PIX // chunk):
        part = pl.ds(n * chunk, chunk)
        copies.append(pltpu.make_async_copy(feat_ref.at[:, :, part], feats.at[:, :, part], sems.at[n]))
        copies[-1].start()
    for move in moves:
        move.wait()
    stack_weights(weight_ref, held)
    kernels = [held[t].astype(bf16) for t in range(TIN)]
    blend_prep(ids_ref[...].astype(f32), profile_ref, own_ref[0], mats_ref, before_ref, after_ref)
    for n in range(PIX // chunk):
        copies[n].wait()
        total = jnp.zeros((STACK, chunk), f32)
        for t in range(TIN):
            total += jnp.dot(kernels[t], feats[t, :, n * chunk : (n + 1) * chunk], preferred_element_type=f32)
        taps[:, n * chunk : (n + 1) * chunk] = total
    lane = iota((8, PIX), 1)
    image = jnp.zeros((8, PIX), f32)
    for kx in range(3):
        column = jnp.zeros((8, PIX), f32)
        for ky in range(3):
            tap = 3 * ky + kx
            moved = shift_lanes(taps[tap * 8 : tap * 8 + 8, :], (ky - 1) * EDGE)
            if ky == 0:
                moved = jnp.where(lane >= EDGE, moved, 0.0)
            elif ky == 2:
                moved = jnp.where(lane < PIX - EDGE, moved, 0.0)
            column = column + moved
        moved = shift_lanes(column, kx - 1)
        if kx == 0:
            moved = jnp.where(lane % EDGE != 0, moved, 0.0)
        elif kx == 2:
            moved = jnp.where(lane % EDGE != EDGE - 1, moved, 0.0)
        image = image + moved
    row = iota((8, 1), 0)
    shift = jnp.zeros((8, 1), f32)
    for o in range(RGB):
        shift = jnp.where(row == o, bias_ref[o], shift)
    taps[0:8, :] = pltpu.roll(image + shift, RGB, 0)
    taps[0:RGB, :] = grad_ref[...].astype(f32)
    for rh in range(2):
        pieces = [taps[0:8, r * LANES : (r + 1) * LANES] for r in rows_of_half(rh)]
        out_ref[rh * LANES : (rh + 1) * LANES, :] = pack_half(pieces).astype(bf16)


def grad_stack(grad, taps):
    lane = iota((8, PIX), 1)
    for kx in range(3):
        moved_x = shift_lanes(grad, 1 - kx)
        if kx == 0:
            moved_x = jnp.where(lane % EDGE != EDGE - 1, moved_x, 0.0)
        elif kx == 2:
            moved_x = jnp.where(lane % EDGE != 0, moved_x, 0.0)
        for ky in range(3):
            moved = shift_lanes(moved_x, (1 - ky) * EDGE)
            if ky == 0:
                moved = jnp.where(lane < PIX - EDGE, moved, 0.0)
            elif ky == 2:
                moved = jnp.where(lane >= EDGE, moved, 0.0)
            tap = 3 * ky + kx
            taps[tap * 8 : tap * 8 + 8, :] = moved


def split_bias(half):
    at = iota((HALF, LANES), 0) == BIAS_ROW
    lane = iota((HALF, LANES), 1)
    total = half + pltpu.roll(half, LANES - RGB, 1)
    high = total.astype(bf16).astype(f32)
    low = pltpu.roll(total - high, RGB, 1)
    pair = jnp.where(lane < RGB, high, jnp.where(lane < 2 * RGB, low, half))
    return jnp.where(at, pair, half).astype(bf16)


def weight_grad_kernel(chunk, got_ref, feat_ref, out_ref, grad_ref, taps):
    row = iota((8, LANES), 0)
    for rh in range(2):
        block = unpack_half(got_ref[rh * LANES : (rh + 1) * LANES, :])
        for n, r in enumerate(rows_of_half(rh)):
            piece = block[n * 8 : n * 8 + 8, :]
            grad_ref[:, r * LANES : (r + 1) * LANES] = jnp.where(row < RGB, piece, 0.0)
    grad = grad_ref[...]
    grad_stack(grad, taps)
    bias = lax.dot_general(
        jnp.ones((8, PIX), bf16), grad.astype(bf16), (((1,), (1,)), ((), ())), preferred_element_type=f32
    )
    sums = [jnp.zeros((CH, STACK), f32) for _ in range(TIN)]
    for at in range(0, PIX, chunk):
        part = taps[:, at : at + chunk].astype(bf16)
        for t in range(TIN):
            sums[t] += lax.dot_general(
                feat_ref[t, :, at : at + chunk], part, (((1,), (1,)), ((), ())), preferred_element_type=f32
            )
    rows = jnp.concatenate([total.T for total in sums], axis=0)
    rows = jnp.concatenate([rows, jnp.zeros((TIN * STACK, LANES - CH), f32)], axis=1).astype(bf16)
    for h in range(2):
        place = iota((HALF, TIN * STACK), 0)
        source = iota((HALF, TIN * STACK), 1)
        rank = jnp.where(source % 8 < RGB, (source // 8) * RGB + source % 8, -1)
        main = (rank == h * MAIN + place) & (place < MAIN)
        side = rank == 2 * MAIN + (h * HALF + place) // 3
        front = jnp.dot(main.astype(f32).astype(bf16), rows, preferred_element_type=f32)
        back = jnp.dot(side.astype(f32).astype(bf16), rows, preferred_element_type=f32)
        third = (h * HALF + iota((HALF, LANES), 0)) % 3
        tail = jnp.zeros((HALF, LANES), f32)
        for c in range(3):
            tail = jnp.where(third == c, pltpu.roll(back, CH - 32 * c, 1), tail)
        half = jnp.where(iota((HALF, LANES), 1) < CH, front, tail)
        at_bias = (iota((HALF, LANES), 0) == BIAS_ROW) & (iota((HALF, LANES), 1) < CH)
        bias_wide = jnp.concatenate([bias, jnp.zeros((8, LANES - 8), f32)], axis=1)[0:1]
        bias_wide = jnp.where(iota((1, LANES), 1) < RGB, bias_wide, 0.0)
        half = split_bias(jnp.where(at_bias, bias_wide, half))
        for y in range(8):
            out_ref[2 * y + h] = half


def feature_grad_kernel(chunk, grad_ref, weight_ref, out_ref, taps, held):
    step = pl.program_id(0)

    @pl.when(step == 0)
    def _():
        stack_weights(weight_ref, held)
        grad_stack(grad_ref[...], taps)

    part = taps[:, pl.ds(pl.multiple_of(step * chunk, chunk), chunk)].astype(bf16)
    for t in range(TIN):
        out_ref[t] = lax.dot_general(
            held[t].astype(bf16), part, (((0,), (0,)), ((), ())), preferred_element_type=f32
        ).astype(bf16)


def decode_kernel(got_ref, image_ref):
    for rh in range(2):
        block = unpack_half(got_ref[rh * LANES : (rh + 1) * LANES, :])
        for n, r in enumerate(rows_of_half(rh)):
            image_ref[:, r * LANES : (r + 1) * LANES] = block[n * 8 + RGB : n * 8 + 2 * RGB].astype(bf16)


def add_up(got_ref, first, count):
    total = got_ref[first].astype(f32)
    for n in range(first + 1, first + count):
        total = total + got_ref[n].astype(f32)
    return total


def sum_kernel(got_ref, out_ref):
    half = split_bias(add_up(got_ref, 0, got_ref.shape[0]))
    for n in range(out_ref.shape[0]):
        out_ref[n] = half


def finish_kernel(scale, got_ref, weight_ref, bias_ref, held, others):
    for h in range(2):
        held[h * HALF : (h + 1) * HALF, :] = add_up(got_ref, 4 * h, 4) * scale
    bias = held[BIAS_ROW : BIAS_ROW + 1, :]
    bias_ref[...] = bias[:, 0:RGB] + bias[:, RGB : 2 * RGB]
    count = TIN * TAPS * RGB - 2 * MAIN
    lane = iota((count, LANES), 1)
    tail = jnp.zeros((count, LANES), f32)
    for c in range(3):
        turned = pltpu.roll(held[pl.ds(c, count, stride=3), :], (32 + 32 * c) % LANES, 1)
        tail = jnp.where(lane // 32 == c, turned, tail)
    others[0:count, :] = tail
    for n in range(TIN * TAPS):
        at = n * RGB
        if at < 2 * MAIN:
            at = (at // MAIN) * HALF + at % MAIN
            value = held[at : at + RGB, 0:CH]
        else:
            at -= 2 * MAIN
            value = others[at : at + RGB, 0:CH]
        weight_ref[n // TAPS, n % TAPS] = value


VM = pl.BlockSpec(memory_space=pltpu.VMEM)
SM = pl.BlockSpec(memory_space=pltpu.SMEM)
HBM = pl.BlockSpec(memory_space=pltpu.HBM)
LIMIT = 40 * 1024 * 1024
FULL = 64 * 1024 * 1024
message = jax.ShapeDtypeStruct((BOTH, LANES), bf16)


def call(body, out_shape, in_specs, scratch=(), flops=1 << 20, size=1 << 17, name=None, limit=LIMIT, **rest):
    return pl.pallas_call(
        body,
        out_shape=out_shape,
        in_specs=in_specs,
        scratch_shapes=list(scratch),
        compiler_params=pltpu.CompilerParams(vmem_limit_bytes=limit),
        cost_estimate=pl.CostEstimate(flops=flops, bytes_accessed=size, transcendentals=0),
        name=name,
        **rest,
    )


def exchange(rows, axes):
    return lax.all_to_all(rows, axes, 0, 0, tiled=True)


def exchange_tiles(rows):
    return exchange(rows.reshape(SLOTS, 2, LANES), ("y", "z", "c")).reshape(BOTH, LANES)


def per_device(features, conv_weight, bias, blend_profile, tile_ids, reward_grad):
    chunk = 1024
    conv_flops = 2 * STACK * TIN * CH * PIX
    own = lax.axis_index(("y", "z", "c")).reshape(1).astype(jnp.int32)
    feats = jnp.transpose(features[0, 0], (1, 0, 2))

    factors = pltpu.VMEM((BOTH, LANES), f32)
    here = [pltpu.with_memory_space_constraint(x, pltpu.HBM) for x in (feats, conv_weight, bias, reward_grad[0, 0], tile_ids, blend_profile)]
    parts_out, mats, before, after, feats_held = call(
        functools.partial(conv_kernel, chunk),
        (
            pltpu.VMEM((BOTH, LANES), bf16),
            pltpu.VMEM((3 * BOTH, BOTH), bf16),
            factors,
            factors,
            pltpu.VMEM((TIN, CH, PIX), bf16),
        ),
        [HBM, HBM, HBM, HBM, HBM, HBM, SM],
        [
            pltpu.VMEM((TIN, TAPS, RGB, CH), bf16),
            pltpu.SMEM((RGB,), f32),
            pltpu.VMEM((RGB, PIX), bf16),
            pltpu.VMEM((1, SLOTS), jnp.int32),
            pltpu.SMEM((OV,), jnp.int32),
            pltpu.VMEM((TIN, STACK, CH), f32),
            pltpu.VMEM((STACK, PIX), f32),
            pltpu.SemaphoreType.DMA((5,)),
            pltpu.SemaphoreType.DMA((PIX // chunk,)),
        ],
        conv_flops,
        1 << 22,
        "conv",
        out_specs=(VM, VM, VM, VM, VM),
    )(*here, own)
    parts_got = exchange_tiles(parts_out)

    blend_out = call(
        blend_kernel, message, [VM, VM, VM, VM], (), 1 << 27, 1 << 20, "blend", out_specs=VM
    )(parts_got, mats, before, after)
    blend_got = exchange_tiles(blend_out)

    sums, grad_rows = call(
        functools.partial(weight_grad_kernel, chunk),
        (
            jax.ShapeDtypeStruct((16, HALF, LANES), bf16),
            jax.ShapeDtypeStruct((8, PIX), f32),
        ),
        [VM, VM],
        [pltpu.VMEM((STACK, PIX), f32)],
        conv_flops,
        1 << 22,
        "weight_grad",
        out_specs=(VM, VM),
    )(blend_got, feats_held)
    feature_rows = call(
        functools.partial(feature_grad_kernel, chunk),
        jax.ShapeDtypeStruct((TIN, CH, PIX), bf16),
        [
            pl.BlockSpec((8, PIX), lambda i: (0, 0)),
            pl.BlockSpec((TIN, TAPS, RGB, CH), lambda i: (0, 0, 0, 0)),
        ],
        [pltpu.VMEM((STACK, PIX), f32), pltpu.VMEM((TIN, STACK, CH), f32)],
        conv_flops,
        1 << 22,
        "feature_grad",
        grid=(PIX // chunk,),
        out_specs=pl.BlockSpec((TIN, CH, chunk), lambda i: (0, 0, i)),
    )(grad_rows, conv_weight)
    feature_grad = jnp.transpose(feature_rows, (1, 0, 2))[None, None]
    decoded = call(
        decode_kernel, jax.ShapeDtypeStruct((RGB, PIX), bf16), [VM], name="decode", out_specs=VM
    )(blend_got)
    sums = exchange(sums, ("y", "c"))
    sums = call(
        sum_kernel, jax.ShapeDtypeStruct((8, HALF, LANES), bf16), [VM], name="sum_y", out_specs=VM
    )(sums)
    sums = exchange(sums, "z")
    sums, decoded, feature_grad = lax.optimization_barrier((sums, decoded, feature_grad))
    sums = call(
        sum_kernel, jax.ShapeDtypeStruct((8, HALF, LANES), bf16), [VM], name="sum_z", out_specs=VM
    )(sums)
    sums = exchange(sums, ("c", "clip"))
    scale = 1.0 / math.sqrt(4 * SLOTS * PIX)
    weight_grad, bias_grad = call(
        functools.partial(finish_kernel, scale),
        (
            jax.ShapeDtypeStruct((TIN, TAPS, RGB, CH), f32),
            jax.ShapeDtypeStruct((1, RGB), f32),
        ),
        [VM],
        [pltpu.VMEM((2 * HALF, LANES), f32), pltpu.VMEM((24, LANES), f32)],
        name="finish",
        out_specs=(VM, VM),
    )(sums)

    return (decoded[None, None], feature_grad, weight_grad, bias_grad.reshape(RGB))


def solution(mesh):
    parts = Mesh(mesh.devices.reshape(8, 8, 2, 4), ("y", "z", "c", "clip"))
    tile = ("y", "z", "c")
    return jax.shard_map(
        per_device,
        mesh=parts,
        in_specs=(
            P("clip", tile, None, None, None),
            P(),
            P(),
            P(),
            P("clip", None),
            P("clip", tile, None, None),
        ),
        out_specs=(P("clip", tile, None, None), P("clip", tile, None, None, None), P(), P()),
        check_vma=False,
    )
```

```python
import functools
import math

import jax
import jax.numpy as jnp
from jax import lax
from jax.experimental import pallas as pl
from jax.experimental.pallas import tpu as pltpu
from jax.sharding import Mesh
from jax.sharding import PartitionSpec as P

EDGE = 64
OV = 32
PIX = EDGE * EDGE
SLOTS = 128
TX = 16
TY = SLOTS // TX
CH = 96
RGB = 3
TIN = 3
LANES = 128
ROWS = PIX // LANES
BOTH = 2 * SLOTS
TAPS = 9
STACK = TAPS * 8
HALF = 32
MAIN = 30
BIAS_ROW = 30

BOTH = 2 * SLOTS
TAPS = 9
STACK = TAPS * 8
PEERS = 16
GRAD_ROWS = RGB * 16
HALF = 32
MAIN = 30
BIAS_ROW = 30

f32 = jnp.float32
bf16 = jnp.bfloat16


def iota(shape, dim):
    return lax.broadcasted_iota(jnp.int32, shape, dim)


def onehot(mask):
    return jnp.where(mask, 1.0, 0.0).astype(bf16)


def pick_rows(mask, rows):
    return jnp.dot(onehot(mask), rows.astype(bf16), preferred_element_type=f32)


def shift_lanes(value, amount):
    size = value.shape[1]
    amount = amount % size
    return value if amount == 0 else pltpu.roll(value, size - amount, 1)


def profile_at(index, profile_ref):
    out = jnp.zeros(index.shape, f32)
    for m in range(OV):
        out = jnp.where(index == m, profile_ref[m].astype(f32), out)
    return out


def no_further(room):
    return jnp.minimum(room, 1.0)


def route_prep(ids, y, z, mats_ref):
    row = iota((BOTH, 1), 0)
    place = iota((BOTH, SLOTS), 0) // 16
    to_slot = (place // 2) * 16 + z * 2 + place % 2
    spread = iota((BOTH, SLOTS), 1) == to_slot
    target = jnp.sum(jnp.where(spread, jnp.broadcast_to(ids, (BOTH, SLOTS)), 0.0), axis=1, keepdims=True)
    from_slot = y * 16 + iota((SLOTS, BOTH), 1) // 16
    source = jnp.dot(
        jnp.broadcast_to(ids, (8, SLOTS)).astype(bf16),
        onehot(iota((SLOTS, BOTH), 0) == from_slot),
        preferred_element_type=f32,
    )[0:1]
    col = target - jnp.floor(target * (1.0 / TX)) * TX
    lane = iota((1, BOTH), 1)
    want = target + (TX * ((row // 8) % 2) + 1024 * (row % 8)).astype(f32)
    have = source + (TX * ((lane // 8) % 2) + 1024 * (lane % 8)).astype(f32)
    right = jnp.where(col < TX - 1.5, want + 1.0, -9999.0)
    left = jnp.where(col > 0.5, want - 1.0, -9999.0)
    for n, key in enumerate((want, left, right)):
        mats_ref[n * BOTH : (n + 1) * BOTH, :] = onehot(have == key)


def class_prep(ids, profile_ref, k, mats_ref, before_ref, after_ref):
    place = iota((SLOTS, SLOTS), 0)
    spread = iota((SLOTS, SLOTS), 1) == (place % 8) * 16 + place // 8
    own = jnp.sum(jnp.where(spread, jnp.broadcast_to(ids, (SLOTS, SLOTS)), 0.0), axis=1, keepdims=True)
    row = jnp.floor(own * (1.0 / TX))
    col = own - row * TX
    right = jnp.where(col < TX - 1.5, own + 1.0, -9999.0)
    left = jnp.where(col > 0.5, own - 1.0, -9999.0)
    n = 0
    for key in (own, left, right):
        gap = ids - key
        for step in (0.0, -float(TX), float(TX)):
            mats_ref[n * SLOTS : (n + 1) * SLOTS, :] = onehot(gap == step)
            n += 1
    h, par, rx = k // 64, (k // 32) % 2, k % 32
    lane = iota((1, LANES), 1)
    east = lane >= 64
    south = (lane // 8) % 2 == 1
    ry = 2 * (8 * h + lane % 8) + par
    fy = profile_at(jnp.where(south, OV - 1 - ry, ry), profile_ref)
    fy_other = profile_at(jnp.where(south, ry, OV - 1 - ry), profile_ref)
    near = profile_ref[rx].astype(f32)
    far = profile_ref[OV - 1 - rx].astype(f32)
    fx = jnp.where(east, far, near)
    fx_other = jnp.where(east, near, far)
    col_there = no_further(jnp.where(east, TX - 1.0 - col, col))
    row_there = no_further(jnp.where(south, TY - 1.0 - row, row))
    before_ref[...] = jnp.broadcast_to(fx * fy, (8, LANES))
    after_ref[...] = 1.0 / ((fx + col_there * fx_other) * (fy + row_there * fy_other))


def ratio_prep(ids, profile_ref, own_slot, ratio_ref):
    own = jnp.sum(jnp.where(iota((1, SLOTS), 1) == own_slot, ids, 0.0), axis=1, keepdims=True)
    row = jnp.floor(own * (1.0 / TX))
    col = own - row * TX
    lane = iota((1, LANES), 1)
    x = lane % EDGE
    y = 2 * iota((ROWS, LANES), 0) + iota((ROWS, LANES), 1) // EDGE
    at_x = jnp.minimum(x, EDGE - 1 - x)
    at_y = jnp.minimum(y, EDGE - 1 - y)
    fx = profile_at(at_x, profile_ref)
    fx_other = profile_at(OV - 1 - at_x, profile_ref)
    fy = profile_at(at_y, profile_ref)
    fy_other = profile_at(OV - 1 - at_y, profile_ref)
    col_there = no_further(jnp.where(x >= OV, TX - 1.0 - col, col))
    row_there = no_further(jnp.where(y >= OV, TY - 1.0 - row, row))
    ratio_ref[...] = fx * fy / ((fx + col_there * fx_other) * (fy + row_there * fy_other))


def swap_rows(slabs):
    block = jnp.concatenate(slabs, axis=0)
    row = iota((SLOTS, SLOTS), 0)
    return pick_rows(iota((SLOTS, SLOTS), 1) == (row % 16) * 8 + row // 16, block)


def route_kernel(got_ref, mats_ref, out_ref):
    slabs = [got_ref[p].astype(f32) for p in range(PEERS)]
    east = iota((BOTH, LANES), 1) % EDGE >= OV
    totals = []
    for o in range(RGB):
        block = jnp.concatenate([slab[o * 16 : o * 16 + 16] for slab in slabs], axis=0).astype(bf16)
        part = [
            jnp.dot(mats_ref[n * BOTH : (n + 1) * BOTH, :], block, preferred_element_type=f32) for n in range(3)
        ]
        side = jnp.where(east, pltpu.roll(part[2], OV, 1), pltpu.roll(part[1], LANES - OV, 1))
        totals.append(part[0] + side)
    images = swap_rows([slab[GRAD_ROWS : GRAD_ROWS + 8] for slab in slabs])
    for t in range(PEERS):
        rows = [total[t * 16 : t * 16 + 16] for total in totals]
        rows.append(images[(t // 2) * 16 : (t // 2) * 16 + 16])
        out_ref[t] = jnp.concatenate(rows, axis=0).astype(bf16)


def blend_classes(images, mats_ref, before_ref, after_ref):
    source = images * before_ref[0:1, :]
    high = source.astype(bf16)
    low = (source - high.astype(f32)).astype(bf16)
    lane = iota((SLOTS, LANES), 1)
    south = (lane // 8) % 2 == 1
    columns = []
    for d in range(3):
        part = []
        for step in range(3):
            mat = mats_ref[(3 * d + step) * SLOTS : (3 * d + step + 1) * SLOTS, :]
            part.append(
                jnp.dot(mat, high, preferred_element_type=f32) + jnp.dot(mat, low, preferred_element_type=f32)
            )
        across = jnp.where(south, part[1], part[2])
        columns.append(part[0] + jnp.where(south, pltpu.roll(across, 8, 1), pltpu.roll(across, LANES - 8, 1)))
    total = columns[0] + pltpu.roll(jnp.where(lane >= 64, columns[1], columns[2]), 64, 1)
    return total * after_ref[...]


def stack_weights(weight_ref, held):
    held[...] = jnp.zeros_like(held)
    for t in range(TIN):
        for tap in range(TAPS):
            held[t, tap * 8 : tap * 8 + RGB, :] = weight_ref[t, tap].astype(f32)


def conv_kernel(
    chunk,
    feat_ref,
    weight_hbm,
    bias_hbm,
    grad_hbm,
    ids_hbm,
    profile_hbm,
    own_ref,
    out_ref,
    route_ref,
    mats_ref,
    before_ref,
    after_ref,
    ratio_ref,
    feats,
    weight_ref,
    bias_ref,
    grad_ref,
    ids_ref,
    profile_ref,
    held,
    taps,
    turned,
    small_sems,
    sems,
):
    small = [(ids_hbm, ids_ref), (profile_hbm, profile_ref), (weight_hbm, weight_ref), (grad_hbm, grad_ref), (bias_hbm, bias_ref)]
    moves = [pltpu.make_async_copy(src, dst, small_sems.at[n]) for n, (src, dst) in enumerate(small)]
    for move in moves:
        move.start()
    copies = []
    for n in range(PIX // chunk):
        part = pl.ds(n * chunk, chunk)
        copies.append(pltpu.make_async_copy(feat_ref.at[:, :, part], feats.at[:, :, part], sems.at[n]))
        copies[-1].start()
    for move in moves:
        move.wait()
    stack_weights(weight_ref, held)
    kernels = [held[t].astype(bf16) for t in range(TIN)]
    ids = ids_ref[...].astype(f32)
    own = own_ref[0]
    y, z, c = own // 16, (own // 2) % 8, own % 2
    route_prep(ids, y, z, route_ref)
    class_prep(ids, profile_ref, (2 * z + c) * 8 + y, mats_ref, before_ref, after_ref)
    ratio_prep(ids, profile_ref, own, ratio_ref)
    taps[0:8, :] = jnp.zeros((8, PIX), f32)
    taps[0:RGB, :] = grad_ref[...].astype(f32)
    halves = []
    for r in range(ROWS):
        turned[r] = taps[0:8, r * LANES : (r + 1) * LANES]
    for h in range(2):
        halves.append(jnp.concatenate(half_rows(turned, h, RGB), axis=0))
    for n in range(PIX // chunk):
        copies[n].wait()
        total = jnp.zeros((STACK, chunk), f32)
        for t in range(TIN):
            total += jnp.dot(kernels[t], feats[t, :, n * chunk : (n + 1) * chunk], preferred_element_type=f32)
        taps[:, n * chunk : (n + 1) * chunk] = total
    lane = iota((8, PIX), 1)
    image = jnp.zeros((8, PIX), f32)
    for kx in range(3):
        column = jnp.zeros((8, PIX), f32)
        for ky in range(3):
            tap = 3 * ky + kx
            moved = shift_lanes(taps[tap * 8 : tap * 8 + 8, :], (ky - 1) * EDGE)
            if ky == 0:
                moved = jnp.where(lane >= EDGE, moved, 0.0)
            elif ky == 2:
                moved = jnp.where(lane < PIX - EDGE, moved, 0.0)
            column = column + moved
        moved = shift_lanes(column, kx - 1)
        if kx == 0:
            moved = jnp.where(lane % EDGE != 0, moved, 0.0)
        elif kx == 2:
            moved = jnp.where(lane % EDGE != EDGE - 1, moved, 0.0)
        image = image + moved
    row = iota((8, 1), 0)
    shift = jnp.zeros((8, 1), f32)
    for o in range(RGB):
        shift = jnp.where(row == o, bias_ref[o], shift)
    image = image + shift
    for r in range(ROWS):
        turned[r] = image[:, r * LANES : (r + 1) * LANES]
    place = iota((LANES, LANES), 0)
    lanes = onehot(iota((LANES, LANES), 1) == ((place // 32) % 2) * 64 + (place // 64) * 32 + place % 32)
    classes = []
    for h in range(2):
        block = half_rows(turned, h, RGB) + [jnp.zeros((16, LANES), f32)]
        block = jnp.concatenate(block, axis=0).astype(bf16)
        both = lax.dot_general(lanes, block, (((1,), (1,)), ((), ())), preferred_element_type=f32)
        classes.append(jnp.concatenate([both[0:64], both[64:128]], axis=1))
    classes = jnp.concatenate(classes, axis=0)
    for p in range(PEERS):
        out_ref[p] = jnp.concatenate([halves[p % 2], classes[p * 8 : p * 8 + 8]], axis=0).astype(bf16)


def half_rows(turned, h, colours):
    return [turned[qy * 16 + h * 8 : qy * 16 + h * 8 + 8, o, :] for o in range(colours) for qy in range(2)]


def grad_stack(grad, taps):
    lane = iota((8, PIX), 1)
    for kx in range(3):
        moved_x = shift_lanes(grad, 1 - kx)
        if kx == 0:
            moved_x = jnp.where(lane % EDGE != EDGE - 1, moved_x, 0.0)
        elif kx == 2:
            moved_x = jnp.where(lane % EDGE != 0, moved_x, 0.0)
        for ky in range(3):
            moved = shift_lanes(moved_x, (1 - ky) * EDGE)
            if ky == 0:
                moved = jnp.where(lane < PIX - EDGE, moved, 0.0)
            elif ky == 2:
                moved = jnp.where(lane >= EDGE, moved, 0.0)
            tap = 3 * ky + kx
            taps[tap * 8 : tap * 8 + 8, :] = moved


def split_bias(half):
    at = iota((HALF, LANES), 0) == BIAS_ROW
    lane = iota((HALF, LANES), 1)
    total = half + pltpu.roll(half, LANES - RGB, 1)
    high = total.astype(bf16).astype(f32)
    low = pltpu.roll(total - high, RGB, 1)
    pair = jnp.where(lane < RGB, high, jnp.where(lane < 2 * RGB, low, half))
    return jnp.where(at, pair, half)


def weight_grad_kernel(
    chunk, got_ref, feat_ref, ratio_ref, mats_ref, before_ref, after_ref, own_ref, out_ref, grad_ref, taps, turned
):
    sums = [got_ref[h].astype(f32) for h in range(2)]
    for n in range(2, PEERS):
        sums[n % 2] = sums[n % 2] + got_ref[n].astype(f32)
    turned[...] = jnp.zeros_like(turned)
    for h in range(2):
        for o in range(RGB):
            for qy in range(2):
                at = qy * 16 + h * 8
                piece = sums[h][o * 16 + qy * 8 : o * 16 + qy * 8 + 8] * ratio_ref[at : at + 8, :]
                turned[at : at + 8, o, :] = piece.astype(bf16).astype(f32)
    for r in range(ROWS):
        grad_ref[:, r * LANES : (r + 1) * LANES] = turned[r]
    core = own_ref[0] % 2
    images = [got_ref[2 * y + core].astype(f32)[GRAD_ROWS : GRAD_ROWS + 16] for y in range(8)]
    blended = blend_classes(jnp.concatenate(images, axis=0), mats_ref, before_ref, after_ref)
    grad = grad_ref[...]
    grad_stack(grad, taps)
    bias = lax.dot_general(
        jnp.ones((8, PIX), bf16), grad.astype(bf16), (((1,), (1,)), ((), ())), preferred_element_type=f32
    )
    total = jnp.zeros((TIN * CH, STACK), f32)
    for at in range(0, PIX, chunk):
        part = taps[:, at : at + chunk].astype(bf16)
        total += lax.dot_general(
            feat_ref[:, :, at : at + chunk].reshape(TIN * CH, chunk),
            part,
            (((1,), (1,)), ((), ())),
            preferred_element_type=f32,
        )
    rows = jnp.concatenate([total[t * CH : (t + 1) * CH].T for t in range(TIN)], axis=0)
    rows = jnp.concatenate([rows, jnp.zeros((TIN * STACK, LANES - CH), f32)], axis=1).astype(bf16)
    place = iota((4 * HALF, TIN * STACK), 0)
    source = iota((4 * HALF, TIN * STACK), 1)
    rank = jnp.where(source % 8 < RGB, (source // 8) * RGB + source % 8, -1)
    within = place % HALF
    main = (rank == (place // HALF) * MAIN + within) & (within < MAIN) & (place < 2 * HALF)
    offset = place - 2 * HALF - RGB * (rank - 2 * MAIN)
    side = (offset >= 0) & (offset < RGB) & (place >= 2 * HALF) & (rank >= 2 * MAIN)
    pick = jnp.where(main | side, 1.0, 0.0).astype(bf16)
    chosen = jnp.dot(pick, rows, preferred_element_type=f32)
    bias_wide = jnp.concatenate([bias, jnp.zeros((8, LANES - 8), f32)], axis=1)[0:1]
    bias_wide = jnp.where(iota((1, LANES), 1) < RGB, bias_wide, 0.0)
    lane = iota((HALF, LANES), 1)
    at_bias = (iota((HALF, LANES), 0) == BIAS_ROW) & (lane < CH)
    halves = []
    for h in range(2):
        front = chosen[h * HALF : (h + 1) * HALF]
        back = chosen[(2 + h) * HALF : (3 + h) * HALF]
        third = (h * HALF + iota((HALF, LANES), 0)) % 3
        tail = jnp.zeros((HALF, LANES), f32)
        for c in range(3):
            tail = jnp.where(third == c, pltpu.roll(back, CH - 32 * c, 1), tail)
        half = jnp.where(at_bias, bias_wide, jnp.where(lane < CH, front, tail))
        halves.append(split_bias(half))
    for p in range(PEERS):
        out_ref[p] = jnp.concatenate([halves[p % 2], blended[p * 8 : p * 8 + 8]], axis=0).astype(bf16)


def feature_grad_kernel(chunk, grad_ref, weight_ref, out_ref, taps, held):
    step = pl.program_id(0)

    @pl.when(step == 0)
    def _():
        stack_weights(weight_ref, held)
        grad_stack(grad_ref[...], taps)

    part = taps[:, pl.ds(pl.multiple_of(step * chunk, chunk), chunk)].astype(bf16)
    for t in range(TIN):
        out_ref[t] = lax.dot_general(
            held[t].astype(bf16), part, (((0,), (0,)), ((), ())), preferred_element_type=f32
        ).astype(bf16)


def decode_kernel(got_ref, own_ref, image_ref, turned):
    core = own_ref[0] % 2
    images = jnp.concatenate([got_ref[2 * y + core].astype(f32)[HALF : HALF + 16] for y in range(8)], axis=0)
    block = jnp.concatenate([images[:, 0:64], images[:, 64:128]], axis=0).astype(bf16)
    row = iota((BOTH, LANES), 0)
    lane = iota((BOTH, LANES), 1)
    k = (row % 16) * 8 + (row // 16) % 8
    spot = ((k // 32) % 2) * 64 + (row // SLOTS) * 32 + k % 32
    for h in range(2):
        lanes = onehot((lane == spot) & (k // 64 == h))
        tile = lax.dot_general(block, lanes, (((0,), (0,)), ((), ())), preferred_element_type=f32)
        for o in range(RGB):
            for qy in range(2):
                turned[qy * 16 + h * 8 : qy * 16 + h * 8 + 8, o, :] = tile[o * 16 + qy * 8 : o * 16 + qy * 8 + 8]
    for r in range(ROWS):
        image_ref[:, r * LANES : (r + 1) * LANES] = turned[r, 0:RGB, :].astype(bf16)


def sum_z_kernel(got_ref, out_ref):
    slabs = [got_ref[p].astype(f32) for p in range(PEERS)]
    half = slabs[0][0:HALF]
    for slab in slabs[1:]:
        half = half + slab[0:HALF]
    half = split_bias(half)
    images = swap_rows([slab[HALF : HALF + 8] for slab in slabs])
    for t in range(PEERS):
        out_ref[t] = jnp.concatenate([half, images[(t // 2) * 16 : (t // 2) * 16 + 16]], axis=0).astype(bf16)


def sum_y_kernel(got_ref, out_ref):
    halves = []
    for h in range(2):
        half = got_ref[h].astype(f32)[0:HALF]
        for y in range(1, 8):
            half = half + got_ref[2 * y + h].astype(f32)[0:HALF]
        halves.append(split_bias(half))
    both = jnp.concatenate(halves, axis=0).astype(bf16)
    for n in range(out_ref.shape[0]):
        out_ref[n] = both


def finish_kernel(scale, got_ref, weight_ref, bias_ref, held, others):
    total = got_ref[0].astype(f32)
    for n in range(1, got_ref.shape[0]):
        total = total + got_ref[n].astype(f32)
    held[...] = total * scale
    bias = held[BIAS_ROW : BIAS_ROW + 1, :]
    bias_ref[...] = bias[:, 0:RGB] + bias[:, RGB : 2 * RGB]
    count = TIN * TAPS * RGB - 2 * MAIN
    lane = iota((count, LANES), 1)
    tail = jnp.zeros((count, LANES), f32)
    for c in range(3):
        turned = pltpu.roll(held[pl.ds(c, count, stride=3), :], (32 + 32 * c) % LANES, 1)
        tail = jnp.where(lane // 32 == c, turned, tail)
    others[0:count, :] = tail
    for n in range(TIN * TAPS):
        at = n * RGB
        if at < 2 * MAIN:
            at = (at // MAIN) * HALF + at % MAIN
            value = held[at : at + RGB, 0:CH]
        else:
            at -= 2 * MAIN
            value = others[at : at + RGB, 0:CH]
        weight_ref[n // TAPS, n % TAPS] = value


VM = pl.BlockSpec(memory_space=pltpu.VMEM)
SM = pl.BlockSpec(memory_space=pltpu.SMEM)
HBM = pl.BlockSpec(memory_space=pltpu.HBM)
LIMIT = 40 * 1024 * 1024


def call(body, out_shape, in_specs, scratch=(), flops=1 << 20, size=1 << 17, name=None, limit=LIMIT, **rest):
    return pl.pallas_call(
        body,
        out_shape=out_shape,
        in_specs=in_specs,
        scratch_shapes=list(scratch),
        compiler_params=pltpu.CompilerParams(vmem_limit_bytes=limit),
        cost_estimate=pl.CostEstimate(flops=flops, bytes_accessed=size, transcendentals=0),
        name=name,
        **rest,
    )


def exchange(rows, axes):
    return lax.all_to_all(rows, axes, 0, 0, tiled=True)


def message(peers, rows):
    return jax.ShapeDtypeStruct((peers, rows, LANES), bf16)


def per_device(features, conv_weight, bias, blend_profile, tile_ids, reward_grad):
    chunk = 1024
    conv_flops = 2 * STACK * TIN * CH * PIX
    own = lax.axis_index(("y", "z", "c")).reshape(1).astype(jnp.int32)
    feats = jnp.transpose(features[0, 0], (1, 0, 2))
    args = (feats, conv_weight, bias, reward_grad[0, 0], tile_ids, blend_profile)
    here = [pltpu.with_memory_space_constraint(x, pltpu.HBM) for x in args]
    rows, route, mats, before, after, ratio, feats_held = call(
        functools.partial(conv_kernel, 2 * chunk),
        (
            pltpu.VMEM((PEERS, GRAD_ROWS + 8, LANES), bf16),
            pltpu.VMEM((3 * BOTH, BOTH), bf16),
            pltpu.VMEM((9 * SLOTS, SLOTS), bf16),
            pltpu.VMEM((8, LANES), f32),
            pltpu.VMEM((SLOTS, LANES), f32),
            pltpu.VMEM((ROWS, LANES), f32),
            pltpu.VMEM((TIN, CH, PIX), bf16),
        ),
        [HBM, HBM, HBM, HBM, HBM, HBM, SM],
        [
            pltpu.VMEM((TIN, TAPS, RGB, CH), bf16),
            pltpu.SMEM((RGB,), f32),
            pltpu.VMEM((RGB, PIX), bf16),
            pltpu.VMEM((1, SLOTS), jnp.int32),
            pltpu.SMEM((OV,), jnp.int32),
            pltpu.VMEM((TIN, STACK, CH), f32),
            pltpu.VMEM((STACK, PIX), f32),
            pltpu.VMEM((ROWS, 8, LANES), f32),
            pltpu.SemaphoreType.DMA((5,)),
            pltpu.SemaphoreType.DMA((PIX // (2 * chunk),)),
        ],
        conv_flops,
        1 << 22,
        "conv",
        out_specs=(VM,) * 7,
    )(*here, own)
    rows = exchange(rows, ("z", "c"))
    rows = call(
        route_kernel, message(PEERS, GRAD_ROWS + 16), [VM, VM], (), 1 << 27, 1 << 20, "route", out_specs=VM
    )(rows, route)
    rows = exchange(rows, ("y", "c"))
    rows, grad_rows = call(
        functools.partial(weight_grad_kernel, chunk),
        (message(PEERS, HALF + 8), jax.ShapeDtypeStruct((8, PIX), f32)),
        [VM, VM, VM, VM, VM, VM, SM],
        [pltpu.VMEM((STACK, PIX), f32), pltpu.VMEM((ROWS, 8, LANES), f32)],
        conv_flops,
        1 << 22,
        "weight_grad",
        out_specs=(VM, VM),
    )(rows, feats_held, ratio, mats, before, after, own)

    feature_rows = call(
        functools.partial(feature_grad_kernel, chunk),
        jax.ShapeDtypeStruct((TIN, CH, PIX), bf16),
        [
            pl.BlockSpec((8, PIX), lambda i: (0, 0)),
            pl.BlockSpec((TIN, TAPS, RGB, CH), lambda i: (0, 0, 0, 0)),
        ],
        [pltpu.VMEM((STACK, PIX), f32), pltpu.VMEM((TIN, STACK, CH), f32)],
        conv_flops,
        1 << 22,
        "feature_grad",
        grid=(PIX // chunk,),
        out_specs=pl.BlockSpec((TIN, CH, chunk), lambda i: (0, 0, i)),
    )(grad_rows, conv_weight)
    feature_grad = jnp.transpose(feature_rows, (1, 0, 2))[None, None]

    rows = exchange(rows, ("z", "c"))
    rows = call(sum_z_kernel, message(PEERS, HALF + 16), [VM], name="sum_z", out_specs=VM)(rows)
    rows = exchange(rows, ("y", "c"))
    decoded = call(
        decode_kernel,
        jax.ShapeDtypeStruct((RGB, PIX), bf16),
        [VM, SM],
        [pltpu.VMEM((ROWS, 8, LANES), f32)],
        name="decode",
        out_specs=VM,
    )(rows, own)
    rows = call(sum_y_kernel, message(4, 2 * HALF), [VM], name="sum_y", out_specs=VM)(rows)
    rows = exchange(rows, "clip")
    rows, decoded, feature_grad = lax.optimization_barrier((rows, decoded, feature_grad))
    scale = 1.0 / math.sqrt(4 * SLOTS * PIX)
    weight_grad, bias_grad = call(
        functools.partial(finish_kernel, scale),
        (
            jax.ShapeDtypeStruct((TIN, TAPS, RGB, CH), f32),
            jax.ShapeDtypeStruct((1, RGB), f32),
        ),
        [VM],
        [pltpu.VMEM((2 * HALF, LANES), f32), pltpu.VMEM((24, LANES), f32)],
        name="finish",
        out_specs=(VM, VM),
    )(rows)
    return (decoded[None, None], feature_grad, weight_grad, bias_grad.reshape(RGB))


def solution(mesh):
    parts = Mesh(mesh.devices.reshape(8, 8, 2, 4), ("y", "z", "c", "clip"))
    tile = ("y", "z", "c")
    return jax.shard_map(
        per_device,
        mesh=parts,
        in_specs=(
            P("clip", tile, None, None, None),
            P(),
            P(),
            P(),
            P("clip", None),
            P("clip", tile, None, None),
        ),
        out_specs=(P("clip", tile, None, None), P("clip", tile, None, None, None), P(), P()),
        check_vma=False,
    )
```

```python
import functools
import math

import jax
import jax.numpy as jnp
from jax import lax
from jax.experimental import pallas as pl
from jax.experimental.pallas import tpu as pltpu
from jax.sharding import Mesh
from jax.sharding import PartitionSpec as P

EDGE = 64
OV = 32
PIX = EDGE * EDGE
SLOTS = 128
TX = 16
TY = SLOTS // TX
CH = 96
RGB = 3
TIN = 3
LANES = 128
ROWS = PIX // LANES
BOTH = 2 * SLOTS
TAPS = 9
STACK = TAPS * 8
HALF = 32
MAIN = 30
BIAS_ROW = 30

BOTH = 2 * SLOTS
TAPS = 9
STACK = TAPS * 8
PEERS = 16
GRAD_ROWS = RGB * 16
HALF = 32
MAIN = 30
BIAS_ROW = 30

f32 = jnp.float32
bf16 = jnp.bfloat16


def iota(shape, dim):
    return lax.broadcasted_iota(jnp.int32, shape, dim)


def onehot(mask):
    return jnp.where(mask, 1.0, 0.0).astype(bf16)


def pick_rows(mask, rows):
    return jnp.dot(onehot(mask), rows.astype(bf16), preferred_element_type=f32)


def shift_lanes(value, amount):
    size = value.shape[1]
    amount = amount % size
    return value if amount == 0 else pltpu.roll(value, size - amount, 1)


def profile_at(index, profile_ref):
    out = jnp.zeros(index.shape, f32)
    for m in range(OV):
        out = jnp.where(index == m, profile_ref[m].astype(f32), out)
    return out


def no_further(room):
    return jnp.minimum(room, 1.0)


def route_prep(ids, y, z, mats_ref):
    row = iota((BOTH, 1), 0)
    place = iota((BOTH, SLOTS), 0) // 16
    to_slot = (place // 2) * 16 + z * 2 + place % 2
    spread = iota((BOTH, SLOTS), 1) == to_slot
    target = jnp.sum(jnp.where(spread, jnp.broadcast_to(ids, (BOTH, SLOTS)), 0.0), axis=1, keepdims=True)
    from_slot = y * 16 + iota((SLOTS, BOTH), 1) // 16
    source = jnp.dot(
        jnp.broadcast_to(ids, (8, SLOTS)).astype(bf16),
        onehot(iota((SLOTS, BOTH), 0) == from_slot),
        preferred_element_type=f32,
    )[0:1]
    col = target - jnp.floor(target * (1.0 / TX)) * TX
    lane = iota((1, BOTH), 1)
    want = target + (TX * ((row // 8) % 2) + 1024 * (row % 8)).astype(f32)
    have = source + (TX * ((lane // 8) % 2) + 1024 * (lane % 8)).astype(f32)
    right = jnp.where(col < TX - 1.5, want + 1.0, -9999.0)
    left = jnp.where(col > 0.5, want - 1.0, -9999.0)
    for n, key in enumerate((want, left, right)):
        mats_ref[n * BOTH : (n + 1) * BOTH, :] = onehot(have == key)


def class_prep(ids, profile_ref, y, z, c, mats_ref, before_ref, after_ref):
    k = (2 * z + c) * 8 + y
    place = iota((SLOTS, SLOTS), 0)
    leaves = (4 * (((place // 8) % 2) ^ c) + place % 4) * 16 + (place // 16) * 2 + (place // 4) % 2
    spread = iota((SLOTS, SLOTS), 1) == leaves
    place = iota((SLOTS, SLOTS), 1)
    comes = (place // 16) * 16 + (place % 8) * 2 + (((place // 8) % 2) ^ (y // 4))
    come = jnp.dot(
        jnp.broadcast_to(ids, (8, SLOTS)).astype(bf16),
        onehot(iota((SLOTS, SLOTS), 0) == comes),
        preferred_element_type=f32,
    )[0:1]
    own = jnp.sum(jnp.where(spread, jnp.broadcast_to(ids, (SLOTS, SLOTS)), 0.0), axis=1, keepdims=True)
    row = jnp.floor(own * (1.0 / TX))
    col = own - row * TX
    right = jnp.where(col < TX - 1.5, own + 1.0, -9999.0)
    left = jnp.where(col > 0.5, own - 1.0, -9999.0)
    n = 0
    for key in (own, left, right):
        gap = come - key
        for step in (0.0, -float(TX), float(TX)):
            mats_ref[n * SLOTS : (n + 1) * SLOTS, :] = onehot(gap == step)
            n += 1
    h, par, rx = k // 64, (k // 32) % 2, k % 32
    lane = iota((1, LANES), 1)
    east = lane >= 64
    south = (lane // 8) % 2 == 1
    ry = 2 * (8 * h + lane % 8) + par
    fy = profile_at(jnp.where(south, OV - 1 - ry, ry), profile_ref)
    fy_other = profile_at(jnp.where(south, ry, OV - 1 - ry), profile_ref)
    near = profile_ref[rx].astype(f32)
    far = profile_ref[OV - 1 - rx].astype(f32)
    fx = jnp.where(east, far, near)
    fx_other = jnp.where(east, near, far)
    col_there = no_further(jnp.where(east, TX - 1.0 - col, col))
    row_there = no_further(jnp.where(south, TY - 1.0 - row, row))
    before_ref[...] = jnp.broadcast_to(fx * fy, (8, LANES))
    after_ref[...] = 1.0 / ((fx + col_there * fx_other) * (fy + row_there * fy_other))


def ratio_prep(ids, profile_ref, own_slot, ratio_ref):
    own = jnp.sum(jnp.where(iota((1, SLOTS), 1) == own_slot, ids, 0.0), axis=1, keepdims=True)
    row = jnp.floor(own * (1.0 / TX))
    col = own - row * TX
    lane = iota((1, LANES), 1)
    x = lane % EDGE
    y = 2 * iota((ROWS, LANES), 0) + iota((ROWS, LANES), 1) // EDGE
    at_x = jnp.minimum(x, EDGE - 1 - x)
    at_y = jnp.minimum(y, EDGE - 1 - y)
    fx = profile_at(at_x, profile_ref)
    fx_other = profile_at(OV - 1 - at_x, profile_ref)
    fy = profile_at(at_y, profile_ref)
    fy_other = profile_at(OV - 1 - at_y, profile_ref)
    col_there = no_further(jnp.where(x >= OV, TX - 1.0 - col, col))
    row_there = no_further(jnp.where(y >= OV, TY - 1.0 - row, row))
    ratio_ref[...] = fx * fy / ((fx + col_there * fx_other) * (fy + row_there * fy_other))


def pass_on(slabs, core):
    block = jnp.concatenate(slabs, axis=0)
    place = iota((SLOTS, SLOTS), 0)
    y = place // 16
    peer = (place % 8) * 2 + (core ^ (y // 4))
    return pick_rows(iota((SLOTS, SLOTS), 1) == peer * 8 + ((place // 8) % 2) * 4 + y % 4, block)


def route_kernel(got_ref, mats_ref, own_ref, out_ref):
    slabs = [got_ref[p].astype(f32) for p in range(PEERS)]
    east = iota((BOTH, LANES), 1) % EDGE >= OV
    totals = []
    for o in range(RGB):
        block = jnp.concatenate([slab[o * 16 : o * 16 + 16] for slab in slabs], axis=0).astype(bf16)
        part = [
            jnp.dot(mats_ref[n * BOTH : (n + 1) * BOTH, :], block, preferred_element_type=f32) for n in range(3)
        ]
        side = jnp.where(east, pltpu.roll(part[2], OV, 1), pltpu.roll(part[1], LANES - OV, 1))
        totals.append(part[0] + side)
    images = pass_on([slab[GRAD_ROWS : GRAD_ROWS + 8] for slab in slabs], own_ref[0] % 2)
    for t in range(PEERS):
        rows = [total[t * 16 : t * 16 + 16] for total in totals]
        rows.append(images[t * 8 : t * 8 + 8])
        out_ref[t] = jnp.concatenate(rows, axis=0).astype(bf16)


def blend_classes(images, mats_ref, before_ref, after_ref):
    source = images * before_ref[0:1, :]
    high = source.astype(bf16)
    low = (source - high.astype(f32)).astype(bf16)
    lane = iota((SLOTS, LANES), 1)
    south = (lane // 8) % 2 == 1
    columns = []
    for d in range(3):
        part = []
        for step in range(3):
            mat = mats_ref[(3 * d + step) * SLOTS : (3 * d + step + 1) * SLOTS, :]
            part.append(
                jnp.dot(mat, high, preferred_element_type=f32) + jnp.dot(mat, low, preferred_element_type=f32)
            )
        across = jnp.where(south, part[1], part[2])
        columns.append(part[0] + jnp.where(south, pltpu.roll(across, 8, 1), pltpu.roll(across, LANES - 8, 1)))
    total = columns[0] + pltpu.roll(jnp.where(lane >= 64, columns[1], columns[2]), 64, 1)
    return total * after_ref[...]


def stack_weights(weight_ref, held):
    held[...] = jnp.zeros_like(held)
    for t in range(TIN):
        for tap in range(TAPS):
            held[t, tap * 8 : tap * 8 + RGB, :] = weight_ref[t, tap].astype(f32)


def conv_kernel(
    chunk,
    feat_ref,
    weight_hbm,
    bias_hbm,
    grad_hbm,
    ids_hbm,
    profile_hbm,
    own_ref,
    out_ref,
    route_ref,
    mats_ref,
    before_ref,
    after_ref,
    ratio_ref,
    feats,
    stacked_ref,
    weight_ref,
    bias_ref,
    grad_ref,
    ids_ref,
    profile_ref,
    held,
    taps,
    turned,
    small_sems,
    sems,
):
    small = [(ids_hbm, ids_ref), (profile_hbm, profile_ref), (weight_hbm, weight_ref), (grad_hbm, grad_ref), (bias_hbm, bias_ref)]
    moves = [pltpu.make_async_copy(src, dst, small_sems.at[n]) for n, (src, dst) in enumerate(small)]
    for move in moves:
        move.start()
    copies = []
    for n in range(PIX // chunk):
        part = pl.ds(n * chunk, chunk)
        copies.append(pltpu.make_async_copy(feat_ref.at[:, :, part], feats.at[:, :, part], sems.at[n]))
        copies[-1].start()
    for move in moves:
        move.wait()
    stack_weights(weight_ref, held)
    kernels = [held[t].astype(bf16) for t in range(TIN)]
    for t in range(TIN):
        stacked_ref[t] = kernels[t]
    ids = ids_ref[...].astype(f32)
    own = own_ref[0]
    y, z, c = own // 16, (own // 2) % 8, own % 2
    route_prep(ids, y, z, route_ref)
    class_prep(ids, profile_ref, y, z, c, mats_ref, before_ref, after_ref)
    ratio_prep(ids, profile_ref, own, ratio_ref)
    taps[0:8, :] = jnp.zeros((8, PIX), f32)
    taps[0:RGB, :] = grad_ref[...].astype(f32)
    halves = []
    for r in range(ROWS):
        turned[r] = taps[0:8, r * LANES : (r + 1) * LANES]
    for h in range(2):
        halves.append(jnp.concatenate(half_rows(turned, h, RGB), axis=0))
    for n in range(PIX // chunk):
        copies[n].wait()
        total = jnp.zeros((STACK, chunk), f32)
        for t in range(TIN):
            total += jnp.dot(kernels[t], feats[t, :, n * chunk : (n + 1) * chunk], preferred_element_type=f32)
        taps[:, n * chunk : (n + 1) * chunk] = total
    lane = iota((8, PIX), 1)
    image = jnp.zeros((8, PIX), f32)
    for kx in range(3):
        column = jnp.zeros((8, PIX), f32)
        for ky in range(3):
            tap = 3 * ky + kx
            moved = shift_lanes(taps[tap * 8 : tap * 8 + 8, :], (ky - 1) * EDGE)
            if ky == 0:
                moved = jnp.where(lane >= EDGE, moved, 0.0)
            elif ky == 2:
                moved = jnp.where(lane < PIX - EDGE, moved, 0.0)
            column = column + moved
        moved = shift_lanes(column, kx - 1)
        if kx == 0:
            moved = jnp.where(lane % EDGE != 0, moved, 0.0)
        elif kx == 2:
            moved = jnp.where(lane % EDGE != EDGE - 1, moved, 0.0)
        image = image + moved
    row = iota((8, 1), 0)
    shift = jnp.zeros((8, 1), f32)
    for o in range(RGB):
        shift = jnp.where(row == o, bias_ref[o], shift)
    image = image + shift
    for r in range(ROWS):
        turned[r] = image[:, r * LANES : (r + 1) * LANES]
    place = iota((LANES, LANES), 0)
    k = (((place // 16) % 4) * 2 + (place // 4) % 2) * 8 + 4 * (((place // 8) % 2) ^ c) + place % 4
    lanes = onehot(iota((LANES, LANES), 1) == (k // 32) * 64 + (place // 64) * 32 + k % 32)
    classes = []
    for h in range(2):
        block = half_rows(turned, h, RGB) + [jnp.zeros((16, LANES), f32)]
        block = jnp.concatenate(block, axis=0).astype(bf16)
        both = lax.dot_general(lanes, block, (((1,), (1,)), ((), ())), preferred_element_type=f32)
        classes.append(jnp.concatenate([both[0:64], both[64:128]], axis=1))
    classes = jnp.concatenate(classes, axis=0)
    for p in range(PEERS):
        out_ref[p] = jnp.concatenate([halves[p % 2], classes[p * 8 : p * 8 + 8]], axis=0).astype(bf16)


def half_rows(turned, h, colours):
    return [turned[qy * 16 + h * 8 : qy * 16 + h * 8 + 8, o, :] for o in range(colours) for qy in range(2)]


def grad_stack(grad, taps):
    lane = iota((8, PIX), 1)
    for kx in range(3):
        moved_x = shift_lanes(grad, 1 - kx)
        if kx == 0:
            moved_x = jnp.where(lane % EDGE != EDGE - 1, moved_x, 0.0)
        elif kx == 2:
            moved_x = jnp.where(lane % EDGE != 0, moved_x, 0.0)
        for ky in range(3):
            moved = shift_lanes(moved_x, (1 - ky) * EDGE)
            if ky == 0:
                moved = jnp.where(lane < PIX - EDGE, moved, 0.0)
            elif ky == 2:
                moved = jnp.where(lane >= EDGE, moved, 0.0)
            tap = 3 * ky + kx
            taps[tap * 8 : tap * 8 + 8, :] = moved


def split_bias(half):
    at = iota((HALF, LANES), 0) == BIAS_ROW
    lane = iota((HALF, LANES), 1)
    total = half + pltpu.roll(half, LANES - RGB, 1)
    high = total.astype(bf16).astype(f32)
    low = pltpu.roll(total - high, RGB, 1)
    pair = jnp.where(lane < RGB, high, jnp.where(lane < 2 * RGB, low, half))
    return jnp.where(at, pair, half)


def weight_grad_kernel(
    chunk, got_ref, feat_ref, ratio_ref, mats_ref, before_ref, after_ref, out_ref, stack_ref, taps, turned
):
    sums = [got_ref[h].astype(f32) for h in range(2)]
    for n in range(2, PEERS):
        sums[n % 2] = sums[n % 2] + got_ref[n].astype(f32)
    turned[...] = jnp.zeros_like(turned)
    for h in range(2):
        for o in range(RGB):
            for qy in range(2):
                at = qy * 16 + h * 8
                piece = sums[h][o * 16 + qy * 8 : o * 16 + qy * 8 + 8] * ratio_ref[at : at + 8, :]
                turned[at : at + 8, o, :] = piece.astype(bf16).astype(f32)
    grad = jnp.concatenate([turned[r] for r in range(ROWS)], axis=1)
    images = [got_ref[n].astype(f32)[GRAD_ROWS : GRAD_ROWS + 8] for n in range(PEERS)]
    blended = blend_classes(jnp.concatenate(images, axis=0), mats_ref, before_ref, after_ref)
    grad_stack(grad, taps)
    bias = lax.dot_general(
        jnp.ones((8, PIX), bf16), grad.astype(bf16), (((1,), (1,)), ((), ())), preferred_element_type=f32
    )
    total = jnp.zeros((TIN * CH, STACK), f32)
    for at in range(0, PIX, chunk):
        part = taps[:, at : at + chunk].astype(bf16)
        stack_ref[:, at : at + chunk] = part
        total += lax.dot_general(
            feat_ref[:, :, at : at + chunk].reshape(TIN * CH, chunk),
            part,
            (((1,), (1,)), ((), ())),
            preferred_element_type=f32,
        )
    rows = jnp.concatenate([total[t * CH : (t + 1) * CH].T for t in range(TIN)], axis=0)
    rows = jnp.concatenate([rows, jnp.zeros((TIN * STACK, LANES - CH), f32)], axis=1).astype(bf16)
    place = iota((4 * HALF, TIN * STACK), 0)
    source = iota((4 * HALF, TIN * STACK), 1)
    rank = jnp.where(source % 8 < RGB, (source // 8) * RGB + source % 8, -1)
    within = place % HALF
    main = (rank == (place // HALF) * MAIN + within) & (within < MAIN) & (place < 2 * HALF)
    offset = place - 2 * HALF - RGB * (rank - 2 * MAIN)
    side = (offset >= 0) & (offset < RGB) & (place >= 2 * HALF) & (rank >= 2 * MAIN)
    pick = jnp.where(main | side, 1.0, 0.0).astype(bf16)
    chosen = jnp.dot(pick, rows, preferred_element_type=f32)
    bias_wide = jnp.concatenate([bias, jnp.zeros((8, LANES - 8), f32)], axis=1)[0:1]
    bias_wide = jnp.where(iota((1, LANES), 1) < RGB, bias_wide, 0.0)
    lane = iota((HALF, LANES), 1)
    at_bias = (iota((HALF, LANES), 0) == BIAS_ROW) & (lane < CH)
    halves = []
    for h in range(2):
        front = chosen[h * HALF : (h + 1) * HALF]
        back = chosen[(2 + h) * HALF : (3 + h) * HALF]
        third = (h * HALF + iota((HALF, LANES), 0)) % 3
        tail = jnp.zeros((HALF, LANES), f32)
        for c in range(3):
            tail = jnp.where(third == c, pltpu.roll(back, CH - 32 * c, 1), tail)
        half = jnp.where(at_bias, bias_wide, jnp.where(lane < CH, front, tail))
        halves.append(split_bias(half))
    for p in range(PEERS):
        out_ref[p] = jnp.concatenate([halves[p % 2], blended[p * 8 : p * 8 + 8]], axis=0).astype(bf16)


def feature_grad_kernel(stack_ref, weight_ref, out_ref):
    for t in range(TIN):
        out_ref[t] = lax.dot_general(
            weight_ref[t], stack_ref[...], (((0,), (0,)), ((), ())), preferred_element_type=f32
        ).astype(bf16)


def decode_kernel(got_ref, own_ref, image_ref, turned):
    images = jnp.concatenate([got_ref[n].astype(f32)[HALF : HALF + 8] for n in range(PEERS)], axis=0)
    block = jnp.concatenate([images[:, 0:64], images[:, 64:128]], axis=0).astype(bf16)
    row = iota((BOTH, LANES), 0)
    lane = iota((BOTH, LANES), 1)
    k = ((row % 8) * 2 + (((row // 8) % 2) ^ (own_ref[0] // 64))) * 8 + (row // 16) % 8
    spot = ((k // 32) % 2) * 64 + (row // SLOTS) * 32 + k % 32
    for h in range(2):
        lanes = onehot((lane == spot) & (k // 64 == h))
        tile = lax.dot_general(block, lanes, (((0,), (0,)), ((), ())), preferred_element_type=f32)
        for o in range(RGB):
            for qy in range(2):
                turned[qy * 16 + h * 8 : qy * 16 + h * 8 + 8, o, :] = tile[o * 16 + qy * 8 : o * 16 + qy * 8 + 8]
    for r in range(ROWS):
        image_ref[:, r * LANES : (r + 1) * LANES] = turned[r, 0:RGB, :].astype(bf16)


def sum_z_kernel(got_ref, own_ref, out_ref):
    slabs = [got_ref[p].astype(f32) for p in range(PEERS)]
    half = slabs[0][0:HALF]
    for slab in slabs[1:]:
        half = half + slab[0:HALF]
    half = split_bias(half)
    images = pass_on([slab[HALF : HALF + 8] for slab in slabs], own_ref[0] % 2)
    for t in range(PEERS):
        out_ref[t] = jnp.concatenate([half, images[t * 8 : t * 8 + 8]], axis=0).astype(bf16)


def sum_y_kernel(got_ref, out_ref):
    halves = []
    for h in range(2):
        half = got_ref[h].astype(f32)[0:HALF]
        for y in range(1, 8):
            half = half + got_ref[2 * y + h].astype(f32)[0:HALF]
        halves.append(split_bias(half))
    both = jnp.concatenate(halves, axis=0).astype(bf16)
    for n in range(out_ref.shape[0]):
        out_ref[n] = both


def finish_kernel(scale, got_ref, weight_ref, bias_ref, held, others):
    total = got_ref[0].astype(f32)
    for n in range(1, got_ref.shape[0]):
        total = total + got_ref[n].astype(f32)
    held[...] = total * scale
    bias = held[BIAS_ROW : BIAS_ROW + 1, :]
    bias_ref[...] = bias[:, 0:RGB] + bias[:, RGB : 2 * RGB]
    count = TIN * TAPS * RGB - 2 * MAIN
    lane = iota((count, LANES), 1)
    tail = jnp.zeros((count, LANES), f32)
    for c in range(3):
        turned = pltpu.roll(held[pl.ds(c, count, stride=3), :], (32 + 32 * c) % LANES, 1)
        tail = jnp.where(lane // 32 == c, turned, tail)
    others[0:count, :] = tail
    for n in range(TIN * TAPS):
        at = n * RGB
        if at < 2 * MAIN:
            at = (at // MAIN) * HALF + at % MAIN
            value = held[at : at + RGB, 0:CH]
        else:
            at -= 2 * MAIN
            value = others[at : at + RGB, 0:CH]
        weight_ref[n // TAPS, n % TAPS] = value


VM = pl.BlockSpec(memory_space=pltpu.VMEM)
SM = pl.BlockSpec(memory_space=pltpu.SMEM)
HBM = pl.BlockSpec(memory_space=pltpu.HBM)
LIMIT = 40 * 1024 * 1024


def call(body, out_shape, in_specs, scratch=(), flops=1 << 20, size=1 << 17, name=None, limit=LIMIT, **rest):
    return pl.pallas_call(
        body,
        out_shape=out_shape,
        in_specs=in_specs,
        scratch_shapes=list(scratch),
        compiler_params=pltpu.CompilerParams(vmem_limit_bytes=limit),
        cost_estimate=pl.CostEstimate(flops=flops, bytes_accessed=size, transcendentals=0),
        name=name,
        **rest,
    )


def exchange(rows, axes):
    return lax.all_to_all(rows, axes, 0, 0, tiled=True)


def message(peers, rows):
    return jax.ShapeDtypeStruct((peers, rows, LANES), bf16)


def per_device(features, conv_weight, bias, blend_profile, tile_ids, reward_grad):
    chunk = 1024
    conv_flops = 2 * STACK * TIN * CH * PIX
    own = lax.axis_index(("y", "z", "c")).reshape(1).astype(jnp.int32)
    feats = jnp.transpose(features[0, 0], (1, 0, 2))
    args = (feats, conv_weight, bias, reward_grad[0, 0], tile_ids, blend_profile)
    here = [pltpu.with_memory_space_constraint(x, pltpu.HBM) for x in args]
    rows, route, mats, before, after, ratio, feats_held, weights_held = call(
        functools.partial(conv_kernel, 2 * chunk),
        (
            pltpu.VMEM((PEERS, GRAD_ROWS + 8, LANES), bf16),
            pltpu.VMEM((3 * BOTH, BOTH), bf16),
            pltpu.VMEM((9 * SLOTS, SLOTS), bf16),
            pltpu.VMEM((8, LANES), f32),
            pltpu.VMEM((SLOTS, LANES), f32),
            pltpu.VMEM((ROWS, LANES), f32),
            pltpu.VMEM((TIN, CH, PIX), bf16),
            pltpu.VMEM((TIN, STACK, CH), bf16),
        ),
        [HBM, HBM, HBM, HBM, HBM, HBM, SM],
        [
            pltpu.VMEM((TIN, TAPS, RGB, CH), bf16),
            pltpu.SMEM((RGB,), f32),
            pltpu.VMEM((RGB, PIX), bf16),
            pltpu.VMEM((1, SLOTS), jnp.int32),
            pltpu.SMEM((OV,), jnp.int32),
            pltpu.VMEM((TIN, STACK, CH), f32),
            pltpu.VMEM((STACK, PIX), f32),
            pltpu.VMEM((ROWS, 8, LANES), f32),
            pltpu.SemaphoreType.DMA((5,)),
            pltpu.SemaphoreType.DMA((PIX // (2 * chunk),)),
        ],
        conv_flops,
        1 << 22,
        "conv",
        out_specs=(VM,) * 8,
    )(*here, own)
    rows = exchange(rows, ("z", "c"))
    rows = call(
        route_kernel, message(PEERS, GRAD_ROWS + 8), [VM, VM, SM], (), 1 << 27, 1 << 20, "route", out_specs=VM
    )(rows, route, own)
    rows = exchange(rows, ("y", "c"))
    rows, stack = call(
        functools.partial(weight_grad_kernel, chunk),
        (message(PEERS, HALF + 8), jax.ShapeDtypeStruct((STACK, PIX), bf16)),
        [VM, VM, VM, VM, VM, VM],
        [pltpu.VMEM((STACK, PIX), f32), pltpu.VMEM((ROWS, 8, LANES), f32)],
        conv_flops,
        1 << 22,
        "weight_grad",
        out_specs=(VM, VM),
    )(rows, feats_held, ratio, mats, before, after)

    feature_rows = call(
        feature_grad_kernel,
        jax.ShapeDtypeStruct((TIN, CH, PIX), bf16),
        [
            pl.BlockSpec((STACK, chunk), lambda i: (0, i)),
            pl.BlockSpec((TIN, STACK, CH), lambda i: (0, 0, 0)),
        ],
        (),
        conv_flops,
        1 << 22,
        "feature_grad",
        grid=(PIX // chunk,),
        out_specs=pl.BlockSpec((TIN, CH, chunk), lambda i: (0, 0, i)),
    )(stack, weights_held)
    feature_grad = jnp.transpose(feature_rows, (1, 0, 2))[None, None]

    rows = exchange(rows, ("z", "c"))
    rows = call(sum_z_kernel, message(PEERS, HALF + 8), [VM, SM], name="sum_z", out_specs=VM)(rows, own)
    rows = exchange(rows, ("y", "c"))
    decoded = call(
        decode_kernel,
        jax.ShapeDtypeStruct((RGB, PIX), bf16),
        [VM, SM],
        [pltpu.VMEM((ROWS, 8, LANES), f32)],
        name="decode",
        out_specs=VM,
    )(rows, own)
    rows = call(sum_y_kernel, message(4, 2 * HALF), [VM], name="sum_y", out_specs=VM)(rows)
    rows = exchange(rows, "clip")
    rows, decoded, feature_grad = lax.optimization_barrier((rows, decoded, feature_grad))
    scale = 1.0 / math.sqrt(4 * SLOTS * PIX)
    weight_grad, bias_grad = call(
        functools.partial(finish_kernel, scale),
        (
            jax.ShapeDtypeStruct((TIN, TAPS, RGB, CH), f32),
            jax.ShapeDtypeStruct((1, RGB), f32),
        ),
        [VM],
        [pltpu.VMEM((2 * HALF, LANES), f32), pltpu.VMEM((24, LANES), f32)],
        name="finish",
        out_specs=(VM, VM),
    )(rows)
    return (decoded[None, None], feature_grad, weight_grad, bias_grad.reshape(RGB))


def solution(mesh):
    parts = Mesh(mesh.devices.reshape(8, 8, 2, 4), ("y", "z", "c", "clip"))
    tile = ("y", "z", "c")
    return jax.shard_map(
        per_device,
        mesh=parts,
        in_specs=(
            P("clip", tile, None, None, None),
            P(),
            P(),
            P(),
            P("clip", None),
            P("clip", tile, None, None),
        ),
        out_specs=(P("clip", tile, None, None), P("clip", tile, None, None, None), P(), P()),
        check_vma=False,
    )
```

```python
import functools
import math

import jax
import jax.numpy as jnp
from jax import lax
from jax.experimental import pallas as pl
from jax.experimental.pallas import tpu as pltpu
from jax.sharding import Mesh
from jax.sharding import PartitionSpec as P

EDGE = 64
OV = 32
PIX = EDGE * EDGE
SLOTS = 128
TX = 16
TY = SLOTS // TX
CH = 96
RGB = 3
TIN = 3
LANES = 128
ROWS = PIX // LANES
BOTH = 2 * SLOTS
TAPS = 9
STACK = TAPS * 8
PARTS = 4
PART = 16
MAIN = 15
BIAS_ROW = 15

BOTH = 2 * SLOTS
TAPS = 9
STACK = TAPS * 8
PEERS = 16
GRAD_ROWS = RGB * 16
PARTS = 4
PART = 16
MAIN = 15
BIAS_ROW = 15

f32 = jnp.float32
bf16 = jnp.bfloat16


def iota(shape, dim):
    return lax.broadcasted_iota(jnp.int32, shape, dim)


def onehot(mask):
    return jnp.where(mask, 1.0, 0.0).astype(bf16)


def pick_rows(mask, rows):
    return jnp.dot(onehot(mask), rows.astype(bf16), preferred_element_type=f32)


def shift_lanes(value, amount):
    size = value.shape[1]
    amount = amount % size
    return value if amount == 0 else pltpu.roll(value, size - amount, 1)


def profile_at(index, profile_ref):
    out = jnp.zeros(index.shape, f32)
    for m in range(OV):
        out = jnp.where(index == m, profile_ref[m].astype(f32), out)
    return out


def no_further(room):
    return jnp.minimum(room, 1.0)


def route_prep(ids, y, z, mats_ref):
    row = iota((BOTH, 1), 0)
    place = iota((BOTH, SLOTS), 0) // 16
    to_slot = (place // 2) * 16 + z * 2 + place % 2
    spread = iota((BOTH, SLOTS), 1) == to_slot
    target = jnp.sum(jnp.where(spread, jnp.broadcast_to(ids, (BOTH, SLOTS)), 0.0), axis=1, keepdims=True)
    from_slot = y * 16 + iota((SLOTS, BOTH), 1) // 16
    source = jnp.dot(
        jnp.broadcast_to(ids, (8, SLOTS)).astype(bf16),
        onehot(iota((SLOTS, BOTH), 0) == from_slot),
        preferred_element_type=f32,
    )[0:1]
    col = target - jnp.floor(target * (1.0 / TX)) * TX
    lane = iota((1, BOTH), 1)
    want = target + (TX * ((row // 8) % 2) + 1024 * (row % 8)).astype(f32)
    have = source + (TX * ((lane // 8) % 2) + 1024 * (lane % 8)).astype(f32)
    right = jnp.where(col < TX - 1.5, want + 1.0, -9999.0)
    left = jnp.where(col > 0.5, want - 1.0, -9999.0)
    for n, key in enumerate((want, left, right)):
        mats_ref[n * BOTH : (n + 1) * BOTH, :] = onehot(have == key)


def class_prep(ids, profile_ref, y, z, c, mats_ref, before_ref, after_ref):
    k = (2 * z + c) * 8 + y
    place = iota((SLOTS, SLOTS), 0)
    leaves = (4 * (((place // 8) % 2) ^ c) + place % 4) * 16 + (place // 16) * 2 + (place // 4) % 2
    spread = iota((SLOTS, SLOTS), 1) == leaves
    place = iota((SLOTS, SLOTS), 1)
    comes = (place // 16) * 16 + (place % 8) * 2 + (((place // 8) % 2) ^ (y // 4))
    come = jnp.dot(
        jnp.broadcast_to(ids, (8, SLOTS)).astype(bf16),
        onehot(iota((SLOTS, SLOTS), 0) == comes),
        preferred_element_type=f32,
    )[0:1]
    own = jnp.sum(jnp.where(spread, jnp.broadcast_to(ids, (SLOTS, SLOTS)), 0.0), axis=1, keepdims=True)
    row = jnp.floor(own * (1.0 / TX))
    col = own - row * TX
    right = jnp.where(col < TX - 1.5, own + 1.0, -9999.0)
    left = jnp.where(col > 0.5, own - 1.0, -9999.0)
    n = 0
    for key in (own, left, right):
        gap = come - key
        for step in (0.0, -float(TX), float(TX)):
            mats_ref[n * SLOTS : (n + 1) * SLOTS, :] = onehot(gap == step)
            n += 1
    h, par, rx = k // 64, (k // 32) % 2, k % 32
    lane = iota((1, LANES), 1)
    east = lane >= 64
    south = (lane // 8) % 2 == 1
    ry = 2 * (8 * h + lane % 8) + par
    fy = profile_at(jnp.where(south, OV - 1 - ry, ry), profile_ref)
    fy_other = profile_at(jnp.where(south, ry, OV - 1 - ry), profile_ref)
    near = profile_ref[rx].astype(f32)
    far = profile_ref[OV - 1 - rx].astype(f32)
    fx = jnp.where(east, far, near)
    fx_other = jnp.where(east, near, far)
    col_there = no_further(jnp.where(east, TX - 1.0 - col, col))
    row_there = no_further(jnp.where(south, TY - 1.0 - row, row))
    before_ref[...] = jnp.broadcast_to(fx * fy, (8, LANES))
    after_ref[...] = 1.0 / ((fx + col_there * fx_other) * (fy + row_there * fy_other))


def ratio_prep(ids, profile_ref, own_slot, ratio_ref):
    own = jnp.sum(jnp.where(iota((1, SLOTS), 1) == own_slot, ids, 0.0), axis=1, keepdims=True)
    row = jnp.floor(own * (1.0 / TX))
    col = own - row * TX
    lane = iota((1, LANES), 1)
    x = lane % EDGE
    y = 2 * iota((ROWS, LANES), 0) + iota((ROWS, LANES), 1) // EDGE
    at_x = jnp.minimum(x, EDGE - 1 - x)
    at_y = jnp.minimum(y, EDGE - 1 - y)
    fx = profile_at(at_x, profile_ref)
    fx_other = profile_at(OV - 1 - at_x, profile_ref)
    fy = profile_at(at_y, profile_ref)
    fy_other = profile_at(OV - 1 - at_y, profile_ref)
    col_there = no_further(jnp.where(x >= OV, TX - 1.0 - col, col))
    row_there = no_further(jnp.where(y >= OV, TY - 1.0 - row, row))
    ratio_ref[...] = fx * fy / ((fx + col_there * fx_other) * (fy + row_there * fy_other))


def pass_on(slabs, core):
    block = jnp.concatenate(slabs, axis=0)
    place = iota((SLOTS, SLOTS), 0)
    y = place // 16
    peer = (place % 8) * 2 + (core ^ (y // 4))
    return pick_rows(iota((SLOTS, SLOTS), 1) == peer * 8 + ((place // 8) % 2) * 4 + y % 4, block)


def route_kernel(got_ref, mats_ref, own_ref, out_ref):
    slabs = [got_ref[p].astype(f32) for p in range(PEERS)]
    east = iota((BOTH, LANES), 1) % EDGE >= OV
    totals = []
    for o in range(RGB):
        block = jnp.concatenate([slab[o * 16 : o * 16 + 16] for slab in slabs], axis=0).astype(bf16)
        part = [
            jnp.dot(mats_ref[n * BOTH : (n + 1) * BOTH, :], block, preferred_element_type=f32) for n in range(3)
        ]
        side = jnp.where(east, pltpu.roll(part[2], OV, 1), pltpu.roll(part[1], LANES - OV, 1))
        totals.append(part[0] + side)
    images = pass_on([slab[GRAD_ROWS : GRAD_ROWS + 8] for slab in slabs], own_ref[0] % 2)
    for t in range(PEERS):
        rows = [total[t * 16 : t * 16 + 16] for total in totals]
        rows.append(images[t * 8 : t * 8 + 8])
        out_ref[t] = jnp.concatenate(rows, axis=0).astype(bf16)


def blend_classes(images, mats_ref, before_ref, after_ref):
    source = images * before_ref[0:1, :]
    high = source.astype(bf16)
    low = (source - high.astype(f32)).astype(bf16)
    lane = iota((SLOTS, LANES), 1)
    south = (lane // 8) % 2 == 1
    columns = []
    for d in range(3):
        part = []
        for step in range(3):
            mat = mats_ref[(3 * d + step) * SLOTS : (3 * d + step + 1) * SLOTS, :]
            part.append(
                jnp.dot(mat, high, preferred_element_type=f32) + jnp.dot(mat, low, preferred_element_type=f32)
            )
        across = jnp.where(south, part[1], part[2])
        columns.append(part[0] + jnp.where(south, pltpu.roll(across, 8, 1), pltpu.roll(across, LANES - 8, 1)))
    total = columns[0] + pltpu.roll(jnp.where(lane >= 64, columns[1], columns[2]), 64, 1)
    return total * after_ref[...]


def stack_weights(weight_ref, held):
    held[...] = jnp.zeros_like(held)
    for t in range(TIN):
        for tap in range(TAPS):
            held[t, tap * 8 : tap * 8 + RGB, :] = weight_ref[t, tap].astype(f32)


def conv_kernel(
    chunk,
    feat_ref,
    weight_hbm,
    bias_hbm,
    grad_hbm,
    ids_hbm,
    profile_hbm,
    own_ref,
    out_ref,
    route_ref,
    mats_ref,
    before_ref,
    after_ref,
    ratio_ref,
    feats,
    stacked_ref,
    weight_ref,
    bias_ref,
    grad_ref,
    ids_ref,
    profile_ref,
    held,
    taps,
    turned,
    small_sems,
    sems,
):
    small = [(ids_hbm, ids_ref), (profile_hbm, profile_ref), (weight_hbm, weight_ref), (grad_hbm, grad_ref), (bias_hbm, bias_ref)]
    moves = [pltpu.make_async_copy(src, dst, small_sems.at[n]) for n, (src, dst) in enumerate(small)]
    for move in moves:
        move.start()
    copies = []
    for n in range(PIX // chunk):
        part = pl.ds(n * chunk, chunk)
        copies.append(pltpu.make_async_copy(feat_ref.at[:, :, part], feats.at[:, :, part], sems.at[n]))
        copies[-1].start()
    for move in moves:
        move.wait()
    stack_weights(weight_ref, held)
    kernels = [held[t].astype(bf16) for t in range(TIN)]
    for t in range(TIN):
        stacked_ref[t] = kernels[t]
    ids = ids_ref[...].astype(f32)
    own = own_ref[0]
    y, z, c = own // 16, (own // 2) % 8, own % 2
    route_prep(ids, y, z, route_ref)
    class_prep(ids, profile_ref, y, z, c, mats_ref, before_ref, after_ref)
    ratio_prep(ids, profile_ref, own, ratio_ref)
    taps[0:8, :] = jnp.zeros((8, PIX), f32)
    taps[0:RGB, :] = grad_ref[...].astype(f32)
    halves = []
    for r in range(ROWS):
        turned[r] = taps[0:8, r * LANES : (r + 1) * LANES]
    for h in range(2):
        halves.append(jnp.concatenate(half_rows(turned, h, RGB), axis=0))
    for n in range(PIX // chunk):
        copies[n].wait()
        total = jnp.zeros((STACK, chunk), f32)
        for t in range(TIN):
            total += jnp.dot(kernels[t], feats[t, :, n * chunk : (n + 1) * chunk], preferred_element_type=f32)
        taps[:, n * chunk : (n + 1) * chunk] = total
    lane = iota((8, PIX), 1)
    image = jnp.zeros((8, PIX), f32)
    for kx in range(3):
        column = jnp.zeros((8, PIX), f32)
        for ky in range(3):
            tap = 3 * ky + kx
            moved = shift_lanes(taps[tap * 8 : tap * 8 + 8, :], (ky - 1) * EDGE)
            if ky == 0:
                moved = jnp.where(lane >= EDGE, moved, 0.0)
            elif ky == 2:
                moved = jnp.where(lane < PIX - EDGE, moved, 0.0)
            column = column + moved
        moved = shift_lanes(column, kx - 1)
        if kx == 0:
            moved = jnp.where(lane % EDGE != 0, moved, 0.0)
        elif kx == 2:
            moved = jnp.where(lane % EDGE != EDGE - 1, moved, 0.0)
        image = image + moved
    row = iota((8, 1), 0)
    shift = jnp.zeros((8, 1), f32)
    for o in range(RGB):
        shift = jnp.where(row == o, bias_ref[o], shift)
    image = image + shift
    for r in range(ROWS):
        turned[r] = image[:, r * LANES : (r + 1) * LANES]
    place = iota((LANES, LANES), 0)
    k = (((place // 16) % 4) * 2 + (place // 4) % 2) * 8 + 4 * (((place // 8) % 2) ^ c) + place % 4
    lanes = onehot(iota((LANES, LANES), 1) == (k // 32) * 64 + (place // 64) * 32 + k % 32)
    classes = []
    for h in range(2):
        block = half_rows(turned, h, RGB) + [jnp.zeros((16, LANES), f32)]
        block = jnp.concatenate(block, axis=0).astype(bf16)
        both = lax.dot_general(lanes, block, (((1,), (1,)), ((), ())), preferred_element_type=f32)
        classes.append(jnp.concatenate([both[0:64], both[64:128]], axis=1))
    classes = jnp.concatenate(classes, axis=0)
    for p in range(PEERS):
        out_ref[p] = jnp.concatenate([halves[p % 2], classes[p * 8 : p * 8 + 8]], axis=0).astype(bf16)


def half_rows(turned, h, colours):
    return [turned[qy * 16 + h * 8 : qy * 16 + h * 8 + 8, o, :] for o in range(colours) for qy in range(2)]


def grad_stack(grad, taps):
    lane = iota((8, PIX), 1)
    for kx in range(3):
        moved_x = shift_lanes(grad, 1 - kx)
        if kx == 0:
            moved_x = jnp.where(lane % EDGE != EDGE - 1, moved_x, 0.0)
        elif kx == 2:
            moved_x = jnp.where(lane % EDGE != 0, moved_x, 0.0)
        for ky in range(3):
            moved = shift_lanes(moved_x, (1 - ky) * EDGE)
            if ky == 0:
                moved = jnp.where(lane < PIX - EDGE, moved, 0.0)
            elif ky == 2:
                moved = jnp.where(lane >= EDGE, moved, 0.0)
            tap = 3 * ky + kx
            taps[tap * 8 : tap * 8 + 8, :] = moved


def split_bias(part):
    at = iota((PART, LANES), 0) == BIAS_ROW
    lane = iota((PART, LANES), 1)
    total = part + pltpu.roll(part, LANES - RGB, 1)
    high = total.astype(bf16).astype(f32)
    low = pltpu.roll(total - high, RGB, 1)
    pair = jnp.where(lane < RGB, high, jnp.where(lane < 2 * RGB, low, part))
    return jnp.where(at, pair, part)


def weight_grad_kernel(
    chunk, got_ref, feat_ref, ratio_ref, mats_ref, before_ref, after_ref, out_ref, stack_ref, taps, turned
):
    sums = [got_ref[h].astype(f32) for h in range(2)]
    for n in range(2, PEERS):
        sums[n % 2] = sums[n % 2] + got_ref[n].astype(f32)
    turned[...] = jnp.zeros_like(turned)
    for h in range(2):
        for o in range(RGB):
            for qy in range(2):
                at = qy * 16 + h * 8
                piece = sums[h][o * 16 + qy * 8 : o * 16 + qy * 8 + 8] * ratio_ref[at : at + 8, :]
                turned[at : at + 8, o, :] = piece.astype(bf16).astype(f32)
    grad = jnp.concatenate([turned[r] for r in range(ROWS)], axis=1)
    images = [got_ref[n].astype(f32)[GRAD_ROWS : GRAD_ROWS + 8] for n in range(PEERS)]
    blended = blend_classes(jnp.concatenate(images, axis=0), mats_ref, before_ref, after_ref)
    grad_stack(grad, taps)
    bias = lax.dot_general(
        jnp.ones((8, PIX), bf16), grad.astype(bf16), (((1,), (1,)), ((), ())), preferred_element_type=f32
    )
    total = jnp.zeros((TIN * CH, STACK), f32)
    for at in range(0, PIX, chunk):
        part = taps[:, at : at + chunk].astype(bf16)
        stack_ref[:, at : at + chunk] = part
        total += lax.dot_general(
            feat_ref[:, :, at : at + chunk].reshape(TIN * CH, chunk),
            part,
            (((1,), (1,)), ((), ())),
            preferred_element_type=f32,
        )
    rows = jnp.concatenate([total[t * CH : (t + 1) * CH].T for t in range(TIN)], axis=0)
    rows = jnp.concatenate([rows, jnp.zeros((TIN * STACK, LANES - CH), f32)], axis=1).astype(bf16)
    every = PARTS * PART
    place = iota((2 * every, TIN * STACK), 0)
    source = iota((2 * every, TIN * STACK), 1)
    rank = jnp.where(source % 8 < RGB, (source // 8) * RGB + source % 8, -1)
    within = place % PART
    main = (rank == (place // PART) * MAIN + within) & (within < MAIN) & (place < every)
    offset = place - every - RGB * (rank - PARTS * MAIN)
    side = (offset >= 0) & (offset < RGB) & (place >= every) & (rank >= PARTS * MAIN)
    chosen = jnp.dot(onehot(main | side), rows, preferred_element_type=f32)
    bias_wide = jnp.concatenate([bias, jnp.zeros((8, LANES - 8), f32)], axis=1)[0:1]
    bias_wide = jnp.where(iota((1, LANES), 1) < RGB, bias_wide, 0.0)
    lane = iota((every, LANES), 1)
    third = iota((every, LANES), 0) % 3
    tail = jnp.zeros((every, LANES), f32)
    for c in range(3):
        tail = jnp.where(third == c, pltpu.roll(chosen[every:], CH - 32 * c, 1), tail)
    packed = jnp.where(lane < CH, chosen[:every], tail)
    packed = jnp.where((iota((every, LANES), 0) % PART == BIAS_ROW) & (lane < CH), bias_wide, packed)
    parts = [split_bias(packed[q * PART : (q + 1) * PART]) for q in range(PARTS)]
    for p in range(PEERS):
        out_ref[p] = jnp.concatenate([parts[p % PARTS], blended[p * 8 : p * 8 + 8]], axis=0).astype(bf16)


def feature_grad_kernel(stack_ref, weight_ref, out_ref):
    for t in range(TIN):
        out_ref[t] = lax.dot_general(
            weight_ref[t], stack_ref[...], (((0,), (0,)), ((), ())), preferred_element_type=f32
        ).astype(bf16)


def decode_kernel(got_ref, own_ref, image_ref, turned):
    images = jnp.concatenate([got_ref[n].astype(f32)[PART : PART + 8] for n in range(PEERS)], axis=0)
    block = jnp.concatenate([images[:, 0:64], images[:, 64:128]], axis=0).astype(bf16)
    row = iota((BOTH, LANES), 0)
    lane = iota((BOTH, LANES), 1)
    k = ((row % 8) * 2 + (((row // 8) % 2) ^ (own_ref[0] // 64))) * 8 + (row // 16) % 8
    spot = ((k // 32) % 2) * 64 + (row // SLOTS) * 32 + k % 32
    for h in range(2):
        lanes = onehot((lane == spot) & (k // 64 == h))
        tile = lax.dot_general(block, lanes, (((0,), (0,)), ((), ())), preferred_element_type=f32)
        for o in range(RGB):
            for qy in range(2):
                turned[qy * 16 + h * 8 : qy * 16 + h * 8 + 8, o, :] = tile[o * 16 + qy * 8 : o * 16 + qy * 8 + 8]
    for r in range(ROWS):
        image_ref[:, r * LANES : (r + 1) * LANES] = turned[r, 0:RGB, :].astype(bf16)


def sum_z_kernel(got_ref, own_ref, out_ref):
    slabs = [got_ref[p].astype(f32) for p in range(PEERS)]
    part = slabs[0][0:PART]
    for slab in slabs[1:]:
        part = part + slab[0:PART]
    part = split_bias(part)
    images = pass_on([slab[PART : PART + 8] for slab in slabs], own_ref[0] % 2)
    for t in range(PEERS):
        out_ref[t] = jnp.concatenate([part, images[t * 8 : t * 8 + 8]], axis=0).astype(bf16)


def sum_y_kernel(got_ref, out_ref):
    parts = []
    for c in range(2):
        part = got_ref[c].astype(f32)[0:PART]
        for y in range(1, 8):
            part = part + got_ref[2 * y + c].astype(f32)[0:PART]
        parts.append(split_bias(part))
    both = jnp.concatenate(parts, axis=0).astype(bf16)
    for n in range(out_ref.shape[0]):
        out_ref[n] = both


def finish_kernel(scale, got_ref, weight_ref, bias_ref, held, others):
    for z in range(2):
        total = got_ref[4 * z].astype(f32)
        for n in range(1, 4):
            total = total + got_ref[4 * z + n].astype(f32)
        held[2 * PART * z : 2 * PART * (z + 1), :] = total * scale
    bias = held[BIAS_ROW : BIAS_ROW + 1, :]
    bias_ref[...] = bias[:, 0:RGB] + bias[:, RGB : 2 * RGB]
    count = TIN * TAPS * RGB - PARTS * MAIN
    lane = iota((count, LANES), 1)
    tail = jnp.zeros((count, LANES), f32)
    for c in range(3):
        turned = pltpu.roll(held[pl.ds(c, count, stride=3), :], (32 + 32 * c) % LANES, 1)
        tail = jnp.where(lane // 32 == c, turned, tail)
    others[0:count, :] = tail
    for n in range(TIN * TAPS):
        at = n * RGB
        if at < PARTS * MAIN:
            at = (at // MAIN) * PART + at % MAIN
            value = held[at : at + RGB, 0:CH]
        else:
            at -= PARTS * MAIN
            value = others[at : at + RGB, 0:CH]
        weight_ref[n // TAPS, n % TAPS] = value


VM = pl.BlockSpec(memory_space=pltpu.VMEM)
SM = pl.BlockSpec(memory_space=pltpu.SMEM)
HBM = pl.BlockSpec(memory_space=pltpu.HBM)
LIMIT = 40 * 1024 * 1024


def call(body, out_shape, in_specs, scratch=(), flops=1 << 20, size=1 << 17, name=None, limit=LIMIT, **rest):
    return pl.pallas_call(
        body,
        out_shape=out_shape,
        in_specs=in_specs,
        scratch_shapes=list(scratch),
        compiler_params=pltpu.CompilerParams(vmem_limit_bytes=limit),
        cost_estimate=pl.CostEstimate(flops=flops, bytes_accessed=size, transcendentals=0),
        name=name,
        **rest,
    )


def exchange(rows, axes):
    return lax.all_to_all(rows, axes, 0, 0, tiled=True)


def message(peers, rows):
    return jax.ShapeDtypeStruct((peers, rows, LANES), bf16)


def per_device(features, conv_weight, bias, blend_profile, tile_ids, reward_grad):
    chunk = 1024
    conv_flops = 2 * STACK * TIN * CH * PIX
    own = lax.axis_index(("y", "z_hi", "z_lo", "c")).reshape(1).astype(jnp.int32)
    feats = jnp.transpose(features[0, 0], (1, 0, 2))
    args = (feats, conv_weight, bias, reward_grad[0, 0], tile_ids, blend_profile)
    here = [pltpu.with_memory_space_constraint(x, pltpu.HBM) for x in args]
    rows, route, mats, before, after, ratio, feats_held, weights_held = call(
        functools.partial(conv_kernel, 2 * chunk),
        (
            pltpu.VMEM((PEERS, GRAD_ROWS + 8, LANES), bf16),
            pltpu.VMEM((3 * BOTH, BOTH), bf16),
            pltpu.VMEM((9 * SLOTS, SLOTS), bf16),
            pltpu.VMEM((8, LANES), f32),
            pltpu.VMEM((SLOTS, LANES), f32),
            pltpu.VMEM((ROWS, LANES), f32),
            pltpu.VMEM((TIN, CH, PIX), bf16),
            pltpu.VMEM((TIN, STACK, CH), bf16),
        ),
        [HBM, HBM, HBM, HBM, HBM, HBM, SM],
        [
            pltpu.VMEM((TIN, TAPS, RGB, CH), bf16),
            pltpu.SMEM((RGB,), f32),
            pltpu.VMEM((RGB, PIX), bf16),
            pltpu.VMEM((1, SLOTS), jnp.int32),
            pltpu.SMEM((OV,), jnp.int32),
            pltpu.VMEM((TIN, STACK, CH), f32),
            pltpu.VMEM((STACK, PIX), f32),
            pltpu.VMEM((ROWS, 8, LANES), f32),
            pltpu.SemaphoreType.DMA((5,)),
            pltpu.SemaphoreType.DMA((PIX // (2 * chunk),)),
        ],
        conv_flops,
        1 << 22,
        "conv",
        out_specs=(VM,) * 8,
    )(*here, own)
    rows = exchange(rows, ("z_hi", "z_lo", "c"))
    rows = call(
        route_kernel, message(PEERS, GRAD_ROWS + 8), [VM, VM, SM], (), 1 << 27, 1 << 20, "route", out_specs=VM
    )(rows, route, own)
    rows = exchange(rows, ("y", "c"))
    rows, stack = call(
        functools.partial(weight_grad_kernel, chunk),
        (message(PEERS, PART + 8), jax.ShapeDtypeStruct((STACK, PIX), bf16)),
        [VM, VM, VM, VM, VM, VM],
        [pltpu.VMEM((STACK, PIX), f32), pltpu.VMEM((ROWS, 8, LANES), f32)],
        conv_flops,
        1 << 22,
        "weight_grad",
        out_specs=(VM, VM),
    )(rows, feats_held, ratio, mats, before, after)

    feature_rows = call(
        feature_grad_kernel,
        jax.ShapeDtypeStruct((TIN, CH, PIX), bf16),
        [
            pl.BlockSpec((STACK, chunk), lambda i: (0, i)),
            pl.BlockSpec((TIN, STACK, CH), lambda i: (0, 0, 0)),
        ],
        (),
        conv_flops,
        1 << 22,
        "feature_grad",
        grid=(PIX // chunk,),
        out_specs=pl.BlockSpec((TIN, CH, chunk), lambda i: (0, 0, i)),
    )(stack, weights_held)
    feature_grad = jnp.transpose(feature_rows, (1, 0, 2))[None, None]

    rows = exchange(rows, ("z_hi", "z_lo", "c"))
    rows = call(sum_z_kernel, message(PEERS, PART + 8), [VM, SM], name="sum_z", out_specs=VM)(rows, own)
    rows = exchange(rows, ("y", "c"))
    decoded = call(
        decode_kernel,
        jax.ShapeDtypeStruct((RGB, PIX), bf16),
        [VM, SM],
        [pltpu.VMEM((ROWS, 8, LANES), f32)],
        name="decode",
        out_specs=VM,
    )(rows, own)
    rows = call(sum_y_kernel, message(8, 2 * PART), [VM], name="sum_y", out_specs=VM)(rows)
    rows = exchange(rows, ("z_lo", "clip"))
    rows, decoded, feature_grad = lax.optimization_barrier((rows, decoded, feature_grad))
    scale = 1.0 / math.sqrt(4 * SLOTS * PIX)
    weight_grad, bias_grad = call(
        functools.partial(finish_kernel, scale),
        (
            jax.ShapeDtypeStruct((TIN, TAPS, RGB, CH), f32),
            jax.ShapeDtypeStruct((1, RGB), f32),
        ),
        [VM],
        [pltpu.VMEM((PARTS * PART, LANES), f32), pltpu.VMEM((24, LANES), f32)],
        name="finish",
        out_specs=(VM, VM),
    )(rows)
    return (decoded[None, None], feature_grad, weight_grad, bias_grad.reshape(RGB))


def solution(mesh):
    parts = Mesh(mesh.devices.reshape(8, 4, 2, 2, 4), ("y", "z_hi", "z_lo", "c", "clip"))
    tile = ("y", "z_hi", "z_lo", "c")
    return jax.shard_map(
        per_device,
        mesh=parts,
        in_specs=(
            P("clip", tile, None, None, None),
            P(),
            P(),
            P(),
            P("clip", None),
            P("clip", tile, None, None),
        ),
        out_specs=(P("clip", tile, None, None), P("clip", tile, None, None, None), P(), P()),
        check_vma=False,
    )
```

```python
import functools
import math

import jax
import jax.numpy as jnp
from jax import lax
from jax.experimental import pallas as pl
from jax.experimental.pallas import tpu as pltpu
from jax.sharding import Mesh
from jax.sharding import PartitionSpec as P

EDGE = 64
OV = 32
PIX = EDGE * EDGE
SLOTS = 128
TX = 16
TY = SLOTS // TX
CH = 96
RGB = 3
TIN = 3
LANES = 128
ROWS = PIX // LANES
BOTH = 2 * SLOTS
TAPS = 9
STACK = TAPS * 8
PARTS = 4
PART = 16
MAIN = 15
BIAS_ROW = 15

BOTH = 2 * SLOTS
TAPS = 9
STACK = TAPS * 8
PEERS = 16
WIDE = 32
SLAB = 16
GRADS = 12
FLAT = WIDE * SLAB
PARTS = 4
PART = 16
MAIN = 15
BIAS_ROW = 15

BOTH = 2 * SLOTS
TAPS = 9
STACK = TAPS * 8
PEERS = 16
WIDE = 32
SLAB = 16
GRADS = 12
FLAT = WIDE * SLAB
PARTS = 4
PART = 16
MAIN = 15
BIAS_ROW = 15

f32 = jnp.float32
bf16 = jnp.bfloat16


def iota(shape, dim):
    return lax.broadcasted_iota(jnp.int32, shape, dim)


def onehot(mask):
    return jnp.where(mask, 1.0, 0.0).astype(bf16)


def pick_rows(mask, rows):
    return jnp.dot(onehot(mask), rows.astype(bf16), preferred_element_type=f32)


def shift_lanes(value, amount):
    size = value.shape[1]
    amount = amount % size
    return value if amount == 0 else pltpu.roll(value, size - amount, 1)


def profile_at(index, profile_ref):
    out = jnp.zeros(index.shape, f32)
    for m in range(OV):
        out = jnp.where(index == m, profile_ref[m].astype(f32), out)
    return out


def no_further(room):
    return jnp.minimum(room, 1.0)


def ids_at(ids, slots):
    spread = onehot(iota(slots.shape, 1) == slots)
    wide = jnp.broadcast_to(ids, (8, SLOTS)).astype(bf16)
    return lax.dot_general(spread, wide, (((1,), (1,)), ((), ())), preferred_element_type=f32)[:, 0:1]


def route_prep(ids, y, z, c, mats_ref, gather_ref):
    y_lo, y_hi, z_lo, z_hi = y % 2, y // 2, z % 2, z // 2
    place = iota((FLAT, SLOTS), 0) // SLAB
    target = ids_at(ids, (place // 4) * 16 + z_hi * 4 + place % 4)
    from_slot = y_hi * WIDE + iota((SLOTS, FLAT), 1) // SLAB
    source = jnp.dot(
        jnp.broadcast_to(ids, (8, SLOTS)).astype(bf16),
        onehot(iota((SLOTS, FLAT), 0) == from_slot),
        preferred_element_type=f32,
    )[0:1]
    row = iota((FLAT, 1), 0)
    col = iota((1, FLAT), 1)
    part = lambda at: (TX * ((at // 2) % 2) + 1024 * (2 * ((at % SLAB) // 4) + at % 2)).astype(f32)
    image = lambda at: 100000.0 + at.astype(f32)
    peer = row // SLAB
    sender = (y_lo ^ ((peer // 4) % 2)) * 16 + (row % 4) * 4 + (z_lo ^ ((peer // 2) % 2)) * 2 + (c ^ (peer % 2))
    is_grad = row % SLAB < GRADS
    want = jnp.where(is_grad, target + part(row), image(sender * SLAB + GRADS + peer // 8))
    have = jnp.where(col % SLAB < GRADS, source + part(col), image(col))
    across = target - jnp.floor(target * (1.0 / TX)) * TX
    blocked = jnp.where(is_grad, 0.0, 99.0)
    right = jnp.where(across + blocked < TX - 1.5, want + 1.0, -9999.0)
    left = jnp.where(across - blocked > 0.5, want - 1.0, -9999.0)
    for n, key in enumerate((want, left, right)):
        mats_ref[n * FLAT : (n + 1) * FLAT, :] = onehot(have == key)
    row = iota((BOTH, 1), 0)
    r, o = row // 8, row % 8
    key = jnp.where(o < RGB, ((r // 2) % 8) * SLAB + o * 4 + (r // 16) * 2 + r % 2, -1)
    gather_ref[0:BOTH, :] = onehot(col % SLOTS == key)
    row = iota((SLOTS, 1), 0)
    gather_ref[BOTH : BOTH + SLOTS, :] = onehot(col == (row // 4) * SLAB + GRADS + row % 4)


def class_prep(ids, profile_ref, y, z, c, mats_ref, before_ref, after_ref):
    k = (2 * z + c) * 8 + y
    place = iota((SLOTS, SLOTS), 0)
    leaves = (4 * (((place // 8) % 2) ^ c) + place % 4) * 16 + (place // 16) * 2 + (place // 4) % 2
    spread = iota((SLOTS, SLOTS), 1) == leaves
    place = iota((SLOTS, SLOTS), 1)
    comes = ((place // 16) ^ (y % 2)) * 16 + (place % 4) * 4 + (((place // 8) % 2) ^ (z % 2)) * 2 + (((place // 4) % 2) ^ c)
    come = jnp.dot(
        jnp.broadcast_to(ids, (8, SLOTS)).astype(bf16),
        onehot(iota((SLOTS, SLOTS), 0) == comes),
        preferred_element_type=f32,
    )[0:1]
    own = jnp.sum(jnp.where(spread, jnp.broadcast_to(ids, (SLOTS, SLOTS)), 0.0), axis=1, keepdims=True)
    row = jnp.floor(own * (1.0 / TX))
    col = own - row * TX
    right = jnp.where(col < TX - 1.5, own + 1.0, -9999.0)
    left = jnp.where(col > 0.5, own - 1.0, -9999.0)
    n = 0
    for key in (own, left, right):
        gap = come - key
        for step in (0.0, -float(TX), float(TX)):
            mats_ref[n * SLOTS : (n + 1) * SLOTS, :] = onehot(gap == step)
            n += 1
    h, par, rx = k // 64, (k // 32) % 2, k % 32
    lane = iota((1, LANES), 1)
    east = lane >= 64
    south = (lane // 8) % 2 == 1
    ry = 2 * (8 * h + lane % 8) + par
    fy = profile_at(jnp.where(south, OV - 1 - ry, ry), profile_ref)
    fy_other = profile_at(jnp.where(south, ry, OV - 1 - ry), profile_ref)
    near = profile_ref[rx].astype(f32)
    far = profile_ref[OV - 1 - rx].astype(f32)
    fx = jnp.where(east, far, near)
    fx_other = jnp.where(east, near, far)
    col_there = no_further(jnp.where(east, TX - 1.0 - col, col))
    row_there = no_further(jnp.where(south, TY - 1.0 - row, row))
    before_ref[...] = jnp.broadcast_to(fx * fy, (8, LANES))
    after_ref[...] = 1.0 / ((fx + col_there * fx_other) * (fy + row_there * fy_other))


def ratio_prep(ids, profile_ref, own_slot, ratio_ref):
    own = jnp.sum(jnp.where(iota((1, SLOTS), 1) == own_slot, ids, 0.0), axis=1, keepdims=True)
    row = jnp.floor(own * (1.0 / TX))
    col = own - row * TX
    lane = iota((1, LANES), 1)
    x = lane % EDGE
    y = 2 * iota((ROWS, LANES), 0) + iota((ROWS, LANES), 1) // EDGE
    at_x = jnp.minimum(x, EDGE - 1 - x)
    at_y = jnp.minimum(y, EDGE - 1 - y)
    fx = profile_at(at_x, profile_ref)
    fx_other = profile_at(OV - 1 - at_x, profile_ref)
    fy = profile_at(at_y, profile_ref)
    fy_other = profile_at(OV - 1 - at_y, profile_ref)
    col_there = no_further(jnp.where(x >= OV, TX - 1.0 - col, col))
    row_there = no_further(jnp.where(y >= OV, TY - 1.0 - row, row))
    ratio_ref[...] = fx * fy / ((fx + col_there * fx_other) * (fy + row_there * fy_other))


def pass_on(slabs, core):
    block = jnp.concatenate(slabs, axis=0)
    place = iota((SLOTS, SLOTS), 0)
    y = place // 16
    peer = (place % 8) * 2 + (core ^ (y // 4))
    return pick_rows(iota((SLOTS, SLOTS), 1) == peer * 8 + ((place // 8) % 2) * 4 + y % 4, block)


def route_kernel(got_ref, mats_ref, out_ref):
    block = got_ref[...].reshape(FLAT, LANES)
    every = jnp.dot(mats_ref[...], block, preferred_element_type=f32)
    here, left, right = (every[n * FLAT : (n + 1) * FLAT] for n in range(3))
    east = iota((FLAT, LANES), 1) % EDGE >= OV
    total = here + jnp.where(east, pltpu.roll(right, OV, 1), pltpu.roll(left, LANES - OV, 1))
    out_ref[...] = total.astype(bf16).reshape(WIDE, SLAB, LANES)


def blend_classes(images, mats_ref, before_ref, after_ref):
    source = images * before_ref[0:1, :]
    high = source.astype(bf16)
    low = (source - high.astype(f32)).astype(bf16)
    lane = iota((SLOTS, LANES), 1)
    south = (lane // 8) % 2 == 1
    every = jnp.dot(mats_ref[...], jnp.concatenate([high, low], axis=1), preferred_element_type=f32)
    every = every[:, :LANES] + every[:, LANES:]
    columns = []
    for d in range(3):
        part = [every[(3 * d + step) * SLOTS : (3 * d + step + 1) * SLOTS] for step in range(3)]
        across = jnp.where(south, part[1], part[2])
        columns.append(part[0] + jnp.where(south, pltpu.roll(across, 8, 1), pltpu.roll(across, LANES - 8, 1)))
    total = columns[0] + pltpu.roll(jnp.where(lane >= 64, columns[1], columns[2]), 64, 1)
    return total * after_ref[...]


def stack_weights(weight_ref, held):
    held[...] = jnp.zeros_like(held)
    for t in range(TIN):
        for tap in range(TAPS):
            held[t, tap * 8 : tap * 8 + RGB, :] = weight_ref[t, tap].astype(f32)


def conv_kernel(
    chunk,
    feat_ref,
    weight_hbm,
    bias_hbm,
    grad_hbm,
    ids_hbm,
    profile_hbm,
    own_ref,
    out_ref,
    route_ref,
    gather_ref,
    mats_ref,
    before_ref,
    after_ref,
    ratio_ref,
    feats,
    stacked_ref,
    weight_ref,
    bias_ref,
    grad_ref,
    ids_ref,
    profile_ref,
    held,
    taps,
    turned,
    small_sems,
    sems,
):
    small = [(ids_hbm, ids_ref), (profile_hbm, profile_ref), (weight_hbm, weight_ref), (grad_hbm, grad_ref), (bias_hbm, bias_ref)]
    moves = [pltpu.make_async_copy(src, dst, small_sems.at[n]) for n, (src, dst) in enumerate(small)]
    for move in moves:
        move.start()
    copies = []
    for n in range(PIX // chunk):
        part = pl.ds(n * chunk, chunk)
        copies.append(pltpu.make_async_copy(feat_ref.at[:, :, part], feats.at[:, :, part], sems.at[n]))
        copies[-1].start()
    for move in moves:
        move.wait()
    stack_weights(weight_ref, held)
    kernels = [held[t].astype(bf16) for t in range(TIN)]
    for t in range(TIN):
        stacked_ref[t] = kernels[t]
    ids = ids_ref[...].astype(f32)
    own = own_ref[0]
    y, z, c = own // 16, (own // 2) % 8, own % 2
    route_prep(ids, y, z, c, route_ref, gather_ref)
    class_prep(ids, profile_ref, y, z, c, mats_ref, before_ref, after_ref)
    ratio_prep(ids, profile_ref, own, ratio_ref)
    taps[0:8, :] = jnp.zeros((8, PIX), f32)
    taps[0:RGB, :] = grad_ref[...].astype(f32)
    grads = jnp.concatenate([taps[0:8, r * LANES : (r + 1) * LANES] for r in range(ROWS)], axis=0)
    row = iota((SLOTS, BOTH), 0)
    part = row % SLAB
    at = ((part // 2) % 2) * 128 + (row // SLAB) * 16 + (part % 2) * 8 + part // 4
    eighths = pick_rows((iota((SLOTS, BOTH), 1) == at) & (part < GRADS), grads)
    for n in range(PIX // chunk):
        copies[n].wait()
        total = jnp.zeros((STACK, chunk), f32)
        for t in range(TIN):
            total += jnp.dot(kernels[t], feats[t, :, n * chunk : (n + 1) * chunk], preferred_element_type=f32)
        taps[:, n * chunk : (n + 1) * chunk] = total
    lane = iota((8, PIX), 1)
    image = jnp.zeros((8, PIX), f32)
    for kx in range(3):
        column = jnp.zeros((8, PIX), f32)
        for ky in range(3):
            tap = 3 * ky + kx
            moved = shift_lanes(taps[tap * 8 : tap * 8 + 8, :], (ky - 1) * EDGE)
            if ky == 0:
                moved = jnp.where(lane >= EDGE, moved, 0.0)
            elif ky == 2:
                moved = jnp.where(lane < PIX - EDGE, moved, 0.0)
            column = column + moved
        moved = shift_lanes(column, kx - 1)
        if kx == 0:
            moved = jnp.where(lane % EDGE != 0, moved, 0.0)
        elif kx == 2:
            moved = jnp.where(lane % EDGE != EDGE - 1, moved, 0.0)
        image = image + moved
    row = iota((8, 1), 0)
    shift = jnp.zeros((8, 1), f32)
    for o in range(RGB):
        shift = jnp.where(row == o, bias_ref[o], shift)
    image = image + shift
    for r in range(ROWS):
        turned[r] = image[:, r * LANES : (r + 1) * LANES]
    place = iota((LANES, LANES), 0)
    lanes = onehot(iota((LANES, LANES), 1) == ((place // 32) % 2) * 64 + (place // 64) * 32 + place % 32)
    classes = []
    for h in range(2):
        block = half_rows(turned, h, RGB) + [jnp.zeros((16, LANES), f32)]
        block = jnp.concatenate(block, axis=0).astype(bf16)
        both = lax.dot_general(lanes, block, (((1,), (1,)), ((), ())), preferred_element_type=f32)
        classes.append(jnp.concatenate([both[0:64], both[64:128]], axis=1))
    row = iota((FLAT, SLOTS), 0)
    peer = row // SLAB
    z_to = (peer // 4) % 4 * 2 + (((peer // 2) % 2) ^ (z % 2))
    k = (2 * z_to + ((peer % 2) ^ c)) * 8 + (row % 4) * 2 + ((peer // 16) ^ (y % 2))
    images = pick_rows((iota((FLAT, SLOTS), 1) == k) & (row % SLAB >= GRADS), jnp.concatenate(classes, axis=0))
    for p in range(WIDE):
        e = (p // 16) * 4 + p % 4
        slab = images[p * SLAB : (p + 1) * SLAB] + eighths[e * SLAB : (e + 1) * SLAB]
        out_ref[p] = slab.astype(bf16)


def half_rows(turned, h, colours):
    return [turned[qy * 16 + h * 8 : qy * 16 + h * 8 + 8, o, :] for o in range(colours) for qy in range(2)]


def grad_stack(grad, taps):
    lane = iota((8, PIX), 1)
    for kx in range(3):
        moved_x = shift_lanes(grad, 1 - kx)
        if kx == 0:
            moved_x = jnp.where(lane % EDGE != EDGE - 1, moved_x, 0.0)
        elif kx == 2:
            moved_x = jnp.where(lane % EDGE != 0, moved_x, 0.0)
        for ky in range(3):
            moved = shift_lanes(moved_x, (1 - ky) * EDGE)
            if ky == 0:
                moved = jnp.where(lane < PIX - EDGE, moved, 0.0)
            elif ky == 2:
                moved = jnp.where(lane >= EDGE, moved, 0.0)
            tap = 3 * ky + kx
            taps[tap * 8 : tap * 8 + 8, :] = moved


def split_bias(part):
    at = iota((PART, LANES), 0) == BIAS_ROW
    lane = iota((PART, LANES), 1)
    total = part + pltpu.roll(part, LANES - RGB, 1)
    high = total.astype(bf16).astype(f32)
    low = pltpu.roll(total - high, RGB, 1)
    pair = jnp.where(lane < RGB, high, jnp.where(lane < 2 * RGB, low, part))
    return jnp.where(at, pair, part)


def weight_grad_kernel(
    chunk, got_ref, feat_ref, ratio_ref, gather_ref, mats_ref, before_ref, after_ref, out_ref, stack_ref, taps
):
    every = jnp.dot(gather_ref[...], got_ref[...].reshape(FLAT, LANES), preferred_element_type=f32)
    pieces = []
    for r in range(ROWS):
        piece = every[r * 8 : r * 8 + 8] * ratio_ref[r : r + 1, :]
        pieces.append(piece.astype(bf16).astype(f32))
    grad = jnp.concatenate(pieces, axis=1)
    blended = blend_classes(every[BOTH : BOTH + SLOTS], mats_ref, before_ref, after_ref)
    grad_stack(grad, taps)
    summed = pieces[0]
    for piece in pieces[1:]:
        summed = summed + piece
    diagonal = iota((8, LANES), 0) == iota((8, LANES), 1)
    bias = jnp.sum(
        jnp.where(diagonal, jnp.sum(summed, axis=1, keepdims=True), 0.0), axis=0, keepdims=True
    )
    total = jnp.zeros((TIN * CH, STACK), f32)
    for at in range(0, PIX, chunk):
        part = taps[:, at : at + chunk].astype(bf16)
        stack_ref[:, at : at + chunk] = part
        total += lax.dot_general(
            feat_ref[:, :, at : at + chunk].reshape(TIN * CH, chunk),
            part,
            (((1,), (1,)), ((), ())),
            preferred_element_type=f32,
        )
    rows = jnp.concatenate([total[t * CH : (t + 1) * CH].T for t in range(TIN)], axis=0)
    rows = jnp.concatenate([rows, jnp.zeros((TIN * STACK, LANES - CH), f32)], axis=1).astype(bf16)
    every = PARTS * PART
    place = iota((2 * every, TIN * STACK), 0)
    source = iota((2 * every, TIN * STACK), 1)
    rank = jnp.where(source % 8 < RGB, (source // 8) * RGB + source % 8, -1)
    within = place % PART
    main = (rank == (place // PART) * MAIN + within) & (within < MAIN) & (place < every)
    offset = place - every - RGB * (rank - PARTS * MAIN)
    side = (offset >= 0) & (offset < RGB) & (place >= every) & (rank >= PARTS * MAIN)
    chosen = jnp.dot(onehot(main | side), rows, preferred_element_type=f32)
    lane = iota((every, LANES), 1)
    third = iota((every, LANES), 0) % 3
    tail = jnp.zeros((every, LANES), f32)
    for c in range(3):
        tail = jnp.where(third == c, pltpu.roll(chosen[every:], CH - 32 * c, 1), tail)
    packed = jnp.where(lane < CH, chosen[:every], tail)
    packed = jnp.where((iota((every, LANES), 0) % PART == BIAS_ROW) & (lane < CH), bias, packed)
    parts = [split_bias(packed[q * PART : (q + 1) * PART]) for q in range(PARTS)]
    for p in range(PEERS):
        out_ref[p] = jnp.concatenate([parts[p % PARTS], blended[p * 8 : p * 8 + 8]], axis=0).astype(bf16)


def feature_grad_kernel(stack_ref, weight_ref, out_ref):
    for t in range(TIN):
        out_ref[t] = lax.dot_general(
            weight_ref[t], stack_ref[...], (((0,), (0,)), ((), ())), preferred_element_type=f32
        ).astype(bf16)


def decode_kernel(got_ref, own_ref, image_ref, turned):
    images = jnp.concatenate([got_ref[n].astype(f32)[PART : PART + 8] for n in range(PEERS)], axis=0)
    block = jnp.concatenate([images[:, 0:64], images[:, 64:128]], axis=0).astype(bf16)
    row = iota((BOTH, LANES), 0)
    lane = iota((BOTH, LANES), 1)
    k = ((row % 8) * 2 + (((row // 8) % 2) ^ (own_ref[0] // 64))) * 8 + (row // 16) % 8
    spot = ((k // 32) % 2) * 64 + (row // SLOTS) * 32 + k % 32
    for h in range(2):
        lanes = onehot((lane == spot) & (k // 64 == h))
        tile = lax.dot_general(block, lanes, (((0,), (0,)), ((), ())), preferred_element_type=f32)
        for o in range(RGB):
            for qy in range(2):
                turned[qy * 16 + h * 8 : qy * 16 + h * 8 + 8, o, :] = tile[o * 16 + qy * 8 : o * 16 + qy * 8 + 8]
    for r in range(ROWS):
        image_ref[:, r * LANES : (r + 1) * LANES] = turned[r, 0:RGB, :].astype(bf16)


def sum_z_kernel(got_ref, own_ref, out_ref):
    slabs = [got_ref[p].astype(f32) for p in range(PEERS)]
    part = slabs[0][0:PART]
    for slab in slabs[1:]:
        part = part + slab[0:PART]
    part = split_bias(part)
    images = pass_on([slab[PART : PART + 8] for slab in slabs], own_ref[0] % 2)
    for t in range(PEERS):
        out_ref[t] = jnp.concatenate([part, images[t * 8 : t * 8 + 8]], axis=0).astype(bf16)


def sum_y_kernel(got_ref, out_ref):
    parts = []
    for c in range(2):
        part = got_ref[c].astype(f32)[0:PART]
        for y in range(1, 8):
            part = part + got_ref[2 * y + c].astype(f32)[0:PART]
        parts.append(split_bias(part))
    both = jnp.concatenate(parts, axis=0).astype(bf16)
    for n in range(out_ref.shape[0]):
        out_ref[n] = both


def finish_kernel(scale, got_ref, weight_ref, bias_ref, held, others):
    for z in range(2):
        total = got_ref[4 * z].astype(f32)
        for n in range(1, 4):
            total = total + got_ref[4 * z + n].astype(f32)
        held[2 * PART * z : 2 * PART * (z + 1), :] = total * scale
    bias = held[BIAS_ROW : BIAS_ROW + 1, :]
    bias_ref[...] = bias[:, 0:RGB] + bias[:, RGB : 2 * RGB]
    count = TIN * TAPS * RGB - PARTS * MAIN
    lane = iota((count, LANES), 1)
    tail = jnp.zeros((count, LANES), f32)
    for c in range(3):
        turned = pltpu.roll(held[pl.ds(c, count, stride=3), :], (32 + 32 * c) % LANES, 1)
        tail = jnp.where(lane // 32 == c, turned, tail)
    others[0:count, :] = tail
    for n in range(TIN * TAPS):
        at = n * RGB
        if at < PARTS * MAIN:
            at = (at // MAIN) * PART + at % MAIN
            value = held[at : at + RGB, 0:CH]
        else:
            at -= PARTS * MAIN
            value = others[at : at + RGB, 0:CH]
        weight_ref[n // TAPS, n % TAPS] = value


VM = pl.BlockSpec(memory_space=pltpu.VMEM)
SM = pl.BlockSpec(memory_space=pltpu.SMEM)
HBM = pl.BlockSpec(memory_space=pltpu.HBM)
LIMIT = 40 * 1024 * 1024


def call(body, out_shape, in_specs, scratch=(), flops=1 << 20, size=1 << 17, name=None, limit=LIMIT, **rest):
    return pl.pallas_call(
        body,
        out_shape=out_shape,
        in_specs=in_specs,
        scratch_shapes=list(scratch),
        compiler_params=pltpu.CompilerParams(vmem_limit_bytes=limit),
        cost_estimate=pl.CostEstimate(flops=flops, bytes_accessed=size, transcendentals=0),
        name=name,
        **rest,
    )


def exchange(rows, axes):
    return lax.all_to_all(rows, axes, 0, 0, tiled=True)


def message(peers, rows):
    return jax.ShapeDtypeStruct((peers, rows, LANES), bf16)


def per_device(features, conv_weight, bias, blend_profile, tile_ids, reward_grad):
    chunk = 1024
    conv_flops = 2 * STACK * TIN * CH * PIX
    own = lax.axis_index(("y_hi", "y_lo", "z_hi", "z_lo", "c")).reshape(1).astype(jnp.int32)
    feats = jnp.transpose(features[0, 0], (1, 0, 2))
    args = (feats, conv_weight, bias, reward_grad[0, 0], tile_ids, blend_profile)
    here = [pltpu.with_memory_space_constraint(x, pltpu.HBM) for x in args]
    rows, route, gather, mats, before, after, ratio, feats_held, weights_held = call(
        functools.partial(conv_kernel, 2 * chunk),
        (
            pltpu.VMEM((WIDE, SLAB, LANES), bf16),
            pltpu.VMEM((3 * FLAT, FLAT), bf16),
            pltpu.VMEM((BOTH + SLOTS, FLAT), bf16),
            pltpu.VMEM((9 * SLOTS, SLOTS), bf16),
            pltpu.VMEM((8, LANES), f32),
            pltpu.VMEM((SLOTS, LANES), f32),
            pltpu.VMEM((ROWS, LANES), f32),
            pltpu.VMEM((TIN, CH, PIX), bf16),
            pltpu.VMEM((TIN, STACK, CH), bf16),
        ),
        [HBM, HBM, HBM, HBM, HBM, HBM, SM],
        [
            pltpu.VMEM((TIN, TAPS, RGB, CH), bf16),
            pltpu.SMEM((RGB,), f32),
            pltpu.VMEM((RGB, PIX), bf16),
            pltpu.VMEM((1, SLOTS), jnp.int32),
            pltpu.SMEM((OV,), jnp.int32),
            pltpu.VMEM((TIN, STACK, CH), f32),
            pltpu.VMEM((STACK, PIX), f32),
            pltpu.VMEM((ROWS, 8, LANES), f32),
            pltpu.SemaphoreType.DMA((5,)),
            pltpu.SemaphoreType.DMA((PIX // (2 * chunk),)),
        ],
        conv_flops,
        1 << 22,
        "conv",
        out_specs=(VM,) * 9,
    )(*here, own)
    rows = exchange(rows, ("y_lo", "z_hi", "z_lo", "c"))
    rows = call(
        route_kernel, message(WIDE, SLAB), [VM, VM], (), 1 << 28, 1 << 21, "route", out_specs=VM
    )(rows, route)
    rows = exchange(rows, ("y_hi", "y_lo", "z_lo", "c"))
    rows, stack = call(
        functools.partial(weight_grad_kernel, chunk),
        (message(PEERS, PART + 8), jax.ShapeDtypeStruct((STACK, PIX), bf16)),
        [VM] * 7,
        [pltpu.VMEM((STACK, PIX), f32)],
        conv_flops,
        1 << 22,
        "weight_grad",
        out_specs=(VM, VM),
    )(rows, feats_held, ratio, gather, mats, before, after)

    feature_rows = call(
        feature_grad_kernel,
        jax.ShapeDtypeStruct((TIN, CH, PIX), bf16),
        [
            pl.BlockSpec((STACK, chunk), lambda i: (0, i)),
            pl.BlockSpec((TIN, STACK, CH), lambda i: (0, 0, 0)),
        ],
        (),
        conv_flops,
        1 << 22,
        "feature_grad",
        grid=(PIX // chunk,),
        out_specs=pl.BlockSpec((TIN, CH, chunk), lambda i: (0, 0, i)),
    )(stack, weights_held)
    feature_grad = jnp.transpose(feature_rows, (1, 0, 2))[None, None]

    rows = exchange(rows, ("z_hi", "z_lo", "c"))
    rows = call(sum_z_kernel, message(PEERS, PART + 8), [VM, SM], name="sum_z", out_specs=VM)(rows, own)
    rows = exchange(rows, ("y_hi", "y_lo", "c"))
    decoded = call(
        decode_kernel,
        jax.ShapeDtypeStruct((RGB, PIX), bf16),
        [VM, SM],
        [pltpu.VMEM((ROWS, 8, LANES), f32)],
        name="decode",
        out_specs=VM,
    )(rows, own)
    rows = call(sum_y_kernel, message(8, 2 * PART), [VM], name="sum_y", out_specs=VM)(rows)
    rows = exchange(rows, ("z_lo", "clip"))
    rows, decoded, feature_grad = lax.optimization_barrier((rows, decoded, feature_grad))
    scale = 1.0 / math.sqrt(4 * SLOTS * PIX)
    weight_grad, bias_grad = call(
        functools.partial(finish_kernel, scale),
        (
            jax.ShapeDtypeStruct((TIN, TAPS, RGB, CH), f32),
            jax.ShapeDtypeStruct((1, RGB), f32),
        ),
        [VM],
        [pltpu.VMEM((PARTS * PART, LANES), f32), pltpu.VMEM((24, LANES), f32)],
        name="finish",
        out_specs=(VM, VM),
    )(rows)
    return (decoded[None, None], feature_grad, weight_grad, bias_grad.reshape(RGB))


def solution(mesh):
    parts = Mesh(mesh.devices.reshape(4, 2, 4, 2, 2, 4), ("y_hi", "y_lo", "z_hi", "z_lo", "c", "clip"))
    tile = ("y_hi", "y_lo", "z_hi", "z_lo", "c")
    return jax.shard_map(
        per_device,
        mesh=parts,
        in_specs=(
            P("clip", tile, None, None, None),
            P(),
            P(),
            P(),
            P("clip", None),
            P("clip", tile, None, None),
        ),
        out_specs=(P("clip", tile, None, None), P("clip", tile, None, None, None), P(), P()),
        check_vma=False,
    )
```

```python
import functools
import math

import jax
import jax.numpy as jnp
from jax import lax
from jax.experimental import pallas as pl
from jax.experimental.pallas import tpu as pltpu
from jax.sharding import Mesh
from jax.sharding import PartitionSpec as P

EDGE = 64
OV = 32
PIX = EDGE * EDGE
SLOTS = 128
TX = 16
TY = SLOTS // TX
CH = 96
RGB = 3
TIN = 3
LANES = 128
ROWS = PIX // LANES
BOTH = 2 * SLOTS
TAPS = 9
STACK = TAPS * 8
PARTS = 4
PART = 16
MAIN = 15
BIAS_ROW = 15

BOTH = 2 * SLOTS
TAPS = 9
STACK = TAPS * 8
PEERS = 16
WIDE = 32
SLAB = 16
GRADS = 12
FLAT = WIDE * SLAB
PARTS = 4
PART = 16
MAIN = 15
BIAS_ROW = 15

BOTH = 2 * SLOTS
TAPS = 9
STACK = TAPS * 8
PEERS = 16
WIDE = 32
SLAB = 16
GRADS = 12
FLAT = WIDE * SLAB
PARTS = 4
PART = 16
MAIN = 15
BIAS_ROW = 15

f32 = jnp.float32
bf16 = jnp.bfloat16


def iota(shape, dim):
    return lax.broadcasted_iota(jnp.int32, shape, dim)


def onehot(mask):
    return jnp.where(mask, 1.0, 0.0).astype(bf16)


def pick_rows(mask, rows):
    return jnp.dot(onehot(mask), rows.astype(bf16), preferred_element_type=f32)


def shift_lanes(value, amount):
    size = value.shape[1]
    amount = amount % size
    return value if amount == 0 else pltpu.roll(value, size - amount, 1)


def profile_at(index, profile_ref):
    out = jnp.zeros(index.shape, f32)
    for m in range(OV):
        out = jnp.where(index == m, profile_ref[m].astype(f32), out)
    return out


def no_further(room):
    return jnp.minimum(room, 1.0)


def ids_at(ids, slots):
    spread = onehot(iota(slots.shape, 1) == slots)
    wide = jnp.broadcast_to(ids, (8, SLOTS)).astype(bf16)
    return lax.dot_general(spread, wide, (((1,), (1,)), ((), ())), preferred_element_type=f32)[:, 0:1]


def route_prep(ids, y, z, c, mats_ref, gather_ref):
    y_lo, y_hi, z_lo, z_hi = y % 2, y // 2, z % 2, z // 2
    place = iota((SLOTS, SLOTS), 0) // 4
    target = ids_at(ids, (place // 4) * 16 + z_hi * 4 + place % 4)
    col = iota((1, SLOTS), 1)
    source = jnp.dot(
        jnp.broadcast_to(ids, (8, SLOTS)).astype(bf16),
        onehot(iota((SLOTS, SLOTS), 0) == y_hi * WIDE + col // 4),
        preferred_element_type=f32,
    )[0:1]
    row = iota((SLOTS, 1), 0)
    want = target + (TX * ((row // 2) % 2) + 1024 * (row % 2)).astype(f32)
    have = source + (TX * ((col // 2) % 2) + 1024 * (col % 2)).astype(f32)
    across = target - jnp.floor(target * (1.0 / TX)) * TX
    right = jnp.where(across < TX - 1.5, want + 1.0, -9999.0)
    left = jnp.where(across > 0.5, want - 1.0, -9999.0)
    for n, key in enumerate((want, left, right)):
        mats_ref[n * SLOTS : (n + 1) * SLOTS, :] = onehot(have == key)
    peer = col // 4
    to_y = (col % 4) * 2 + (y_lo ^ (peer // 16))
    to_peer = to_y * 4 + (z_lo ^ ((peer // 2) % 2)) * 2 + (c ^ (peer % 2))
    to_row = to_peer * 4 + (peer // 4) % 4
    mats_ref[3 * SLOTS : 4 * SLOTS, :] = onehot(iota((SLOTS, SLOTS), 0) == to_row)
    col = iota((1, FLAT), 1)
    peer, at = col // SLAB, col % SLAB
    grad_row = (((at // 2) % 2) * 16 + (peer % 8) * 2 + at % 2) * 8 + at // 4
    to_row = jnp.where(at < GRADS, grad_row, BOTH + peer * 4 + at - GRADS)
    gather_ref[...] = onehot(iota((BOTH + SLOTS, FLAT), 0) == to_row)


def class_prep(ids, profile_ref, y, z, c, mats_ref, before_ref, after_ref):
    k = (2 * z + c) * 8 + y
    place = iota((SLOTS, SLOTS), 0)
    leaves = (4 * (((place // 8) % 2) ^ c) + place % 4) * 16 + (place // 16) * 2 + (place // 4) % 2
    spread = iota((SLOTS, SLOTS), 1) == leaves
    place = iota((SLOTS, SLOTS), 1)
    comes = ((place // 16) ^ (y % 2)) * 16 + (place % 4) * 4 + (((place // 8) % 2) ^ (z % 2)) * 2 + (((place // 4) % 2) ^ c)
    come = jnp.dot(
        jnp.broadcast_to(ids, (8, SLOTS)).astype(bf16),
        onehot(iota((SLOTS, SLOTS), 0) == comes),
        preferred_element_type=f32,
    )[0:1]
    own = jnp.sum(jnp.where(spread, jnp.broadcast_to(ids, (SLOTS, SLOTS)), 0.0), axis=1, keepdims=True)
    row = jnp.floor(own * (1.0 / TX))
    col = own - row * TX
    right = jnp.where(col < TX - 1.5, own + 1.0, -9999.0)
    left = jnp.where(col > 0.5, own - 1.0, -9999.0)
    n = 0
    for key in (own, left, right):
        gap = come - key
        for step in (0.0, -float(TX), float(TX)):
            mats_ref[n * SLOTS : (n + 1) * SLOTS, :] = onehot(gap == step)
            n += 1
    h, par, rx = k // 64, (k // 32) % 2, k % 32
    lane = iota((1, LANES), 1)
    east = lane >= 64
    south = (lane // 8) % 2 == 1
    ry = 2 * (8 * h + lane % 8) + par
    fy = profile_at(jnp.where(south, OV - 1 - ry, ry), profile_ref)
    fy_other = profile_at(jnp.where(south, ry, OV - 1 - ry), profile_ref)
    near = profile_ref[rx].astype(f32)
    far = profile_ref[OV - 1 - rx].astype(f32)
    fx = jnp.where(east, far, near)
    fx_other = jnp.where(east, near, far)
    col_there = no_further(jnp.where(east, TX - 1.0 - col, col))
    row_there = no_further(jnp.where(south, TY - 1.0 - row, row))
    before_ref[...] = jnp.broadcast_to(fx * fy, (8, LANES))
    after_ref[...] = 1.0 / ((fx + col_there * fx_other) * (fy + row_there * fy_other))


def ratio_prep(ids, profile_ref, own_slot, ratio_ref):
    own = jnp.sum(jnp.where(iota((1, SLOTS), 1) == own_slot, ids, 0.0), axis=1, keepdims=True)
    row = jnp.floor(own * (1.0 / TX))
    col = own - row * TX
    lane = iota((1, LANES), 1)
    x = lane % EDGE
    y = 2 * iota((ROWS, LANES), 0) + iota((ROWS, LANES), 1) // EDGE
    at_x = jnp.minimum(x, EDGE - 1 - x)
    at_y = jnp.minimum(y, EDGE - 1 - y)
    fx = profile_at(at_x, profile_ref)
    fx_other = profile_at(OV - 1 - at_x, profile_ref)
    fy = profile_at(at_y, profile_ref)
    fy_other = profile_at(OV - 1 - at_y, profile_ref)
    col_there = no_further(jnp.where(x >= OV, TX - 1.0 - col, col))
    row_there = no_further(jnp.where(y >= OV, TY - 1.0 - row, row))
    ratio_ref[...] = fx * fy / ((fx + col_there * fx_other) * (fy + row_there * fy_other))


def pass_on(slabs, core):
    block = jnp.concatenate(slabs, axis=0)
    place = iota((SLOTS, SLOTS), 0)
    y = place // 16
    peer = (place % 8) * 2 + (core ^ (y // 4))
    return pick_rows(iota((SLOTS, SLOTS), 1) == peer * 8 + ((place // 8) % 2) * 4 + y % 4, block)


def route_kernel(got_ref, mats_ref, out_ref):
    slabs = [got_ref[p].astype(f32) for p in range(WIDE)]
    blocks = [jnp.concatenate([slab[4 * o : 4 * o + 4] for slab in slabs], axis=0) for o in range(RGB + 1)]
    every = jnp.dot(
        mats_ref[0 : 3 * SLOTS, :], jnp.concatenate(blocks[:RGB], axis=1).astype(bf16), preferred_element_type=f32
    )
    east = iota((SLOTS, LANES), 1) % EDGE >= OV
    totals = []
    for o in range(RGB):
        here, left, right = (every[n * SLOTS : (n + 1) * SLOTS, o * LANES : (o + 1) * LANES] for n in range(3))
        totals.append(here + jnp.where(east, pltpu.roll(right, OV, 1), pltpu.roll(left, LANES - OV, 1)))
    totals.append(jnp.dot(mats_ref[3 * SLOTS :, :], blocks[RGB].astype(bf16), preferred_element_type=f32))
    for t in range(WIDE):
        out_ref[t] = jnp.concatenate([total[4 * t : 4 * t + 4] for total in totals], axis=0).astype(bf16)


def blend_classes(images, mats_ref, before_ref, after_ref):
    source = images * before_ref[0:1, :]
    high = source.astype(bf16)
    low = (source - high.astype(f32)).astype(bf16)
    lane = iota((SLOTS, LANES), 1)
    south = (lane // 8) % 2 == 1
    every = jnp.dot(mats_ref[...], jnp.concatenate([high, low], axis=1), preferred_element_type=f32)
    every = every[:, :LANES] + every[:, LANES:]
    columns = []
    for d in range(3):
        part = [every[(3 * d + step) * SLOTS : (3 * d + step + 1) * SLOTS] for step in range(3)]
        across = jnp.where(south, part[1], part[2])
        columns.append(part[0] + jnp.where(south, pltpu.roll(across, 8, 1), pltpu.roll(across, LANES - 8, 1)))
    total = columns[0] + pltpu.roll(jnp.where(lane >= 64, columns[1], columns[2]), 64, 1)
    return total * after_ref[...]


def stack_weights(weight_ref, held):
    held[...] = jnp.zeros_like(held)
    for t in range(TIN):
        for tap in range(TAPS):
            held[t, tap * 8 : tap * 8 + RGB, :] = weight_ref[t, tap].astype(f32)


def conv_kernel(
    chunk,
    feat_ref,
    weight_hbm,
    bias_hbm,
    grad_hbm,
    ids_hbm,
    profile_hbm,
    own_ref,
    out_ref,
    route_ref,
    gather_ref,
    mats_ref,
    before_ref,
    after_ref,
    ratio_ref,
    feats,
    stacked_ref,
    weight_ref,
    bias_ref,
    grad_ref,
    ids_ref,
    profile_ref,
    held,
    taps,
    turned,
    place_ref,
    small_sems,
    sems,
):
    small = [(ids_hbm, ids_ref), (profile_hbm, profile_ref), (weight_hbm, weight_ref), (grad_hbm, grad_ref), (bias_hbm, bias_ref)]
    moves = [pltpu.make_async_copy(src, dst, small_sems.at[n]) for n, (src, dst) in enumerate(small)]
    for move in moves:
        move.start()
    copies = []
    for n in range(PIX // chunk):
        part = pl.ds(n * chunk, chunk)
        copies.append(pltpu.make_async_copy(feat_ref.at[:, :, part], feats.at[:, :, part], sems.at[n]))
        copies[-1].start()
    for move in moves:
        move.wait()
    stack_weights(weight_ref, held)
    kernels = [held[t].astype(bf16) for t in range(TIN)]
    for t in range(TIN):
        stacked_ref[t] = kernels[t]
    ids = ids_ref[...].astype(f32)
    own = own_ref[0]
    y, z, c = own // 16, (own // 2) % 8, own % 2
    route_prep(ids, y, z, c, route_ref, gather_ref)
    class_prep(ids, profile_ref, y, z, c, mats_ref, before_ref, after_ref)
    ratio_prep(ids, profile_ref, own, ratio_ref)
    taps[0:8, :] = jnp.zeros((8, PIX), f32)
    taps[0:RGB, :] = grad_ref[...].astype(f32)
    grads = jnp.concatenate([taps[0:8, r * LANES : (r + 1) * LANES] for r in range(ROWS)], axis=0)
    col = iota((1, BOTH), 1)
    r, o = col // 8, col % 8
    to_row = jnp.where(o < RGB, ((r // 2) % 8) * SLAB + o * 4 + (r // 16) * 2 + r % 2, -1)
    eighths = pick_rows(iota((SLOTS, BOTH), 0) == to_row, grads)
    k = iota((1, SLOTS), 1)
    peer = ((k % 2) ^ (y % 2)) * 16 + (k // 32) * 4 + (((k // 16) % 2) ^ (z % 2)) * 2 + (((k // 8) % 2) ^ c)
    place_ref[...] = onehot(iota((FLAT, SLOTS), 0) == peer * SLAB + GRADS + (k % 8) // 2)
    for n in range(PIX // chunk):
        copies[n].wait()
        total = jnp.zeros((STACK, chunk), f32)
        for t in range(TIN):
            total += jnp.dot(kernels[t], feats[t, :, n * chunk : (n + 1) * chunk], preferred_element_type=f32)
        taps[:, n * chunk : (n + 1) * chunk] = total
    lane = iota((8, PIX), 1)
    image = jnp.zeros((8, PIX), f32)
    for kx in range(3):
        column = jnp.zeros((8, PIX), f32)
        for ky in range(3):
            tap = 3 * ky + kx
            moved = shift_lanes(taps[tap * 8 : tap * 8 + 8, :], (ky - 1) * EDGE)
            if ky == 0:
                moved = jnp.where(lane >= EDGE, moved, 0.0)
            elif ky == 2:
                moved = jnp.where(lane < PIX - EDGE, moved, 0.0)
            column = column + moved
        moved = shift_lanes(column, kx - 1)
        if kx == 0:
            moved = jnp.where(lane % EDGE != 0, moved, 0.0)
        elif kx == 2:
            moved = jnp.where(lane % EDGE != EDGE - 1, moved, 0.0)
        image = image + moved
    row = iota((8, 1), 0)
    shift = jnp.zeros((8, 1), f32)
    for o in range(RGB):
        shift = jnp.where(row == o, bias_ref[o], shift)
    image = image + shift
    for r in range(ROWS):
        turned[r] = image[:, r * LANES : (r + 1) * LANES]
    place = iota((LANES, LANES), 0)
    lanes = onehot(iota((LANES, LANES), 1) == ((place // 32) % 2) * 64 + (place // 64) * 32 + place % 32)
    classes = []
    for h in range(2):
        block = half_rows(turned, h, RGB) + [jnp.zeros((16, LANES), f32)]
        block = jnp.concatenate(block, axis=0).astype(bf16)
        both = lax.dot_general(lanes, block, (((1,), (1,)), ((), ())), preferred_element_type=f32)
        classes.append(jnp.concatenate([both[0:64], both[64:128]], axis=1))
    classes = jnp.concatenate(classes, axis=0).astype(bf16)
    images = jnp.dot(place_ref[...], classes, preferred_element_type=f32)
    for p in range(WIDE):
        e = (p // 16) * 4 + p % 4
        slab = images[p * SLAB : (p + 1) * SLAB] + eighths[e * SLAB : (e + 1) * SLAB]
        out_ref[p] = slab.astype(bf16)


def half_rows(turned, h, colours):
    return [turned[qy * 16 + h * 8 : qy * 16 + h * 8 + 8, o, :] for o in range(colours) for qy in range(2)]


def grad_stack(grad, taps):
    lane = iota((8, PIX), 1)
    for kx in range(3):
        moved_x = shift_lanes(grad, 1 - kx)
        if kx == 0:
            moved_x = jnp.where(lane % EDGE != EDGE - 1, moved_x, 0.0)
        elif kx == 2:
            moved_x = jnp.where(lane % EDGE != 0, moved_x, 0.0)
        for ky in range(3):
            moved = shift_lanes(moved_x, (1 - ky) * EDGE)
            if ky == 0:
                moved = jnp.where(lane < PIX - EDGE, moved, 0.0)
            elif ky == 2:
                moved = jnp.where(lane >= EDGE, moved, 0.0)
            tap = 3 * ky + kx
            taps[tap * 8 : tap * 8 + 8, :] = moved


def split_bias(part):
    at = iota((PART, LANES), 0) == BIAS_ROW
    lane = iota((PART, LANES), 1)
    total = part + pltpu.roll(part, LANES - RGB, 1)
    high = total.astype(bf16).astype(f32)
    low = pltpu.roll(total - high, RGB, 1)
    pair = jnp.where(lane < RGB, high, jnp.where(lane < 2 * RGB, low, part))
    return jnp.where(at, pair, part)


def weight_grad_kernel(
    chunk, got_ref, feat_ref, ratio_ref, gather_ref, mats_ref, before_ref, after_ref, out_ref, stack_ref, taps
):
    every = jnp.dot(gather_ref[...], got_ref[...].reshape(FLAT, LANES), preferred_element_type=f32)
    pieces = []
    for r in range(ROWS):
        piece = every[r * 8 : r * 8 + 8] * ratio_ref[r : r + 1, :]
        pieces.append(piece.astype(bf16).astype(f32))
    grad = jnp.concatenate(pieces, axis=1)
    blended = blend_classes(every[BOTH : BOTH + SLOTS], mats_ref, before_ref, after_ref)
    grad_stack(grad, taps)
    summed = pieces[0]
    for piece in pieces[1:]:
        summed = summed + piece
    diagonal = iota((8, LANES), 0) == iota((8, LANES), 1)
    bias = jnp.sum(
        jnp.where(diagonal, jnp.sum(summed, axis=1, keepdims=True), 0.0), axis=0, keepdims=True
    )
    total = jnp.zeros((TIN * CH, STACK), f32)
    for at in range(0, PIX, chunk):
        part = taps[:, at : at + chunk].astype(bf16)
        stack_ref[:, at : at + chunk] = part
        total += lax.dot_general(
            feat_ref[:, :, at : at + chunk].reshape(TIN * CH, chunk),
            part,
            (((1,), (1,)), ((), ())),
            preferred_element_type=f32,
        )
    rows = jnp.concatenate([total[t * CH : (t + 1) * CH].T for t in range(TIN)], axis=0)
    rows = jnp.concatenate([rows, jnp.zeros((TIN * STACK, LANES - CH), f32)], axis=1).astype(bf16)
    every = PARTS * PART
    place = iota((2 * every, TIN * STACK), 0)
    source = iota((2 * every, TIN * STACK), 1)
    rank = jnp.where(source % 8 < RGB, (source // 8) * RGB + source % 8, -1)
    within = place % PART
    main = (rank == (place // PART) * MAIN + within) & (within < MAIN) & (place < every)
    offset = place - every - RGB * (rank - PARTS * MAIN)
    side = (offset >= 0) & (offset < RGB) & (place >= every) & (rank >= PARTS * MAIN)
    chosen = jnp.dot(onehot(main | side), rows, preferred_element_type=f32)
    lane = iota((every, LANES), 1)
    third = iota((every, LANES), 0) % 3
    tail = jnp.zeros((every, LANES), f32)
    for c in range(3):
        tail = jnp.where(third == c, pltpu.roll(chosen[every:], CH - 32 * c, 1), tail)
    packed = jnp.where(lane < CH, chosen[:every], tail)
    packed = jnp.where((iota((every, LANES), 0) % PART == BIAS_ROW) & (lane < CH), bias, packed)
    parts = [split_bias(packed[q * PART : (q + 1) * PART]) for q in range(PARTS)]
    for p in range(PEERS):
        out_ref[p] = jnp.concatenate([parts[p % PARTS], blended[p * 8 : p * 8 + 8]], axis=0).astype(bf16)


def feature_grad_kernel(stack_ref, weight_ref, out_ref):
    for t in range(TIN):
        out_ref[t] = lax.dot_general(
            weight_ref[t], stack_ref[...], (((0,), (0,)), ((), ())), preferred_element_type=f32
        ).astype(bf16)


def decode_kernel(got_ref, own_ref, image_ref, turned):
    images = jnp.concatenate([got_ref[n].astype(f32)[PART : PART + 8] for n in range(PEERS)], axis=0)
    block = jnp.concatenate([images[:, 0:64], images[:, 64:128]], axis=0).astype(bf16)
    row = iota((BOTH, LANES), 0)
    lane = iota((BOTH, LANES), 1)
    k = ((row % 8) * 2 + (((row // 8) % 2) ^ (own_ref[0] // 64))) * 8 + (row // 16) % 8
    spot = ((k // 32) % 2) * 64 + (row // SLOTS) * 32 + k % 32
    for h in range(2):
        lanes = onehot((lane == spot) & (k // 64 == h))
        tile = lax.dot_general(block, lanes, (((0,), (0,)), ((), ())), preferred_element_type=f32)
        for o in range(RGB):
            for qy in range(2):
                turned[qy * 16 + h * 8 : qy * 16 + h * 8 + 8, o, :] = tile[o * 16 + qy * 8 : o * 16 + qy * 8 + 8]
    for r in range(ROWS):
        image_ref[:, r * LANES : (r + 1) * LANES] = turned[r, 0:RGB, :].astype(bf16)


def sum_z_kernel(got_ref, own_ref, out_ref):
    slabs = [got_ref[p].astype(f32) for p in range(PEERS)]
    part = slabs[0][0:PART]
    for slab in slabs[1:]:
        part = part + slab[0:PART]
    part = split_bias(part)
    images = pass_on([slab[PART : PART + 8] for slab in slabs], own_ref[0] % 2)
    for t in range(PEERS):
        out_ref[t] = jnp.concatenate([part, images[t * 8 : t * 8 + 8]], axis=0).astype(bf16)


def sum_y_kernel(got_ref, out_ref):
    parts = []
    for c in range(2):
        part = got_ref[c].astype(f32)[0:PART]
        for y in range(1, 8):
            part = part + got_ref[2 * y + c].astype(f32)[0:PART]
        parts.append(split_bias(part))
    both = jnp.concatenate(parts, axis=0).astype(bf16)
    for n in range(out_ref.shape[0]):
        out_ref[n] = both


def finish_kernel(scale, got_ref, weight_ref, bias_ref, held, others):
    for z in range(2):
        total = got_ref[4 * z].astype(f32)
        for n in range(1, 4):
            total = total + got_ref[4 * z + n].astype(f32)
        held[2 * PART * z : 2 * PART * (z + 1), :] = total * scale
    bias = held[BIAS_ROW : BIAS_ROW + 1, :]
    bias_ref[...] = bias[:, 0:RGB] + bias[:, RGB : 2 * RGB]
    count = TIN * TAPS * RGB - PARTS * MAIN
    lane = iota((count, LANES), 1)
    tail = jnp.zeros((count, LANES), f32)
    for c in range(3):
        turned = pltpu.roll(held[pl.ds(c, count, stride=3), :], (32 + 32 * c) % LANES, 1)
        tail = jnp.where(lane // 32 == c, turned, tail)
    others[0:count, :] = tail
    for n in range(TIN * TAPS):
        at = n * RGB
        if at < PARTS * MAIN:
            at = (at // MAIN) * PART + at % MAIN
            value = held[at : at + RGB, 0:CH]
        else:
            at -= PARTS * MAIN
            value = others[at : at + RGB, 0:CH]
        weight_ref[n // TAPS, n % TAPS] = value


VM = pl.BlockSpec(memory_space=pltpu.VMEM)
SM = pl.BlockSpec(memory_space=pltpu.SMEM)
HBM = pl.BlockSpec(memory_space=pltpu.HBM)
LIMIT = 40 * 1024 * 1024


def call(body, out_shape, in_specs, scratch=(), flops=1 << 20, size=1 << 17, name=None, limit=LIMIT, **rest):
    return pl.pallas_call(
        body,
        out_shape=out_shape,
        in_specs=in_specs,
        scratch_shapes=list(scratch),
        compiler_params=pltpu.CompilerParams(vmem_limit_bytes=limit),
        cost_estimate=pl.CostEstimate(flops=flops, bytes_accessed=size, transcendentals=0),
        name=name,
        **rest,
    )


def exchange(rows, axes):
    return lax.all_to_all(rows, axes, 0, 0, tiled=True)


def message(peers, rows):
    return jax.ShapeDtypeStruct((peers, rows, LANES), bf16)


def per_device(features, conv_weight, bias, blend_profile, tile_ids, reward_grad):
    chunk = 1024
    conv_flops = 2 * STACK * TIN * CH * PIX
    own = lax.axis_index(("y_hi", "y_lo", "z_hi", "z_lo", "c")).reshape(1).astype(jnp.int32)
    feats = jnp.transpose(features[0, 0], (1, 0, 2))
    args = (feats, conv_weight, bias, reward_grad[0, 0], tile_ids, blend_profile)
    here = [pltpu.with_memory_space_constraint(x, pltpu.HBM) for x in args]
    rows, route, gather, mats, before, after, ratio, feats_held, weights_held = call(
        functools.partial(conv_kernel, 2 * chunk),
        (
            pltpu.VMEM((WIDE, SLAB, LANES), bf16),
            pltpu.VMEM((4 * SLOTS, SLOTS), bf16),
            pltpu.VMEM((BOTH + SLOTS, FLAT), bf16),
            pltpu.VMEM((9 * SLOTS, SLOTS), bf16),
            pltpu.VMEM((8, LANES), f32),
            pltpu.VMEM((SLOTS, LANES), f32),
            pltpu.VMEM((ROWS, LANES), f32),
            pltpu.VMEM((TIN, CH, PIX), bf16),
            pltpu.VMEM((TIN, STACK, CH), bf16),
        ),
        [HBM, HBM, HBM, HBM, HBM, HBM, SM],
        [
            pltpu.VMEM((TIN, TAPS, RGB, CH), bf16),
            pltpu.SMEM((RGB,), f32),
            pltpu.VMEM((RGB, PIX), bf16),
            pltpu.VMEM((1, SLOTS), jnp.int32),
            pltpu.SMEM((OV,), jnp.int32),
            pltpu.VMEM((TIN, STACK, CH), f32),
            pltpu.VMEM((STACK, PIX), f32),
            pltpu.VMEM((ROWS, 8, LANES), f32),
            pltpu.VMEM((FLAT, SLOTS), bf16),
            pltpu.SemaphoreType.DMA((5,)),
            pltpu.SemaphoreType.DMA((PIX // (2 * chunk),)),
        ],
        conv_flops,
        1 << 22,
        "conv",
        out_specs=(VM,) * 9,
    )(*here, own)
    rows = exchange(rows, ("y_lo", "z_hi", "z_lo", "c"))
    rows = call(
        route_kernel, message(WIDE, SLAB), [VM, VM], (), 1 << 28, 1 << 21, "route", out_specs=VM
    )(rows, route)
    rows = exchange(rows, ("y_hi", "y_lo", "z_lo", "c"))
    rows, stack = call(
        functools.partial(weight_grad_kernel, chunk),
        (message(PEERS, PART + 8), jax.ShapeDtypeStruct((STACK, PIX), bf16)),
        [VM] * 7,
        [pltpu.VMEM((STACK, PIX), f32)],
        conv_flops,
        1 << 22,
        "weight_grad",
        out_specs=(VM, VM),
    )(rows, feats_held, ratio, gather, mats, before, after)

    feature_rows = call(
        feature_grad_kernel,
        jax.ShapeDtypeStruct((TIN, CH, PIX), bf16),
        [
            pl.BlockSpec((STACK, chunk), lambda i: (0, i)),
            pl.BlockSpec((TIN, STACK, CH), lambda i: (0, 0, 0)),
        ],
        (),
        conv_flops,
        1 << 22,
        "feature_grad",
        grid=(PIX // chunk,),
        out_specs=pl.BlockSpec((TIN, CH, chunk), lambda i: (0, 0, i)),
    )(stack, weights_held)
    feature_grad = jnp.transpose(feature_rows, (1, 0, 2))[None, None]

    rows = exchange(rows, ("z_hi", "z_lo", "c"))
    rows = call(sum_z_kernel, message(PEERS, PART + 8), [VM, SM], name="sum_z", out_specs=VM)(rows, own)
    rows = exchange(rows, ("y_hi", "y_lo", "c"))
    decoded = call(
        decode_kernel,
        jax.ShapeDtypeStruct((RGB, PIX), bf16),
        [VM, SM],
        [pltpu.VMEM((ROWS, 8, LANES), f32)],
        name="decode",
        out_specs=VM,
    )(rows, own)
    rows = call(sum_y_kernel, message(8, 2 * PART), [VM], name="sum_y", out_specs=VM)(rows)
    rows = exchange(rows, ("z_lo", "clip"))
    rows, decoded, feature_grad = lax.optimization_barrier((rows, decoded, feature_grad))
    scale = 1.0 / math.sqrt(4 * SLOTS * PIX)
    weight_grad, bias_grad = call(
        functools.partial(finish_kernel, scale),
        (
            jax.ShapeDtypeStruct((TIN, TAPS, RGB, CH), f32),
            jax.ShapeDtypeStruct((1, RGB), f32),
        ),
        [VM],
        [pltpu.VMEM((PARTS * PART, LANES), f32), pltpu.VMEM((24, LANES), f32)],
        name="finish",
        out_specs=(VM, VM),
    )(rows)
    return (decoded[None, None], feature_grad, weight_grad, bias_grad.reshape(RGB))


def solution(mesh):
    parts = Mesh(mesh.devices.reshape(4, 2, 4, 2, 2, 4), ("y_hi", "y_lo", "z_hi", "z_lo", "c", "clip"))
    tile = ("y_hi", "y_lo", "z_hi", "z_lo", "c")
    return jax.shard_map(
        per_device,
        mesh=parts,
        in_specs=(
            P("clip", tile, None, None, None),
            P(),
            P(),
            P(),
            P("clip", None),
            P("clip", tile, None, None),
        ),
        out_specs=(P("clip", tile, None, None), P("clip", tile, None, None, None), P(), P()),
        check_vma=False,
    )
```

```python
import functools
import math

import jax
import jax.numpy as jnp
from jax import lax
from jax.experimental import pallas as pl
from jax.experimental.pallas import tpu as pltpu
from jax.sharding import Mesh
from jax.sharding import PartitionSpec as P

EDGE = 64
OV = 32
PIX = EDGE * EDGE
SLOTS = 128
TX = 16
TY = SLOTS // TX
CH = 96
RGB = 3
TIN = 3
LANES = 128
ROWS = PIX // LANES
BOTH = 2 * SLOTS
TAPS = 9
STACK = TAPS * 8
PARTS = 4
PART = 16
MAIN = 15
BIAS_ROW = 15

BOTH = 2 * SLOTS
TAPS = 9
STACK = TAPS * 8
PEERS = 16
WIDE = 32
SLAB = 16
GRADS = 12
FLAT = WIDE * SLAB
PARTS = 4
PART = 16
MAIN = 15
BIAS_ROW = 15

BOTH = 2 * SLOTS
TAPS = 9
STACK = TAPS * 8
PEERS = 16
WIDE = 32
SLAB = 16
GRADS = 12
FLAT = WIDE * SLAB
PARTS = 4
PART = 16
MAIN = 15
BIAS_ROW = 15

f32 = jnp.float32
bf16 = jnp.bfloat16


def iota(shape, dim):
    return lax.broadcasted_iota(jnp.int32, shape, dim)


def onehot(mask):
    return jnp.where(mask, 1.0, 0.0).astype(bf16)


def pick_rows(mask, rows):
    return jnp.dot(onehot(mask), rows.astype(bf16), preferred_element_type=f32)


def shift_lanes(value, amount):
    size = value.shape[1]
    amount = amount % size
    return value if amount == 0 else pltpu.roll(value, size - amount, 1)


def profile_at(index, profile_ref):
    out = jnp.zeros(index.shape, f32)
    for m in range(OV):
        out = jnp.where(index == m, profile_ref[m].astype(f32), out)
    return out


def no_further(room):
    return jnp.minimum(room, 1.0)


def ids_at(ids, slots):
    spread = onehot(iota(slots.shape, 1) == slots)
    wide = jnp.broadcast_to(ids, (8, SLOTS)).astype(bf16)
    return lax.dot_general(spread, wide, (((1,), (1,)), ((), ())), preferred_element_type=f32)[:, 0:1]


def route_prep(ids, y, z, c, mats_ref):
    y_lo, y_hi, z_lo, z_hi = y % 2, y // 2, z % 2, z // 2
    place = iota((SLOTS, SLOTS), 0) // 4
    target = ids_at(ids, (place // 4) * 16 + z_hi * 4 + place % 4)
    col = iota((1, SLOTS), 1)
    source = jnp.dot(
        jnp.broadcast_to(ids, (8, SLOTS)).astype(bf16),
        onehot(iota((SLOTS, SLOTS), 0) == y_hi * WIDE + col // 4),
        preferred_element_type=f32,
    )[0:1]
    row = iota((SLOTS, 1), 0)
    want = target + (TX * ((row // 2) % 2) + 1024 * (row % 2)).astype(f32)
    have = source + (TX * ((col // 2) % 2) + 1024 * (col % 2)).astype(f32)
    across = target - jnp.floor(target * (1.0 / TX)) * TX
    right = jnp.where(across < TX - 1.5, want + 1.0, -9999.0)
    left = jnp.where(across > 0.5, want - 1.0, -9999.0)
    for n, key in enumerate((want, left, right)):
        mats_ref[n * SLOTS : (n + 1) * SLOTS, :] = onehot(have == key)
    peer = col // 4
    to_y = (col % 4) * 2 + (y_lo ^ (peer // 16))
    to_peer = to_y * 4 + (z_lo ^ ((peer // 2) % 2)) * 2 + (c ^ (peer % 2))
    to_row = to_peer * 4 + (peer // 4) % 4
    mats_ref[3 * SLOTS : 4 * SLOTS, :] = onehot(iota((SLOTS, SLOTS), 0) == to_row)


def class_prep(ids, profile_ref, y, z, c, mats_ref, before_ref, after_ref):
    k = (2 * z + c) * 8 + y
    place = iota((SLOTS, SLOTS), 0)
    leaves = (4 * (((place // 8) % 2) ^ c) + place % 4) * 16 + (place // 16) * 2 + (place // 4) % 2
    spread = iota((SLOTS, SLOTS), 1) == leaves
    place = iota((SLOTS, SLOTS), 1)
    comes = ((place // 16) ^ (y % 2)) * 16 + (place % 4) * 4 + (((place // 8) % 2) ^ (z % 2)) * 2 + (((place // 4) % 2) ^ c)
    come = jnp.dot(
        jnp.broadcast_to(ids, (8, SLOTS)).astype(bf16),
        onehot(iota((SLOTS, SLOTS), 0) == comes),
        preferred_element_type=f32,
    )[0:1]
    own = jnp.sum(jnp.where(spread, jnp.broadcast_to(ids, (SLOTS, SLOTS)), 0.0), axis=1, keepdims=True)
    row = jnp.floor(own * (1.0 / TX))
    col = own - row * TX
    right = jnp.where(col < TX - 1.5, own + 1.0, -9999.0)
    left = jnp.where(col > 0.5, own - 1.0, -9999.0)
    n = 0
    for key in (own, left, right):
        gap = come - key
        for step in (0.0, -float(TX), float(TX)):
            mats_ref[n * SLOTS : (n + 1) * SLOTS, :] = onehot(gap == step)
            n += 1
    h, par, rx = k // 64, (k // 32) % 2, k % 32
    lane = iota((1, LANES), 1)
    east = lane >= 64
    south = (lane // 8) % 2 == 1
    ry = 2 * (8 * h + lane % 8) + par
    fy = profile_at(jnp.where(south, OV - 1 - ry, ry), profile_ref)
    fy_other = profile_at(jnp.where(south, ry, OV - 1 - ry), profile_ref)
    near = profile_ref[rx].astype(f32)
    far = profile_ref[OV - 1 - rx].astype(f32)
    fx = jnp.where(east, far, near)
    fx_other = jnp.where(east, near, far)
    col_there = no_further(jnp.where(east, TX - 1.0 - col, col))
    row_there = no_further(jnp.where(south, TY - 1.0 - row, row))
    before_ref[...] = jnp.broadcast_to(fx * fy, (8, LANES))
    after_ref[...] = 1.0 / ((fx + col_there * fx_other) * (fy + row_there * fy_other))


def ratio_prep(ids, profile_ref, own_slot, ratio_ref):
    own = jnp.sum(jnp.where(iota((1, SLOTS), 1) == own_slot, ids, 0.0), axis=1, keepdims=True)
    row = jnp.floor(own * (1.0 / TX))
    col = own - row * TX
    lane = iota((1, LANES), 1)
    x = lane % EDGE
    y = 2 * iota((ROWS, LANES), 0) + iota((ROWS, LANES), 1) // EDGE
    at_x = jnp.minimum(x, EDGE - 1 - x)
    at_y = jnp.minimum(y, EDGE - 1 - y)
    fx = profile_at(at_x, profile_ref)
    fx_other = profile_at(OV - 1 - at_x, profile_ref)
    fy = profile_at(at_y, profile_ref)
    fy_other = profile_at(OV - 1 - at_y, profile_ref)
    col_there = no_further(jnp.where(x >= OV, TX - 1.0 - col, col))
    row_there = no_further(jnp.where(y >= OV, TY - 1.0 - row, row))
    ratio_ref[...] = fx * fy / ((fx + col_there * fx_other) * (fy + row_there * fy_other))


def pass_on(slabs, core):
    block = jnp.concatenate(slabs, axis=0)
    place = iota((SLOTS, SLOTS), 0)
    y = place // 16
    peer = (place % 8) * 2 + (core ^ (y // 4))
    return pick_rows(iota((SLOTS, SLOTS), 1) == peer * 8 + ((place // 8) % 2) * 4 + y % 4, block)


def route_kernel(got_ref, mats_ref, out_ref):
    slabs = [got_ref[p].astype(f32) for p in range(WIDE)]
    blocks = [jnp.concatenate([slab[4 * o : 4 * o + 4] for slab in slabs], axis=0) for o in range(RGB + 1)]
    every = jnp.dot(
        mats_ref[0 : 3 * SLOTS, :], jnp.concatenate(blocks[:RGB], axis=1).astype(bf16), preferred_element_type=f32
    )
    east = iota((SLOTS, LANES), 1) % EDGE >= OV
    totals = []
    for o in range(RGB):
        here, left, right = (every[n * SLOTS : (n + 1) * SLOTS, o * LANES : (o + 1) * LANES] for n in range(3))
        totals.append(here + jnp.where(east, pltpu.roll(right, OV, 1), pltpu.roll(left, LANES - OV, 1)))
    totals.append(jnp.dot(mats_ref[3 * SLOTS :, :], blocks[RGB].astype(bf16), preferred_element_type=f32))
    for t in range(WIDE):
        out_ref[t] = jnp.concatenate([total[4 * t : 4 * t + 4] for total in totals], axis=0).astype(bf16)


def blend_classes(images, mats_ref, before_ref, after_ref):
    source = images * before_ref[0:1, :]
    high = source.astype(bf16)
    low = (source - high.astype(f32)).astype(bf16)
    lane = iota((SLOTS, LANES), 1)
    south = (lane // 8) % 2 == 1
    every = jnp.dot(mats_ref[...], jnp.concatenate([high, low], axis=1), preferred_element_type=f32)
    every = every[:, :LANES] + every[:, LANES:]
    columns = []
    for d in range(3):
        part = [every[(3 * d + step) * SLOTS : (3 * d + step + 1) * SLOTS] for step in range(3)]
        across = jnp.where(south, part[1], part[2])
        columns.append(part[0] + jnp.where(south, pltpu.roll(across, 8, 1), pltpu.roll(across, LANES - 8, 1)))
    total = columns[0] + pltpu.roll(jnp.where(lane >= 64, columns[1], columns[2]), 64, 1)
    return total * after_ref[...]


def stack_weights(weight_ref, held):
    held[...] = jnp.zeros_like(held)
    for t in range(TIN):
        for tap in range(TAPS):
            held[t, tap * 8 : tap * 8 + RGB, :] = weight_ref[t, tap].astype(f32)


def conv_kernel(
    chunk,
    feat_ref,
    weight_hbm,
    bias_hbm,
    grad_hbm,
    ids_hbm,
    profile_hbm,
    own_ref,
    out_ref,
    route_ref,
    mats_ref,
    before_ref,
    after_ref,
    ratio_ref,
    feats,
    stacked_ref,
    weight_ref,
    bias_ref,
    grad_ref,
    ids_ref,
    profile_ref,
    held,
    taps,
    turned,
    place_ref,
    small_sems,
    sems,
):
    small = [(ids_hbm, ids_ref), (profile_hbm, profile_ref), (weight_hbm, weight_ref), (grad_hbm, grad_ref), (bias_hbm, bias_ref)]
    moves = [pltpu.make_async_copy(src, dst, small_sems.at[n]) for n, (src, dst) in enumerate(small)]
    for move in moves:
        move.start()
    copies = []
    for n in range(PIX // chunk):
        part = pl.ds(n * chunk, chunk)
        copies.append(pltpu.make_async_copy(feat_ref.at[:, :, part], feats.at[:, :, part], sems.at[n]))
        copies[-1].start()
    for move in moves:
        move.wait()
    stack_weights(weight_ref, held)
    kernels = [held[t].astype(bf16) for t in range(TIN)]
    for t in range(TIN):
        stacked_ref[t] = kernels[t]
    ids = ids_ref[...].astype(f32)
    own = own_ref[0]
    y, z, c = own // 16, (own // 2) % 8, own % 2
    route_prep(ids, y, z, c, route_ref)
    class_prep(ids, profile_ref, y, z, c, mats_ref, before_ref, after_ref)
    ratio_prep(ids, profile_ref, own, ratio_ref)
    taps[0:8, :] = jnp.zeros((8, PIX), f32)
    taps[0:RGB, :] = grad_ref[...].astype(f32)
    grads = jnp.concatenate([taps[0:8, r * LANES : (r + 1) * LANES] for r in range(ROWS)], axis=0)
    col = iota((1, BOTH), 1)
    r, o = col // 8, col % 8
    to_row = jnp.where(o < RGB, ((r // 2) % 8) * SLAB + o * 4 + (r // 16) * 2 + r % 2, -1)
    eighths = pick_rows(iota((SLOTS, BOTH), 0) == to_row, grads)
    k = iota((1, SLOTS), 1)
    peer = ((k % 2) ^ (y % 2)) * 16 + (k // 32) * 4 + (((k // 16) % 2) ^ (z % 2)) * 2 + (((k // 8) % 2) ^ c)
    place_ref[...] = onehot(iota((FLAT, SLOTS), 0) == peer * SLAB + GRADS + (k % 8) // 2)
    for n in range(PIX // chunk):
        copies[n].wait()
        total = jnp.zeros((STACK, chunk), f32)
        for t in range(TIN):
            total += jnp.dot(kernels[t], feats[t, :, n * chunk : (n + 1) * chunk], preferred_element_type=f32)
        taps[:, n * chunk : (n + 1) * chunk] = total
    lane = iota((8, PIX), 1)
    image = jnp.zeros((8, PIX), f32)
    for kx in range(3):
        column = jnp.zeros((8, PIX), f32)
        for ky in range(3):
            tap = 3 * ky + kx
            moved = shift_lanes(taps[tap * 8 : tap * 8 + 8, :], (ky - 1) * EDGE)
            if ky == 0:
                moved = jnp.where(lane >= EDGE, moved, 0.0)
            elif ky == 2:
                moved = jnp.where(lane < PIX - EDGE, moved, 0.0)
            column = column + moved
        moved = shift_lanes(column, kx - 1)
        if kx == 0:
            moved = jnp.where(lane % EDGE != 0, moved, 0.0)
        elif kx == 2:
            moved = jnp.where(lane % EDGE != EDGE - 1, moved, 0.0)
        image = image + moved
    row = iota((8, 1), 0)
    shift = jnp.zeros((8, 1), f32)
    for o in range(RGB):
        shift = jnp.where(row == o, bias_ref[o], shift)
    image = image + shift
    for r in range(ROWS):
        turned[r] = image[:, r * LANES : (r + 1) * LANES]
    place = iota((LANES, LANES), 0)
    lanes = onehot(iota((LANES, LANES), 1) == ((place // 32) % 2) * 64 + (place // 64) * 32 + place % 32)
    classes = []
    for h in range(2):
        block = half_rows(turned, h, RGB) + [jnp.zeros((16, LANES), f32)]
        block = jnp.concatenate(block, axis=0).astype(bf16)
        both = lax.dot_general(lanes, block, (((1,), (1,)), ((), ())), preferred_element_type=f32)
        classes.append(jnp.concatenate([both[0:64], both[64:128]], axis=1))
    classes = jnp.concatenate(classes, axis=0).astype(bf16)
    images = jnp.dot(place_ref[...], classes, preferred_element_type=f32)
    for p in range(WIDE):
        e = (p // 16) * 4 + p % 4
        slab = images[p * SLAB : (p + 1) * SLAB] + eighths[e * SLAB : (e + 1) * SLAB]
        out_ref[p] = slab.astype(bf16)


def half_rows(turned, h, colours):
    return [turned[qy * 16 + h * 8 : qy * 16 + h * 8 + 8, o, :] for o in range(colours) for qy in range(2)]


def grad_stack(grad, taps):
    lane = iota((8, PIX), 1)
    for kx in range(3):
        moved_x = shift_lanes(grad, 1 - kx)
        if kx == 0:
            moved_x = jnp.where(lane % EDGE != EDGE - 1, moved_x, 0.0)
        elif kx == 2:
            moved_x = jnp.where(lane % EDGE != 0, moved_x, 0.0)
        for ky in range(3):
            moved = shift_lanes(moved_x, (1 - ky) * EDGE)
            if ky == 0:
                moved = jnp.where(lane < PIX - EDGE, moved, 0.0)
            elif ky == 2:
                moved = jnp.where(lane >= EDGE, moved, 0.0)
            tap = 3 * ky + kx
            taps[tap * 8 : tap * 8 + 8, :] = moved


def split_bias(part):
    at = iota((PART, LANES), 0) == BIAS_ROW
    lane = iota((PART, LANES), 1)
    total = part + pltpu.roll(part, LANES - RGB, 1)
    high = total.astype(bf16).astype(f32)
    low = pltpu.roll(total - high, RGB, 1)
    pair = jnp.where(lane < RGB, high, jnp.where(lane < 2 * RGB, low, part))
    return jnp.where(at, pair, part)


def weight_grad_kernel(
    chunk, got_ref, feat_ref, ratio_ref, mats_ref, before_ref, after_ref, out_ref, stack_ref, taps, added
):
    slabs = [got_ref[n].astype(f32) for n in range(WIDE)]
    for e in range(8):
        added[e * SLAB : (e + 1) * SLAB, :] = slabs[e] + slabs[e + 8] + slabs[e + 16] + slabs[e + 24]
    added[SLOTS:, :] = jnp.zeros((32, LANES), f32)
    colour = iota((8, LANES), 0) < RGB
    pieces = []
    for r in range(ROWS):
        first = ((r // 2) % 8) * SLAB + (r // 16) * 2 + r % 2
        piece = added[pl.ds(first, 8, stride=4), :] * ratio_ref[r : r + 1, :]
        pieces.append(jnp.where(colour, piece, 0.0).astype(bf16).astype(f32))
    grad = jnp.concatenate(pieces, axis=1)
    images = jnp.concatenate([slab[GRADS:] for slab in slabs], axis=0)
    blended = blend_classes(images, mats_ref, before_ref, after_ref)
    grad_stack(grad, taps)
    summed = pieces[0]
    for piece in pieces[1:]:
        summed = summed + piece
    diagonal = iota((8, LANES), 0) == iota((8, LANES), 1)
    bias = jnp.sum(
        jnp.where(diagonal, jnp.sum(summed, axis=1, keepdims=True), 0.0), axis=0, keepdims=True
    )
    total = jnp.zeros((TIN * CH, STACK), f32)
    for at in range(0, PIX, chunk):
        part = taps[:, at : at + chunk].astype(bf16)
        stack_ref[:, at : at + chunk] = part
        total += lax.dot_general(
            feat_ref[:, :, at : at + chunk].reshape(TIN * CH, chunk),
            part,
            (((1,), (1,)), ((), ())),
            preferred_element_type=f32,
        )
    rows = jnp.concatenate([total[t * CH : (t + 1) * CH].T for t in range(TIN)], axis=0)
    rows = jnp.concatenate([rows, jnp.zeros((TIN * STACK, LANES - CH), f32)], axis=1).astype(bf16)
    every = PARTS * PART
    place = iota((2 * every, TIN * STACK), 0)
    source = iota((2 * every, TIN * STACK), 1)
    rank = jnp.where(source % 8 < RGB, (source // 8) * RGB + source % 8, -1)
    within = place % PART
    main = (rank == (place // PART) * MAIN + within) & (within < MAIN) & (place < every)
    offset = place - every - RGB * (rank - PARTS * MAIN)
    side = (offset >= 0) & (offset < RGB) & (place >= every) & (rank >= PARTS * MAIN)
    chosen = jnp.dot(onehot(main | side), rows, preferred_element_type=f32)
    lane = iota((every, LANES), 1)
    third = iota((every, LANES), 0) % 3
    tail = jnp.zeros((every, LANES), f32)
    for c in range(3):
        tail = jnp.where(third == c, pltpu.roll(chosen[every:], CH - 32 * c, 1), tail)
    packed = jnp.where(lane < CH, chosen[:every], tail)
    packed = jnp.where((iota((every, LANES), 0) % PART == BIAS_ROW) & (lane < CH), bias, packed)
    parts = [split_bias(packed[q * PART : (q + 1) * PART]) for q in range(PARTS)]
    for p in range(PEERS):
        out_ref[p] = jnp.concatenate([parts[p % PARTS], blended[p * 8 : p * 8 + 8]], axis=0).astype(bf16)


def feature_grad_kernel(stack_ref, weight_ref, out_ref):
    for t in range(TIN):
        out_ref[t] = lax.dot_general(
            weight_ref[t], stack_ref[...], (((0,), (0,)), ((), ())), preferred_element_type=f32
        ).astype(bf16)


def decode_kernel(got_ref, own_ref, image_ref, turned):
    images = jnp.concatenate([got_ref[n].astype(f32)[PART : PART + 8] for n in range(PEERS)], axis=0)
    block = jnp.concatenate([images[:, 0:64], images[:, 64:128]], axis=0).astype(bf16)
    row = iota((BOTH, LANES), 0)
    lane = iota((BOTH, LANES), 1)
    k = ((row % 8) * 2 + (((row // 8) % 2) ^ (own_ref[0] // 64))) * 8 + (row // 16) % 8
    spot = ((k // 32) % 2) * 64 + (row // SLOTS) * 32 + k % 32
    for h in range(2):
        lanes = onehot((lane == spot) & (k // 64 == h))
        tile = lax.dot_general(block, lanes, (((0,), (0,)), ((), ())), preferred_element_type=f32)
        for o in range(RGB):
            for qy in range(2):
                turned[qy * 16 + h * 8 : qy * 16 + h * 8 + 8, o, :] = tile[o * 16 + qy * 8 : o * 16 + qy * 8 + 8]
    for r in range(ROWS):
        image_ref[:, r * LANES : (r + 1) * LANES] = turned[r, 0:RGB, :].astype(bf16)


def sum_z_kernel(got_ref, own_ref, out_ref):
    slabs = [got_ref[p].astype(f32) for p in range(PEERS)]
    part = slabs[0][0:PART]
    for slab in slabs[1:]:
        part = part + slab[0:PART]
    part = split_bias(part)
    images = pass_on([slab[PART : PART + 8] for slab in slabs], own_ref[0] % 2)
    for t in range(PEERS):
        out_ref[t] = jnp.concatenate([part, images[t * 8 : t * 8 + 8]], axis=0).astype(bf16)


def sum_y_kernel(got_ref, out_ref):
    parts = []
    for c in range(2):
        part = got_ref[c].astype(f32)[0:PART]
        for y in range(1, 8):
            part = part + got_ref[2 * y + c].astype(f32)[0:PART]
        parts.append(split_bias(part))
    both = jnp.concatenate(parts, axis=0).astype(bf16)
    for n in range(out_ref.shape[0]):
        out_ref[n] = both


def finish_kernel(scale, got_ref, weight_ref, bias_ref, held, others):
    for z in range(2):
        total = got_ref[4 * z].astype(f32)
        for n in range(1, 4):
            total = total + got_ref[4 * z + n].astype(f32)
        held[2 * PART * z : 2 * PART * (z + 1), :] = total * scale
    bias = held[BIAS_ROW : BIAS_ROW + 1, :]
    bias_ref[...] = bias[:, 0:RGB] + bias[:, RGB : 2 * RGB]
    count = TIN * TAPS * RGB - PARTS * MAIN
    lane = iota((count, LANES), 1)
    tail = jnp.zeros((count, LANES), f32)
    for c in range(3):
        turned = pltpu.roll(held[pl.ds(c, count, stride=3), :], (32 + 32 * c) % LANES, 1)
        tail = jnp.where(lane // 32 == c, turned, tail)
    others[0:count, :] = tail
    for n in range(TIN * TAPS):
        at = n * RGB
        if at < PARTS * MAIN:
            at = (at // MAIN) * PART + at % MAIN
            value = held[at : at + RGB, 0:CH]
        else:
            at -= PARTS * MAIN
            value = others[at : at + RGB, 0:CH]
        weight_ref[n // TAPS, n % TAPS] = value


VM = pl.BlockSpec(memory_space=pltpu.VMEM)
SM = pl.BlockSpec(memory_space=pltpu.SMEM)
HBM = pl.BlockSpec(memory_space=pltpu.HBM)
LIMIT = 40 * 1024 * 1024


def call(body, out_shape, in_specs, scratch=(), flops=1 << 20, size=1 << 17, name=None, limit=LIMIT, **rest):
    return pl.pallas_call(
        body,
        out_shape=out_shape,
        in_specs=in_specs,
        scratch_shapes=list(scratch),
        compiler_params=pltpu.CompilerParams(vmem_limit_bytes=limit),
        cost_estimate=pl.CostEstimate(flops=flops, bytes_accessed=size, transcendentals=0),
        name=name,
        **rest,
    )


def exchange(rows, axes):
    return lax.all_to_all(rows, axes, 0, 0, tiled=True)


def message(peers, rows):
    return jax.ShapeDtypeStruct((peers, rows, LANES), bf16)


def per_device(features, conv_weight, bias, blend_profile, tile_ids, reward_grad):
    chunk = 1024
    conv_flops = 2 * STACK * TIN * CH * PIX
    own = lax.axis_index(("y_hi", "y_lo", "z_hi", "z_lo", "c")).reshape(1).astype(jnp.int32)
    feats = jnp.transpose(features[0, 0], (1, 0, 2))
    args = (feats, conv_weight, bias, reward_grad[0, 0], tile_ids, blend_profile)
    here = [pltpu.with_memory_space_constraint(x, pltpu.HBM) for x in args]
    rows, route, mats, before, after, ratio, feats_held, weights_held = call(
        functools.partial(conv_kernel, 2 * chunk),
        (
            pltpu.VMEM((WIDE, SLAB, LANES), bf16),
            pltpu.VMEM((4 * SLOTS, SLOTS), bf16),
            pltpu.VMEM((9 * SLOTS, SLOTS), bf16),
            pltpu.VMEM((8, LANES), f32),
            pltpu.VMEM((SLOTS, LANES), f32),
            pltpu.VMEM((ROWS, LANES), f32),
            pltpu.VMEM((TIN, CH, PIX), bf16),
            pltpu.VMEM((TIN, STACK, CH), bf16),
        ),
        [HBM, HBM, HBM, HBM, HBM, HBM, SM],
        [
            pltpu.VMEM((TIN, TAPS, RGB, CH), bf16),
            pltpu.SMEM((RGB,), f32),
            pltpu.VMEM((RGB, PIX), bf16),
            pltpu.VMEM((1, SLOTS), jnp.int32),
            pltpu.SMEM((OV,), jnp.int32),
            pltpu.VMEM((TIN, STACK, CH), f32),
            pltpu.VMEM((STACK, PIX), f32),
            pltpu.VMEM((ROWS, 8, LANES), f32),
            pltpu.VMEM((FLAT, SLOTS), bf16),
            pltpu.SemaphoreType.DMA((5,)),
            pltpu.SemaphoreType.DMA((PIX // (2 * chunk),)),
        ],
        conv_flops,
        1 << 22,
        "conv",
        out_specs=(VM,) * 8,
    )(*here, own)
    rows = exchange(rows, ("y_lo", "z_hi", "z_lo", "c"))
    rows = call(
        route_kernel, message(WIDE, SLAB), [VM, VM], (), 1 << 28, 1 << 21, "route", out_specs=VM
    )(rows, route)
    rows = exchange(rows, ("y_hi", "y_lo", "z_lo", "c"))
    rows, stack = call(
        functools.partial(weight_grad_kernel, chunk),
        (message(PEERS, PART + 8), jax.ShapeDtypeStruct((STACK, PIX), bf16)),
        [VM] * 6,
        [pltpu.VMEM((STACK, PIX), f32), pltpu.VMEM((SLOTS + 32, LANES), f32)],
        conv_flops,
        1 << 22,
        "weight_grad",
        out_specs=(VM, VM),
    )(rows, feats_held, ratio, mats, before, after)

    feature_rows = call(
        feature_grad_kernel,
        jax.ShapeDtypeStruct((TIN, CH, PIX), bf16),
        [
            pl.BlockSpec((STACK, chunk), lambda i: (0, i)),
            pl.BlockSpec((TIN, STACK, CH), lambda i: (0, 0, 0)),
        ],
        (),
        conv_flops,
        1 << 22,
        "feature_grad",
        grid=(PIX // chunk,),
        out_specs=pl.BlockSpec((TIN, CH, chunk), lambda i: (0, 0, i)),
    )(stack, weights_held)
    feature_grad = jnp.transpose(feature_rows, (1, 0, 2))[None, None]

    rows = exchange(rows, ("z_hi", "z_lo", "c"))
    rows = call(sum_z_kernel, message(PEERS, PART + 8), [VM, SM], name="sum_z", out_specs=VM)(rows, own)
    rows = exchange(rows, ("y_hi", "y_lo", "c"))
    decoded = call(
        decode_kernel,
        jax.ShapeDtypeStruct((RGB, PIX), bf16),
        [VM, SM],
        [pltpu.VMEM((ROWS, 8, LANES), f32)],
        name="decode",
        out_specs=VM,
    )(rows, own)
    rows = call(sum_y_kernel, message(8, 2 * PART), [VM], name="sum_y", out_specs=VM)(rows)
    rows = exchange(rows, ("z_lo", "clip"))
    rows, decoded, feature_grad = lax.optimization_barrier((rows, decoded, feature_grad))
    scale = 1.0 / math.sqrt(4 * SLOTS * PIX)
    weight_grad, bias_grad = call(
        functools.partial(finish_kernel, scale),
        (
            jax.ShapeDtypeStruct((TIN, TAPS, RGB, CH), f32),
            jax.ShapeDtypeStruct((1, RGB), f32),
        ),
        [VM],
        [pltpu.VMEM((PARTS * PART, LANES), f32), pltpu.VMEM((24, LANES), f32)],
        name="finish",
        out_specs=(VM, VM),
    )(rows)
    return (decoded[None, None], feature_grad, weight_grad, bias_grad.reshape(RGB))


def solution(mesh):
    parts = Mesh(mesh.devices.reshape(4, 2, 4, 2, 2, 4), ("y_hi", "y_lo", "z_hi", "z_lo", "c", "clip"))
    tile = ("y_hi", "y_lo", "z_hi", "z_lo", "c")
    return jax.shard_map(
        per_device,
        mesh=parts,
        in_specs=(
            P("clip", tile, None, None, None),
            P(),
            P(),
            P(),
            P("clip", None),
            P("clip", tile, None, None),
        ),
        out_specs=(P("clip", tile, None, None), P("clip", tile, None, None, None), P(), P()),
        check_vma=False,
    )
```

```python
import functools
import math

import jax
import jax.numpy as jnp
from jax import lax
from jax.experimental import pallas as pl
from jax.experimental.pallas import tpu as pltpu
from jax.sharding import Mesh
from jax.sharding import PartitionSpec as P

EDGE = 64
OV = 32
PIX = EDGE * EDGE
SLOTS = 128
TX = 16
TY = SLOTS // TX
CH = 96
RGB = 3
TIN = 3
LANES = 128
ROWS = PIX // LANES
BOTH = 2 * SLOTS
TAPS = 9
STACK = TAPS * 8
PARTS = 4
PART = 16
MAIN = 15
BIAS_ROW = 15

BOTH = 2 * SLOTS
TAPS = 9
STACK = TAPS * 8
PEERS = 16
WIDE = 32
SLAB = 16
GRADS = 12
FLAT = WIDE * SLAB
PARTS = 4
PART = 16
MAIN = 15
BIAS_ROW = 15

BOTH = 2 * SLOTS
TAPS = 9
STACK = TAPS * 8
PEERS = 16
WIDE = 32
SLAB = 16
GRADS = 12
FLAT = WIDE * SLAB
PARTS = 4
PART = 16
MAIN = 15
BIAS_ROW = 15

f32 = jnp.float32
bf16 = jnp.bfloat16


def iota(shape, dim):
    return lax.broadcasted_iota(jnp.int32, shape, dim)


def onehot(mask):
    return jnp.where(mask, 1.0, 0.0).astype(bf16)


def pick_rows(mask, rows):
    return jnp.dot(onehot(mask), rows.astype(bf16), preferred_element_type=f32)


def shift_lanes(value, amount):
    size = value.shape[1]
    amount = amount % size
    return value if amount == 0 else pltpu.roll(value, size - amount, 1)


def profile_at(index, profile_ref):
    out = jnp.zeros(index.shape, f32)
    for m in range(OV):
        out = jnp.where(index == m, profile_ref[m].astype(f32), out)
    return out


def no_further(room):
    return jnp.minimum(room, 1.0)


def ids_at(ids, slots):
    spread = onehot(iota(slots.shape, 1) == slots)
    wide = jnp.broadcast_to(ids, (8, SLOTS)).astype(bf16)
    return lax.dot_general(spread, wide, (((1,), (1,)), ((), ())), preferred_element_type=f32)[:, 0:1]


def route_prep(ids, y, z, c, mats_ref):
    y_lo, y_hi, z_lo, z_hi = y % 2, y // 2, z % 2, z // 2
    place = iota((SLOTS, SLOTS), 0) // 4
    target = ids_at(ids, (place // 4) * 16 + z_hi * 4 + place % 4)
    col = iota((1, SLOTS), 1)
    source = jnp.dot(
        jnp.broadcast_to(ids, (8, SLOTS)).astype(bf16),
        onehot(iota((SLOTS, SLOTS), 0) == y_hi * WIDE + col // 4),
        preferred_element_type=f32,
    )[0:1]
    row = iota((SLOTS, 1), 0)
    want = target + (TX * ((row // 2) % 2) + 1024 * (row % 2)).astype(f32)
    have = source + (TX * ((col // 2) % 2) + 1024 * (col % 2)).astype(f32)
    across = target - jnp.floor(target * (1.0 / TX)) * TX
    right = jnp.where(across < TX - 1.5, want + 1.0, -9999.0)
    left = jnp.where(across > 0.5, want - 1.0, -9999.0)
    for n, key in enumerate((want, left, right)):
        mats_ref[n * SLOTS : (n + 1) * SLOTS, :] = onehot(have == key)
    peer = col // 4
    to_y = (col % 4) * 2 + (y_lo ^ (peer // 16))
    to_peer = to_y * 4 + (z_lo ^ ((peer // 2) % 2)) * 2 + (c ^ (peer % 2))
    to_row = to_peer * 4 + (peer // 4) % 4
    mats_ref[3 * SLOTS : 4 * SLOTS, :] = onehot(iota((SLOTS, SLOTS), 0) == to_row)


def class_prep(ids, profile_ref, y, z, c, mats_ref, before_ref, after_ref):
    k = (2 * z + c) * 8 + y
    place = iota((SLOTS, SLOTS), 0)
    leaves = (4 * (((place // 8) % 2) ^ c) + place % 4) * 16 + (place // 16) * 2 + (place // 4) % 2
    spread = iota((SLOTS, SLOTS), 1) == leaves
    place = iota((SLOTS, SLOTS), 1)
    comes = ((place // 16) ^ (y % 2)) * 16 + (place % 4) * 4 + (((place // 8) % 2) ^ (z % 2)) * 2 + (((place // 4) % 2) ^ c)
    come = jnp.dot(
        jnp.broadcast_to(ids, (8, SLOTS)).astype(bf16),
        onehot(iota((SLOTS, SLOTS), 0) == comes),
        preferred_element_type=f32,
    )[0:1]
    own = jnp.sum(jnp.where(spread, jnp.broadcast_to(ids, (SLOTS, SLOTS)), 0.0), axis=1, keepdims=True)
    row = jnp.floor(own * (1.0 / TX))
    col = own - row * TX
    right = jnp.where(col < TX - 1.5, own + 1.0, -9999.0)
    left = jnp.where(col > 0.5, own - 1.0, -9999.0)
    n = 0
    for key in (own, left, right):
        gap = come - key
        for step in (0.0, -float(TX), float(TX)):
            mats_ref[n * SLOTS : (n + 1) * SLOTS, :] = onehot(gap == step)
            n += 1
    h, par, rx = k // 64, (k // 32) % 2, k % 32
    lane = iota((1, LANES), 1)
    east = lane >= 64
    south = (lane // 8) % 2 == 1
    ry = 2 * (8 * h + lane % 8) + par
    fy = profile_at(jnp.where(south, OV - 1 - ry, ry), profile_ref)
    fy_other = profile_at(jnp.where(south, ry, OV - 1 - ry), profile_ref)
    near = profile_ref[rx].astype(f32)
    far = profile_ref[OV - 1 - rx].astype(f32)
    fx = jnp.where(east, far, near)
    fx_other = jnp.where(east, near, far)
    col_there = no_further(jnp.where(east, TX - 1.0 - col, col))
    row_there = no_further(jnp.where(south, TY - 1.0 - row, row))
    before_ref[...] = jnp.broadcast_to(fx * fy, (8, LANES))
    after_ref[...] = 1.0 / ((fx + col_there * fx_other) * (fy + row_there * fy_other))


def ratio_prep(ids, profile_ref, own_slot, ratio_ref):
    own = jnp.sum(jnp.where(iota((1, SLOTS), 1) == own_slot, ids, 0.0), axis=1, keepdims=True)
    row = jnp.floor(own * (1.0 / TX))
    col = own - row * TX
    lane = iota((1, LANES), 1)
    x = lane % EDGE
    y = 2 * iota((ROWS, LANES), 0) + iota((ROWS, LANES), 1) // EDGE
    at_x = jnp.minimum(x, EDGE - 1 - x)
    at_y = jnp.minimum(y, EDGE - 1 - y)
    fx = profile_at(at_x, profile_ref)
    fx_other = profile_at(OV - 1 - at_x, profile_ref)
    fy = profile_at(at_y, profile_ref)
    fy_other = profile_at(OV - 1 - at_y, profile_ref)
    col_there = no_further(jnp.where(x >= OV, TX - 1.0 - col, col))
    row_there = no_further(jnp.where(y >= OV, TY - 1.0 - row, row))
    ratio_ref[...] = fx * fy / ((fx + col_there * fx_other) * (fy + row_there * fy_other))


def pass_on(slabs, core):
    block = jnp.concatenate(slabs, axis=0)
    place = iota((SLOTS, SLOTS), 0)
    y = place // 16
    peer = (place % 8) * 2 + (core ^ (y // 4))
    return pick_rows(iota((SLOTS, SLOTS), 1) == peer * 8 + ((place // 8) % 2) * 4 + y % 4, block)


def route_kernel(got_ref, mats_ref, out_ref):
    slabs = [got_ref[p].astype(f32) for p in range(WIDE)]
    blocks = [jnp.concatenate([slab[4 * o : 4 * o + 4] for slab in slabs], axis=0) for o in range(RGB + 1)]
    every = jnp.dot(
        mats_ref[0 : 3 * SLOTS, :], jnp.concatenate(blocks[:RGB], axis=1).astype(bf16), preferred_element_type=f32
    )
    east = iota((SLOTS, LANES), 1) % EDGE >= OV
    totals = []
    for o in range(RGB):
        here, left, right = (every[n * SLOTS : (n + 1) * SLOTS, o * LANES : (o + 1) * LANES] for n in range(3))
        totals.append(here + jnp.where(east, pltpu.roll(right, OV, 1), pltpu.roll(left, LANES - OV, 1)))
    totals.append(jnp.dot(mats_ref[3 * SLOTS :, :], blocks[RGB].astype(bf16), preferred_element_type=f32))
    for t in range(WIDE):
        out_ref[t] = jnp.concatenate([total[4 * t : 4 * t + 4] for total in totals], axis=0).astype(bf16)


def blend_classes(images, mats_ref, before_ref, after_ref):
    source = images * before_ref[0:1, :]
    high = source.astype(bf16)
    low = (source - high.astype(f32)).astype(bf16)
    lane = iota((SLOTS, LANES), 1)
    south = (lane // 8) % 2 == 1
    every = jnp.dot(mats_ref[...], jnp.concatenate([high, low], axis=1), preferred_element_type=f32)
    every = every[:, :LANES] + every[:, LANES:]
    columns = []
    for d in range(3):
        part = [every[(3 * d + step) * SLOTS : (3 * d + step + 1) * SLOTS] for step in range(3)]
        across = jnp.where(south, part[1], part[2])
        columns.append(part[0] + jnp.where(south, pltpu.roll(across, 8, 1), pltpu.roll(across, LANES - 8, 1)))
    total = columns[0] + pltpu.roll(jnp.where(lane >= 64, columns[1], columns[2]), 64, 1)
    return total * after_ref[...]


def stack_weights(weight_ref, held):
    held[...] = jnp.zeros_like(held)
    for t in range(TIN):
        for tap in range(TAPS):
            held[t, tap * 8 : tap * 8 + RGB, :] = weight_ref[t, tap].astype(f32)


def conv_kernel(
    chunk,
    feat_ref,
    weight_hbm,
    bias_hbm,
    grad_hbm,
    ids_hbm,
    profile_hbm,
    own_ref,
    out_ref,
    route_ref,
    mats_ref,
    before_ref,
    after_ref,
    ratio_ref,
    feats,
    stacked_ref,
    weight_ref,
    bias_ref,
    grad_ref,
    ids_ref,
    profile_ref,
    held,
    taps,
    turned,
    place_ref,
    small_sems,
    sems,
):
    small = [(ids_hbm, ids_ref), (profile_hbm, profile_ref), (weight_hbm, weight_ref), (grad_hbm, grad_ref), (bias_hbm, bias_ref)]
    moves = [pltpu.make_async_copy(src, dst, small_sems.at[n]) for n, (src, dst) in enumerate(small)]
    for move in moves:
        move.start()
    copies = []
    for n in range(PIX // chunk):
        part = pl.ds(n * chunk, chunk)
        copies.append(pltpu.make_async_copy(feat_ref.at[:, :, part], feats.at[:, :, part], sems.at[n]))
        copies[-1].start()
    for move in moves:
        move.wait()
    stack_weights(weight_ref, held)
    kernels = [held[t].astype(bf16) for t in range(TIN)]
    for t in range(TIN):
        stacked_ref[t] = kernels[t]
    ids = ids_ref[...].astype(f32)
    own = own_ref[0]
    y, z, c = own // 16, (own // 2) % 8, own % 2
    route_prep(ids, y, z, c, route_ref)
    class_prep(ids, profile_ref, y, z, c, mats_ref, before_ref, after_ref)
    ratio_prep(ids, profile_ref, own, ratio_ref)
    taps[0:8, :] = jnp.zeros((8, PIX), f32)
    taps[0:RGB, :] = grad_ref[...].astype(f32)
    grads = jnp.concatenate([taps[0:8, r * LANES : (r + 1) * LANES] for r in range(ROWS)], axis=0)
    col = iota((1, BOTH), 1)
    r, o = col // 8, col % 8
    to_row = jnp.where(o < RGB, ((r // 2) % 8) * SLAB + o * 4 + (r // 16) * 2 + r % 2, -1)
    eighths = pick_rows(iota((SLOTS, BOTH), 0) == to_row, grads)
    k = iota((1, SLOTS), 1)
    peer = ((k % 2) ^ (y % 2)) * 16 + (k // 32) * 4 + (((k // 16) % 2) ^ (z % 2)) * 2 + (((k // 8) % 2) ^ c)
    place_ref[...] = onehot(iota((SLOTS, SLOTS), 0) == peer * 4 + (k % 8) // 2)
    for n in range(PIX // chunk):
        copies[n].wait()
        total = jnp.zeros((STACK, chunk), f32)
        for t in range(TIN):
            total += jnp.dot(kernels[t], feats[t, :, n * chunk : (n + 1) * chunk], preferred_element_type=f32)
        taps[:, n * chunk : (n + 1) * chunk] = total
    lane = iota((8, PIX), 1)
    image = jnp.zeros((8, PIX), f32)
    for kx in range(3):
        column = jnp.zeros((8, PIX), f32)
        for ky in range(3):
            tap = 3 * ky + kx
            moved = shift_lanes(taps[tap * 8 : tap * 8 + 8, :], (ky - 1) * EDGE)
            if ky == 0:
                moved = jnp.where(lane >= EDGE, moved, 0.0)
            elif ky == 2:
                moved = jnp.where(lane < PIX - EDGE, moved, 0.0)
            column = column + moved
        moved = shift_lanes(column, kx - 1)
        if kx == 0:
            moved = jnp.where(lane % EDGE != 0, moved, 0.0)
        elif kx == 2:
            moved = jnp.where(lane % EDGE != EDGE - 1, moved, 0.0)
        image = image + moved
    row = iota((8, 1), 0)
    shift = jnp.zeros((8, 1), f32)
    for o in range(RGB):
        shift = jnp.where(row == o, bias_ref[o], shift)
    image = image + shift
    for r in range(ROWS):
        turned[r] = image[:, r * LANES : (r + 1) * LANES]
    place = iota((LANES, LANES), 0)
    lanes = onehot(iota((LANES, LANES), 1) == ((place // 32) % 2) * 64 + (place // 64) * 32 + place % 32)
    classes = []
    for h in range(2):
        block = half_rows(turned, h, RGB) + [jnp.zeros((16, LANES), f32)]
        block = jnp.concatenate(block, axis=0).astype(bf16)
        both = lax.dot_general(lanes, block, (((1,), (1,)), ((), ())), preferred_element_type=f32)
        classes.append(jnp.concatenate([both[0:64], both[64:128]], axis=1))
    classes = jnp.concatenate(classes, axis=0).astype(bf16)
    images = jnp.dot(place_ref[...], classes, preferred_element_type=f32)
    for p in range(WIDE):
        e = (p // 16) * 4 + p % 4
        slab = [eighths[e * SLAB : e * SLAB + GRADS], images[4 * p : 4 * p + 4]]
        out_ref[p] = jnp.concatenate(slab, axis=0).astype(bf16)


def half_rows(turned, h, colours):
    return [turned[qy * 16 + h * 8 : qy * 16 + h * 8 + 8, o, :] for o in range(colours) for qy in range(2)]


def grad_stack(grad, taps):
    lane = iota((8, PIX), 1)
    for kx in range(3):
        moved_x = shift_lanes(grad, 1 - kx)
        if kx == 0:
            moved_x = jnp.where(lane % EDGE != EDGE - 1, moved_x, 0.0)
        elif kx == 2:
            moved_x = jnp.where(lane % EDGE != 0, moved_x, 0.0)
        for ky in range(3):
            moved = shift_lanes(moved_x, (1 - ky) * EDGE)
            if ky == 0:
                moved = jnp.where(lane < PIX - EDGE, moved, 0.0)
            elif ky == 2:
                moved = jnp.where(lane >= EDGE, moved, 0.0)
            tap = 3 * ky + kx
            taps[tap * 8 : tap * 8 + 8, :] = moved


def split_bias(part):
    at = iota((PART, LANES), 0) == BIAS_ROW
    lane = iota((PART, LANES), 1)
    total = part + pltpu.roll(part, LANES - RGB, 1)
    high = total.astype(bf16).astype(f32)
    low = pltpu.roll(total - high, RGB, 1)
    pair = jnp.where(lane < RGB, high, jnp.where(lane < 2 * RGB, low, part))
    return jnp.where(at, pair, part)


def weight_grad_kernel(
    chunk, got_ref, feat_ref, ratio_ref, mats_ref, before_ref, after_ref, out_ref, stack_ref, taps, added
):
    slabs = [got_ref[n].astype(f32) for n in range(WIDE)]
    for e in range(8):
        added[e * SLAB : (e + 1) * SLAB, :] = slabs[e] + slabs[e + 8] + slabs[e + 16] + slabs[e + 24]
    added[SLOTS:, :] = jnp.zeros((32, LANES), f32)
    colour = iota((8, LANES), 0) < RGB
    pieces = []
    for r in range(ROWS):
        first = ((r // 2) % 8) * SLAB + (r // 16) * 2 + r % 2
        piece = added[pl.ds(first, 8, stride=4), :] * ratio_ref[r : r + 1, :]
        pieces.append(jnp.where(colour, piece, 0.0).astype(bf16).astype(f32))
    grad = jnp.concatenate(pieces, axis=1)
    images = jnp.concatenate([slab[GRADS:] for slab in slabs], axis=0)
    blended = blend_classes(images, mats_ref, before_ref, after_ref)
    grad_stack(grad, taps)
    summed = pieces[0]
    for piece in pieces[1:]:
        summed = summed + piece
    diagonal = iota((8, LANES), 0) == iota((8, LANES), 1)
    bias = jnp.sum(
        jnp.where(diagonal, jnp.sum(summed, axis=1, keepdims=True), 0.0), axis=0, keepdims=True
    )
    total = jnp.zeros((TIN * CH, STACK), f32)
    for at in range(0, PIX, chunk):
        part = taps[:, at : at + chunk].astype(bf16)
        stack_ref[:, at : at + chunk] = part
        total += lax.dot_general(
            feat_ref[:, :, at : at + chunk].reshape(TIN * CH, chunk),
            part,
            (((1,), (1,)), ((), ())),
            preferred_element_type=f32,
        )
    rows = jnp.concatenate([total[t * CH : (t + 1) * CH].T for t in range(TIN)], axis=0)
    rows = jnp.concatenate([rows, jnp.zeros((TIN * STACK, LANES - CH), f32)], axis=1).astype(bf16)
    every = PARTS * PART
    place = iota((2 * every, TIN * STACK), 0)
    source = iota((2 * every, TIN * STACK), 1)
    rank = jnp.where(source % 8 < RGB, (source // 8) * RGB + source % 8, -1)
    within = place % PART
    main = (rank == (place // PART) * MAIN + within) & (within < MAIN) & (place < every)
    offset = place - every - RGB * (rank - PARTS * MAIN)
    side = (offset >= 0) & (offset < RGB) & (place >= every) & (rank >= PARTS * MAIN)
    chosen = jnp.dot(onehot(main | side), rows, preferred_element_type=f32)
    lane = iota((every, LANES), 1)
    third = iota((every, LANES), 0) % 3
    tail = jnp.zeros((every, LANES), f32)
    for c in range(3):
        tail = jnp.where(third == c, pltpu.roll(chosen[every:], CH - 32 * c, 1), tail)
    packed = jnp.where(lane < CH, chosen[:every], tail)
    packed = jnp.where((iota((every, LANES), 0) % PART == BIAS_ROW) & (lane < CH), bias, packed)
    parts = [split_bias(packed[q * PART : (q + 1) * PART]) for q in range(PARTS)]
    for p in range(PEERS):
        out_ref[p] = jnp.concatenate([parts[p % PARTS], blended[p * 8 : p * 8 + 8]], axis=0).astype(bf16)


def feature_grad_kernel(stack_ref, weight_ref, out_ref):
    for t in range(TIN):
        out_ref[t] = lax.dot_general(
            weight_ref[t], stack_ref[...], (((0,), (0,)), ((), ())), preferred_element_type=f32
        ).astype(bf16)


def decode_kernel(got_ref, own_ref, image_ref, turned):
    images = jnp.concatenate([got_ref[n].astype(f32)[PART : PART + 8] for n in range(PEERS)], axis=0)
    block = jnp.concatenate([images[:, 0:64], images[:, 64:128]], axis=0).astype(bf16)
    row = iota((BOTH, LANES), 0)
    lane = iota((BOTH, LANES), 1)
    k = ((row % 8) * 2 + (((row // 8) % 2) ^ (own_ref[0] // 64))) * 8 + (row // 16) % 8
    spot = ((k // 32) % 2) * 64 + (row // SLOTS) * 32 + k % 32
    for h in range(2):
        lanes = onehot((lane == spot) & (k // 64 == h))
        tile = lax.dot_general(block, lanes, (((0,), (0,)), ((), ())), preferred_element_type=f32)
        for o in range(RGB):
            for qy in range(2):
                turned[qy * 16 + h * 8 : qy * 16 + h * 8 + 8, o, :] = tile[o * 16 + qy * 8 : o * 16 + qy * 8 + 8]
    for r in range(ROWS):
        image_ref[:, r * LANES : (r + 1) * LANES] = turned[r, 0:RGB, :].astype(bf16)


def sum_z_kernel(got_ref, own_ref, out_ref):
    slabs = [got_ref[p].astype(f32) for p in range(PEERS)]
    part = slabs[0][0:PART]
    for slab in slabs[1:]:
        part = part + slab[0:PART]
    part = split_bias(part)
    images = pass_on([slab[PART : PART + 8] for slab in slabs], own_ref[0] % 2)
    for t in range(PEERS):
        out_ref[t] = jnp.concatenate([part, images[t * 8 : t * 8 + 8]], axis=0).astype(bf16)


def sum_y_kernel(got_ref, out_ref):
    parts = []
    for c in range(2):
        part = got_ref[c].astype(f32)[0:PART]
        for y in range(1, 8):
            part = part + got_ref[2 * y + c].astype(f32)[0:PART]
        parts.append(split_bias(part))
    both = jnp.concatenate(parts, axis=0).astype(bf16)
    for n in range(out_ref.shape[0]):
        out_ref[n] = both


def finish_kernel(scale, got_ref, weight_ref, bias_ref, held, others):
    for z in range(2):
        total = got_ref[4 * z].astype(f32)
        for n in range(1, 4):
            total = total + got_ref[4 * z + n].astype(f32)
        held[2 * PART * z : 2 * PART * (z + 1), :] = total * scale
    bias = held[BIAS_ROW : BIAS_ROW + 1, :]
    bias_ref[...] = bias[:, 0:RGB] + bias[:, RGB : 2 * RGB]
    count = TIN * TAPS * RGB - PARTS * MAIN
    lane = iota((count, LANES), 1)
    tail = jnp.zeros((count, LANES), f32)
    for c in range(3):
        turned = pltpu.roll(held[pl.ds(c, count, stride=3), :], (32 + 32 * c) % LANES, 1)
        tail = jnp.where(lane // 32 == c, turned, tail)
    others[0:count, :] = tail
    for n in range(TIN * TAPS):
        at = n * RGB
        if at < PARTS * MAIN:
            at = (at // MAIN) * PART + at % MAIN
            value = held[at : at + RGB, 0:CH]
        else:
            at -= PARTS * MAIN
            value = others[at : at + RGB, 0:CH]
        weight_ref[n // TAPS, n % TAPS] = value


VM = pl.BlockSpec(memory_space=pltpu.VMEM)
SM = pl.BlockSpec(memory_space=pltpu.SMEM)
HBM = pl.BlockSpec(memory_space=pltpu.HBM)
LIMIT = 40 * 1024 * 1024


def call(body, out_shape, in_specs, scratch=(), flops=1 << 20, size=1 << 17, name=None, limit=LIMIT, **rest):
    return pl.pallas_call(
        body,
        out_shape=out_shape,
        in_specs=in_specs,
        scratch_shapes=list(scratch),
        compiler_params=pltpu.CompilerParams(vmem_limit_bytes=limit),
        cost_estimate=pl.CostEstimate(flops=flops, bytes_accessed=size, transcendentals=0),
        name=name,
        **rest,
    )


def exchange(rows, axes):
    return lax.all_to_all(rows, axes, 0, 0, tiled=True)


def message(peers, rows):
    return jax.ShapeDtypeStruct((peers, rows, LANES), bf16)


def per_device(features, conv_weight, bias, blend_profile, tile_ids, reward_grad):
    chunk = 1024
    conv_flops = 2 * STACK * TIN * CH * PIX
    own = lax.axis_index(("y_hi", "y_lo", "z_hi", "z_lo", "c")).reshape(1).astype(jnp.int32)
    feats = jnp.transpose(features[0, 0], (1, 0, 2))
    args = (feats, conv_weight, bias, reward_grad[0, 0], tile_ids, blend_profile)
    here = [pltpu.with_memory_space_constraint(x, pltpu.HBM) for x in args]
    rows, route, mats, before, after, ratio, feats_held, weights_held = call(
        functools.partial(conv_kernel, 2 * chunk),
        (
            pltpu.VMEM((WIDE, SLAB, LANES), bf16),
            pltpu.VMEM((4 * SLOTS, SLOTS), bf16),
            pltpu.VMEM((9 * SLOTS, SLOTS), bf16),
            pltpu.VMEM((8, LANES), f32),
            pltpu.VMEM((SLOTS, LANES), f32),
            pltpu.VMEM((ROWS, LANES), f32),
            pltpu.VMEM((TIN, CH, PIX), bf16),
            pltpu.VMEM((TIN, STACK, CH), bf16),
        ),
        [HBM, HBM, HBM, HBM, HBM, HBM, SM],
        [
            pltpu.VMEM((TIN, TAPS, RGB, CH), bf16),
            pltpu.SMEM((RGB,), f32),
            pltpu.VMEM((RGB, PIX), bf16),
            pltpu.VMEM((1, SLOTS), jnp.int32),
            pltpu.SMEM((OV,), jnp.int32),
            pltpu.VMEM((TIN, STACK, CH), f32),
            pltpu.VMEM((STACK, PIX), f32),
            pltpu.VMEM((ROWS, 8, LANES), f32),
            pltpu.VMEM((SLOTS, SLOTS), bf16),
            pltpu.SemaphoreType.DMA((5,)),
            pltpu.SemaphoreType.DMA((PIX // (2 * chunk),)),
        ],
        conv_flops,
        1 << 22,
        "conv",
        out_specs=(VM,) * 8,
    )(*here, own)
    rows = exchange(rows, ("y_lo", "z_hi", "z_lo", "c"))
    rows = call(
        route_kernel, message(WIDE, SLAB), [VM, VM], (), 1 << 28, 1 << 21, "route", out_specs=VM
    )(rows, route)
    rows = exchange(rows, ("y_hi", "y_lo", "z_lo", "c"))
    rows, stack = call(
        functools.partial(weight_grad_kernel, chunk),
        (message(PEERS, PART + 8), jax.ShapeDtypeStruct((STACK, PIX), bf16)),
        [VM] * 6,
        [pltpu.VMEM((STACK, PIX), f32), pltpu.VMEM((SLOTS + 32, LANES), f32)],
        conv_flops,
        1 << 22,
        "weight_grad",
        out_specs=(VM, VM),
    )(rows, feats_held, ratio, mats, before, after)

    feature_rows = call(
        feature_grad_kernel,
        jax.ShapeDtypeStruct((TIN, CH, PIX), bf16),
        [
            pl.BlockSpec((STACK, chunk), lambda i: (0, i)),
            pl.BlockSpec((TIN, STACK, CH), lambda i: (0, 0, 0)),
        ],
        (),
        conv_flops,
        1 << 22,
        "feature_grad",
        grid=(PIX // chunk,),
        out_specs=pl.BlockSpec((TIN, CH, chunk), lambda i: (0, 0, i)),
    )(stack, weights_held)
    feature_grad = jnp.transpose(feature_rows, (1, 0, 2))[None, None]

    rows = exchange(rows, ("z_hi", "z_lo", "c"))
    rows = call(sum_z_kernel, message(PEERS, PART + 8), [VM, SM], name="sum_z", out_specs=VM)(rows, own)
    rows = exchange(rows, ("y_hi", "y_lo", "c"))
    decoded = call(
        decode_kernel,
        jax.ShapeDtypeStruct((RGB, PIX), bf16),
        [VM, SM],
        [pltpu.VMEM((ROWS, 8, LANES), f32)],
        name="decode",
        out_specs=VM,
    )(rows, own)
    rows = call(sum_y_kernel, message(8, 2 * PART), [VM], name="sum_y", out_specs=VM)(rows)
    rows = exchange(rows, ("z_lo", "clip"))
    rows, decoded, feature_grad = lax.optimization_barrier((rows, decoded, feature_grad))
    scale = 1.0 / math.sqrt(4 * SLOTS * PIX)
    weight_grad, bias_grad = call(
        functools.partial(finish_kernel, scale),
        (
            jax.ShapeDtypeStruct((TIN, TAPS, RGB, CH), f32),
            jax.ShapeDtypeStruct((1, RGB), f32),
        ),
        [VM],
        [pltpu.VMEM((PARTS * PART, LANES), f32), pltpu.VMEM((24, LANES), f32)],
        name="finish",
        out_specs=(VM, VM),
    )(rows)
    return (decoded[None, None], feature_grad, weight_grad, bias_grad.reshape(RGB))


def solution(mesh):
    parts = Mesh(mesh.devices.reshape(4, 2, 4, 2, 2, 4), ("y_hi", "y_lo", "z_hi", "z_lo", "c", "clip"))
    tile = ("y_hi", "y_lo", "z_hi", "z_lo", "c")
    return jax.shard_map(
        per_device,
        mesh=parts,
        in_specs=(
            P("clip", tile, None, None, None),
            P(),
            P(),
            P(),
            P("clip", None),
            P("clip", tile, None, None),
        ),
        out_specs=(P("clip", tile, None, None), P("clip", tile, None, None, None), P(), P()),
        check_vma=False,
    )
```
